512 devices in a mesh: dp: 16 (over x, z_hi), section: 8 (over y), tensor: 4 (over z_lo, core).
Axes of the slice: x: 4, y: 8, z: 8 (z_hi: 4, z_lo: 2; z = z_hi * 2 + z_lo), core: 2. Of those that a mesh axis runs over, the one named last changes fastest.
Arguments:
- tokens: bfloat16 [2048, 8192], P('dp', 'tensor'), may hold values from -6 to 6
- owner_indices: int32 [2048, 1], P('dp'), may hold values from 0 to 15; in each aligned block of 64 rows (0 to 63, 64 to 127, ...) at most 5 rows name the same one
- local_adapter_index: int32 [2048], P('dp'), may hold values from 0 to 1
- gains: bfloat16 [8, 8192], P('section', 'tensor'), may hold values from 0.099609375 to 1.8984375
- adapter_down_weights: bfloat16 [8, 32, 64, 8192], P('section', 'dp', None, 'tensor'), may hold values from -0.0625 to 0.0625
- adapter_up_weights: bfloat16 [8, 32, 64, 8192], P('section', 'dp', None, 'tensor'), may hold values from -0.75 to 0.75
- cotangent: bfloat16 [2048, 8192], P('dp', 'tensor'), may hold values from -6 to 6
Outputs:
- grad_down: bfloat16 [8, 32, 64, 8192], P('section', 'dp', None, 'tensor')
- grad_up: bfloat16 [8, 32, 64, 8192], P('section', 'dp', None, 'tensor')
- norm_slopes: float32 [8, 2048], P('section', 'dp')
The draws below stay inside these ranges and needn't reach their ends.
Inputs may be any that keep to these rules, and one draw needn't show every extreme that they name: `owner_indices`: in each aligned block of 64 rows (one micro-batch), no value appears in more than 5 rows.
All inputs are finite; a program needn't handle non-finite values.
Results may differ from the reference program's by a relative error of at most 0.02.
Values may be sent and summed in bfloat16 or wider, within the bound.
A program may use at most 64 MiB of HBM per device.

```python
import math
import jax
import jax.numpy as jnp
import numpy as np
from jax import lax

MODEL_WIDTH = 8192
LOW_RANK = 64
ADAPT_DEV = 2
MTOK = 64
MICRO = 2
SECTION_LAYERS = 8
ADAPTER_TOTAL = 32
OWN_CAP = 5
TOKENS = 2048
N_DP = 16


def place_ends(array, rng, least, top_value):
    extent = array.shape
    index_at = [jax.random.randint(jax.random.fold_in(rng, axis), (), 0, extent[axis]) for axis in range(len(extent))]
    array = array.at[tuple(index_at)].set(least)
    longest = extent.index(max(extent))
    index_at[longest] = (index_at[longest] + 1) % extent[longest]
    return array.at[tuple(index_at)].set(top_value)


def block_levels(rng, shape, pieces, low, largest):
    factor_of, own = 1.0, jax.random.fold_in(rng, 6)
    for dim, blocks in pieces:
        draws = jnp.exp(jax.random.uniform(jax.random.fold_in(own, dim), (blocks,), jnp.float32, low / len(pieces), largest / len(pieces)))
        factor_of = factor_of * jnp.repeat(draws, shape[dim] // blocks).reshape([-1 if axis == dim else 1 for axis in range(len(shape))])
    return factor_of


def shared_out(key, own, number, rows, amount, top, most, slope):
    ranking = jax.random.permutation(key, amount)
    packed, common = portions_of(amount, rows * top, most, slope, True), portions_of(amount, rows * top, most, slope, False)
    places = jnp.arange(amount)

    def named(lengths, turn):
        used = int((lengths > 0).sum())
        fixed = max(1, used // 4)
        shifted = fixed + (places - fixed + turn * (used - fixed)) % max(1, amount - fixed)
        return jnp.zeros((amount,), jnp.int32).at[ranking[jnp.where(places < fixed, places, shifted)]].set(jnp.asarray(lengths, jnp.int32))

    lengths = jnp.where(number % 4 == 0, named(packed, number // 4), named(common, number - number // 4 - 1))
    mixed = jax.random.permutation(jax.random.fold_in(own, 3), amount)
    giver, taker = mixed[0:amount // 2 * 2:2], mixed[1:amount // 2 * 2:2]
    margin = jnp.minimum(lengths[giver] - 1, most - lengths[taker]) // 2
    margin = jnp.where((giver == ranking[0]) | (taker == ranking[0]) | (lengths[taker] == 0), 0, jnp.maximum(margin, 0))
    shifted = jax.random.randint(jax.random.fold_in(own, 4), (amount // 2,), 0, 1 << 20) % (margin + 1)
    lengths = lengths.at[giver].add(-shifted).at[taker].add(shifted)
    labels = jnp.searchsorted(jnp.cumsum(lengths), jnp.arange(rows * top), side="right").astype(jnp.int32)
    table = labels.reshape(top, rows).T
    table = table[jax.random.permutation(jax.random.fold_in(own, 1), rows)]
    turn = jax.random.randint(jax.random.fold_in(own, 2), (rows, 1), 0, top)
    return jnp.take_along_axis(table, (jnp.arange(top)[None, :] + turn) % top, axis=1)


def portions_of(amount, total, most, lean, full):
    weights = [(1 << 20) // math.isqrt(rank ** lean) + 1 for rank in range(1, amount + 1)]
    largest = most if full else min(most, max(-(-total // amount), total * weights[0] // sum(weights)))
    least = 1 if total - largest >= amount - 1 else 0
    holding, rest = [largest] + [least] * (amount - 1), total - largest - least * (amount - 1)
    while rest > 0:
        movable = [i for i in range(1, amount) if holding[i] < largest] or [i for i in range(1, amount) if holding[i] < most]
        mass, remaining = sum([weights[i] for i in movable]), rest
        for i in movable:
            extra = min(most - holding[i], max(1, remaining * weights[i] // mass), rest)
            holding[i] = holding[i] + extra
            rest = rest - extra
    return np.array(holding)


def bell_draw(stream_key, dims, deviation, most, shards=(), kind=jnp.bfloat16):
    loudness = block_levels(stream_key, dims, shards, -0.22, 0.18) if shards else 1.0
    array = jax.random.normal(stream_key, dims, jnp.float32) * deviation * loudness
    return jnp.minimum(jnp.maximum(array, -most), most).astype(kind)


def setup_inputs(seed: int = 0) -> dict:
    streams_of = jax.random.split(jax.random.key(seed), 8)
    tokens = bell_draw(streams_of[0], (TOKENS, MODEL_WIDTH), 1.0, 6.0, ((0, 16), (1, 4)))
    owner_indices_keys = jax.random.split(jax.random.fold_in(streams_of[1], 1), TOKENS // MTOK)
    owner_indices_turns = jax.random.permutation(jax.random.fold_in(streams_of[1], 3), TOKENS // MTOK)
    owner_indices = jax.vmap(lambda own, number: shared_out(jax.random.fold_in(streams_of[1], 2), own, number, MTOK, N_DP, 1, OWN_CAP, 1))(owner_indices_keys, owner_indices_turns).reshape((TOKENS, 1))
    local_adapter_index = place_ends(jax.random.randint(streams_of[2], (TOKENS,), 0, ADAPT_DEV), jax.random.fold_in(streams_of[2], 1), 0, ADAPT_DEV - 1).astype(jnp.int32)
    gains = jnp.clip(1.0 + 0.18 * jax.random.normal(streams_of[3], (SECTION_LAYERS, MODEL_WIDTH), jnp.float32), 0.099609375, 1.8984375).astype(jnp.bfloat16)
    adapter_down_weights = bell_draw(streams_of[4], (SECTION_LAYERS, ADAPTER_TOTAL, LOW_RANK, MODEL_WIDTH), MODEL_WIDTH ** -0.5, 0.0625, ((0, 8), (1, 16), (3, 4)))
    adapter_up_weights = bell_draw(streams_of[5], (SECTION_LAYERS, ADAPTER_TOTAL, LOW_RANK, MODEL_WIDTH), LOW_RANK ** -0.5, 0.75, ((0, 8), (1, 16), (3, 4)))
    cotangent = bell_draw(streams_of[6], (TOKENS, MODEL_WIDTH), 1.0, 6.0, ((0, 16), (1, 4)))
    return {"tokens": tokens, "owner_indices": owner_indices, "local_adapter_index": local_adapter_index, "gains": gains, "adapter_down_weights": adapter_down_weights, "adapter_up_weights": adapter_up_weights, "cotangent": cotangent}


eps = 1e-05
adapter_scale = 0.5

def reference(tokens, owner_indices, local_adapter_index, gains, adapter_down_weights, adapter_up_weights, cotangent):
    most_each = N_DP * MICRO * OWN_CAP
    adapter = (owner_indices[:, 0] * ADAPT_DEV + local_adapter_index).astype(jnp.int32)
    onehot = (adapter[:, None] == jnp.arange(ADAPTER_TOTAL, dtype=jnp.int32)[None, :]).astype(jnp.int32)
    rank_in = lax.optimization_barrier(jnp.sum((jnp.cumsum(onehot, 0) - onehot) * onehot, 1)).astype(jnp.int32)
    place = (adapter * most_each + rank_in).astype(jnp.int32)
    table = jnp.full((ADAPTER_TOTAL * most_each,), TOKENS, jnp.int32).at[place].set(jnp.arange(TOKENS, dtype=jnp.int32))

    def to_slots(values):
        padded = jnp.concatenate([values, jnp.zeros((1, values.shape[1]), values.dtype)], 0)
        return padded[table].reshape(ADAPTER_TOTAL, most_each, values.shape[1])

    def from_slots(values):
        return values.reshape(ADAPTER_TOTAL * most_each, values.shape[2])[place]
    kept = []
    state = tokens
    for layer_index in range(SECTION_LAYERS):
        wide = state.astype(jnp.float32)
        scale_rows = lax.rsqrt(lax.optimization_barrier(jnp.mean(wide * wide, 1)) + eps)
        normed = (wide * scale_rows[:, None] * gains[layer_index].astype(jnp.float32)).astype(jnp.bfloat16)
        slot_row_values = to_slots(normed)
        rank_latent = jnp.einsum('ilo,igo->ilg', slot_row_values.astype(jnp.float32), adapter_down_weights[layer_index].astype(jnp.float32)).astype(jnp.bfloat16)
        adapter_branch = (adapter_scale * jnp.einsum('yfh,yhv->yfv', rank_latent.astype(jnp.float32), adapter_up_weights[layer_index].astype(jnp.float32))).astype(jnp.bfloat16)
        kept.append((state, scale_rows, slot_row_values, rank_latent))
        state = (wide + from_slots(adapter_branch).astype(jnp.float32)).astype(jnp.bfloat16)
    grads_down = [None] * SECTION_LAYERS
    up_gradients = [None] * SECTION_LAYERS
    slopes = [None] * SECTION_LAYERS
    flowing = cotangent
    for layer_index in reversed(range(SECTION_LAYERS)):
        state, scale_rows, slot_row_values, rank_latent = kept[layer_index]
        wide = state.astype(jnp.float32)
        cotangent_rows = to_slots(flowing).astype(jnp.float32)
        up_gradients[layer_index] = adapter_scale * jnp.einsum('mjh,mjc->mhc', rank_latent.astype(jnp.float32), cotangent_rows)
        rank_gradient = (adapter_scale * jnp.einsum('ilo,igo->ilg', cotangent_rows, adapter_up_weights[layer_index].astype(jnp.float32))).astype(jnp.bfloat16)
        grads_down[layer_index] = jnp.einsum('mjh,mjc->mhc', rank_gradient.astype(jnp.float32), slot_row_values.astype(jnp.float32))
        normalized_gradient = jnp.einsum('yfh,yhv->yfv', rank_gradient.astype(jnp.float32), adapter_down_weights[layer_index].astype(jnp.float32)).astype(jnp.bfloat16)
        spread = from_slots(normalized_gradient).astype(jnp.float32) * gains[layer_index].astype(jnp.float32)
        product = lax.optimization_barrier(jnp.sum(spread * wide, 1)) / MODEL_WIDTH
        slopes[layer_index] = product * scale_rows * math.sqrt(MODEL_WIDTH)
        flowing = (flowing.astype(jnp.float32) + scale_rows[:, None] * spread - (scale_rows ** 3 * product)[:, None] * wide).astype(jnp.bfloat16)
    grad_down = jnp.stack(grads_down, 0).astype(jnp.bfloat16)
    grad_up = jnp.stack(up_gradients, 0).astype(jnp.bfloat16)
    norm_slopes = jnp.stack(slopes, 0).astype(jnp.float32)
    return (grad_down, grad_up, norm_slopes)
```

```python
import functools
import math

import jax
import jax.numpy as jnp
import numpy as np
from jax import lax
from jax.experimental import pallas as pl
from jax.experimental.pallas import tpu as pltpu
from jax.sharding import PartitionSpec as P

MTOK = 64
LANES = 128
TILE = 16
EPS = 1e-05
SCALE = 0.5
MESH = pl.DeviceIdType.MESH


def round_up(value, unit):
    return -(-value // unit) * unit


def matmul(a, b, contract):
    return lax.dot_general(a, b, (contract, ((), ())), preferred_element_type=jnp.float32)


def drain(ref, sem):
    pltpu.make_async_copy(ref, ref, sem).wait()


def peers(axis):
    count, me = lax.axis_size(axis), lax.axis_index(axis)
    return [(o - 1, lax.rem(me + o, count)) for o in range(1, count)]


def kernel(
    cap,
    own_col,
    own_row,
    choose_row,
    gains,
    down,
    compact,
    tokens,
    cotangent,
    up,
    grad_down,
    grad_up,
    slopes,
    sendbuf,
    recvbuf,
    tokv,
    cotv,
    down_scaled,
    w_down,
    w_up,
    p1,
    f1,
    p2,
    f2,
    q1,
    h1,
    q2,
    h2,
    xs,
    zs,
    rs,
    cur,
    first_cot,
    mask,
    back_d,
    back_u,
    slope_rows,
    loc_sem,
    tok_s,
    tok_r,
    wd_s,
    wu_s,
    wd_r,
    wu_r,
    ss1,
    rs1,
    ss2,
    rs2,
    gd_s,
    gu_s,
    gd_r,
    gu_r,
    sl_s,
    sl_r,
):
    dp = lax.axis_index("dp")
    section = lax.axis_index("section")
    groups = lax.axis_size("dp")
    layers = lax.axis_size("section")
    count = tokens.shape[0]
    fw = tokv.shape[1]
    width = tokens.shape[1] * lax.axis_size("tensor")
    spad = sendbuf.shape[1]
    slots = xs.shape[1]
    half = slots // 2

    barrier = pltpu.get_barrier_semaphore()
    greeted = 0
    for axis in ("tensor", "section", "dp"):
        for _, peer in peers(axis):
            pl.semaphore_signal(barrier, inc=1, device_id={axis: peer}, device_id_type=MESH)
            greeted += 1

    def columns(index):
        return pl.ds(pl.multiple_of(index * fw, LANES), fw)

    tok_copy = pltpu.make_async_copy(tokens.at[:, columns(section)], tokv, loc_sem.at[0])
    cot_copy = pltpu.make_async_copy(cotangent.at[:, columns(section)], cotv, loc_sem.at[1])
    tok_copy.start()
    cot_copy.start()

    early = lax.broadcasted_iota(jnp.int32, (count, count), 0)
    late = lax.broadcasted_iota(jnp.int32, (count, count), 1)
    shift = MTOK.bit_length() - 1
    before = (own_col[...] == own_row[...]) & (early < late) & ((early >> shift) == (late >> shift))
    rank_in = jnp.sum(jnp.where(before, 1.0, 0.0), 0, keepdims=True)
    micro_of = (lax.broadcasted_iota(jnp.int32, (1, count), 1) >> shift).astype(jnp.float32)
    place = micro_of * cap + rank_in
    spots = lax.broadcasted_iota(jnp.int32, (spad, count), 0).astype(jnp.float32)
    fits = place == spots
    member = jnp.concatenate(
        [jnp.where(fits & (own_row[...] == d), 1.0, 0.0) for d in range(groups)], 0
    )
    flag = jnp.sum(member * choose_row[...].astype(jnp.float32), 1, keepdims=True)
    member = member.astype(jnp.bfloat16)

    tok_copy.wait()
    cot_copy.wait()
    contract_mid = ((1,), (0,))
    sendbuf[:, :, 0:fw] = (
        matmul(member, tokv[...], contract_mid).astype(jnp.bfloat16).reshape(groups, spad, fw)
    )
    sendbuf[:, :, fw : 2 * fw] = (
        matmul(member, cotv[...], contract_mid).astype(jnp.bfloat16).reshape(groups, spad, fw)
    )
    sendbuf[:, :, 2 * fw :] = (
        jnp.broadcast_to(flag, (groups * spad, LANES))
        .astype(jnp.bfloat16)
        .reshape(groups, spad, LANES)
    )

    pl.semaphore_wait(barrier, greeted)

    for _, peer in peers("dp"):
        pltpu.make_async_remote_copy(
            sendbuf.at[peer], recvbuf.at[dp], tok_s, tok_r, {"dp": peer}, MESH
        ).start()
    recvbuf[dp] = sendbuf[dp]

    down_scaled[...] = (down[...].astype(jnp.float32) * gains[...].astype(jnp.float32)).astype(
        jnp.bfloat16
    )
    for source, target, send, recv in (
        (down_scaled, w_down, wd_s, wd_r),
        (up, w_up, wu_s, wu_r),
    ):
        for _, peer in peers("section"):
            pltpu.make_async_remote_copy(
                source.at[:, columns(peer)],
                target.at[section],
                send,
                recv.at[section],
                {"section": peer},
                MESH,
            ).start()
        pltpu.make_async_copy(
            source.at[:, columns(section)], target.at[section], recv.at[section]
        ).start()

    drain(recvbuf.at[pl.ds(0, groups - 1)], tok_r)
    arrived = matmul(
        compact[...], recvbuf[...].reshape(groups * spad, 2 * fw + LANES), contract_mid
    )
    cur[...] = arrived[:, 0:fw]
    first_cot[...] = arrived[:, fw : 2 * fw]
    lane = lax.broadcasted_iota(jnp.int32, (slots, LANES), 1)
    second = arrived[:, 2 * fw :] > 0.5
    mask[...] = jnp.where(second == (lane >= LANES // 2), 1.0, 0.0)

    low = lax.broadcasted_iota(jnp.int32, (half, LANES), 1) < LANES // 2
    tall = lax.broadcasted_iota(jnp.int32, (TILE, LANES), 1)

    def packed(total):
        kept = total * mask[...]
        both = kept + pltpu.roll(kept, LANES // 2, 1)
        return jnp.where(low, both[0:half], both[half:])

    def unpacked(total):
        turned = pltpu.roll(total, LANES // 2, 1)
        both = jnp.concatenate(
            [jnp.where(low, total, turned), jnp.where(low, turned, total)], 0
        )
        return both * mask[...]

    def start_stage(axis, layer, slot, mine, theirs, send, recv):
        for place_at, peer in peers(axis):
            pltpu.make_async_remote_copy(
                mine.at[layer],
                theirs.at[layer, place_at],
                send,
                recv.at[slot],
                {axis: peer},
                MESH,
            ).start()

    def end_stage(layer, slot, theirs, recv):
        drain(theirs.at[layer], recv.at[slot])
        return sum(theirs[layer, i].astype(jnp.float32) for i in range(theirs.shape[1]))

    def forward(layer, _):
        x = cur[...]
        x_low = x.astype(jnp.bfloat16)
        xs[layer] = x_low
        squares = jnp.sum(x * x, 1, keepdims=True)
        folded = jnp.zeros((TILE, LANES), jnp.float32)
        for q in range(slots // TILE):
            folded = jnp.where(tall == q, squares[q * TILE : (q + 1) * TILE], folded)
        drain(w_down.at[layer], wd_r.at[layer])
        part = packed(matmul(x_low, w_down[layer], ((1,), (1,))))
        part = jnp.concatenate([part, folded], 0)
        p1[layer] = part.astype(jnp.bfloat16)
        start_stage("tensor", layer, layer, p1, f1, ss1, rs1)
        part = part + end_stage(layer, layer, f1, rs1)
        p2[layer] = part.astype(jnp.bfloat16)
        start_stage("section", layer, layer, p2, f2, ss2, rs2)
        part = part + end_stage(layer, layer, f2, rs2)
        folded = part[half:]
        squares = jnp.concatenate(
            [
                jnp.sum(jnp.where(tall == q, folded, 0.0), 1, keepdims=True)
                for q in range(slots // TILE)
            ],
            0,
        )
        scale_rows = lax.rsqrt(squares / width + EPS)
        rs[layer] = jnp.broadcast_to(scale_rows, (slots, LANES))
        latent = (unpacked(part[0:half]) * scale_rows).astype(jnp.bfloat16)
        zs[layer] = latent
        drain(w_up.at[layer], wu_r.at[layer])

        @pl.when(layer < layers - 1)
        def _():
            cur[...] = x + SCALE * matmul(latent, w_up[layer], contract_mid)

        return 0

    lax.fori_loop(0, layers, forward, 0)

    cur[...] = first_cot[...]

    def give_back(layer, product, store, target, send, recv):
        store[layer] = product.astype(jnp.bfloat16)

        @pl.when(layer == section)
        def _():
            pltpu.make_async_copy(store.at[layer], target.at[:, columns(section)], recv).start()

        @pl.when(layer != section)
        def _():
            pltpu.make_async_remote_copy(
                store.at[layer],
                target.at[:, columns(section)],
                send,
                recv,
                {"section": layer},
                MESH,
            ).start()

    contract_rows = ((0,), (0,))

    def backward(step, rank_gradient):
        layer = layers - 1 - step
        g = cur[...]
        g_low = g.astype(jnp.bfloat16)
        part = packed(matmul(g_low, w_up[layer], ((1,), (1,))))
        q1[layer] = part.astype(jnp.bfloat16)
        start_stage("tensor", layer, layers + layer, q1, h1, ss1, rs1)
        latent = zs[layer]
        give_back(
            layer,
            SCALE * matmul(latent, g_low, contract_rows),
            back_u,
            grad_up,
            gu_s,
            gu_r,
        )
        part = part + end_stage(layer, layers + layer, h1, rs1)
        q2[layer] = part.astype(jnp.bfloat16)
        start_stage("section", layer, layers + layer, q2, h2, ss2, rs2)

        @pl.when(step > 0)
        def _():
            give_back(
                layer + 1,
                matmul(rank_gradient, xs[layer + 1], contract_rows),
                back_d,
                grad_down,
                gd_s,
                gd_r,
            )

        part = part + end_stage(layer, layers + layer, h2, rs2)
        rank_low = (SCALE * unpacked(part)).astype(jnp.bfloat16)
        scale_rows = rs[layer][:, 0:1]
        product = rank_low.astype(jnp.float32) * latent.astype(jnp.float32)
        slope_rows[layer, :, 0:slots] = lax.dot_general(
            jnp.full((8, LANES), 1.0 / math.sqrt(width), jnp.float32),
            product,
            (((1,), (1,)), ((), ())),
            preferred_element_type=jnp.float32,
            precision=lax.Precision.HIGHEST,
        )

        @pl.when(layer > 0)
        def _():
            inner = jnp.sum(product, 1, keepdims=True) / width
            cur[...] = (
                g
                + scale_rows * matmul(rank_low, w_down[layer], contract_mid)
                - (scale_rows * scale_rows * inner) * xs[layer].astype(jnp.float32)
            )

        return (rank_low.astype(jnp.float32) * scale_rows).astype(jnp.bfloat16)

    rank_gradient = lax.fori_loop(
        0, layers, backward, jnp.zeros((slots, LANES), jnp.bfloat16)
    )
    give_back(0, matmul(rank_gradient, xs[0], contract_rows), back_d, grad_down, gd_s, gd_r)

    for _, peer in peers("dp"):
        pltpu.make_async_remote_copy(
            slope_rows.at[section], slopes.at[dp], sl_s, sl_r, {"dp": peer}, MESH
        ).start()
    slopes[dp] = slope_rows[section]

    drain(recvbuf.at[pl.ds(0, groups - 1)], tok_s)
    drain(w_down.at[pl.ds(0, layers - 1)], wd_s)
    drain(w_up.at[pl.ds(0, layers - 1)], wu_s)
    drain(f1, ss1)
    drain(h1, ss1)
    drain(f2, ss2)
    drain(h2, ss2)
    drain(back_d.at[pl.ds(0, layers - 1)], gd_s)
    drain(back_u.at[pl.ds(0, layers - 1)], gu_s)
    drain(slopes.at[pl.ds(0, groups - 1)], sl_s)
    drain(grad_up, gu_r)
    drain(grad_down, gd_r)
    drain(slopes.at[pl.ds(0, groups - 1)], sl_r)


def on_device(
    tokens,
    owner_indices,
    local_adapter_index,
    gains,
    adapter_down_weights,
    adapter_up_weights,
    cotangent,
):
    groups, layers, ranks = (lax.axis_size(a) for a in ("dp", "section", "tensor"))
    count, local = tokens.shape
    micro = count // MTOK
    cap = 5 * MTOK // (4 * groups)
    each = micro * cap
    spad = round_up(each, TILE)
    slots = groups * each
    fw = local // layers
    adapters, rank = adapter_down_weights.shape[1:3]
    rows = adapters * rank
    half = slots // 2
    down = adapter_down_weights.reshape(rows, local)
    up = adapter_up_weights.reshape(rows, local)
    own_row = owner_indices.reshape(1, count)
    choose_row = local_adapter_index.reshape(1, count)
    slot_ids = np.arange(slots)
    compact = np.zeros((slots, groups * spad), np.float32)
    compact[slot_ids, slot_ids // each * spad + slot_ids % each] = 1.0
    wide = round_up(slots, LANES)
    vmem = pl.BlockSpec(memory_space=pltpu.VMEM)
    anywhere = pl.BlockSpec(memory_space=pl.ANY)
    b16, f32 = jnp.bfloat16, jnp.float32
    dma = pltpu.SemaphoreType.DMA
    high = half + TILE
    grad_down, grad_up, slopes = pl.pallas_call(
        functools.partial(kernel, cap),
        out_shape=(
            jax.ShapeDtypeStruct((rows, local), b16),
            jax.ShapeDtypeStruct((rows, local), b16),
            jax.ShapeDtypeStruct((groups, 8, wide), f32),
        ),
        in_specs=[vmem] * 6 + [anywhere] * 3,
        out_specs=(vmem, vmem, vmem),
        scratch_shapes=[
            pltpu.VMEM((groups, spad, 2 * fw + LANES), b16),
            pltpu.VMEM((groups, spad, 2 * fw + LANES), b16),
            pltpu.VMEM((count, fw), b16),
            pltpu.VMEM((count, fw), b16),
            pltpu.VMEM((rows, local), b16),
            pltpu.VMEM((layers, rows, fw), b16),
            pltpu.VMEM((layers, rows, fw), b16),
            pltpu.VMEM((layers, high, LANES), b16),
            pltpu.VMEM((layers, ranks - 1, high, LANES), b16),
            pltpu.VMEM((layers, high, LANES), b16),
            pltpu.VMEM((layers, layers - 1, high, LANES), b16),
            pltpu.VMEM((layers, half, LANES), b16),
            pltpu.VMEM((layers, ranks - 1, half, LANES), b16),
            pltpu.VMEM((layers, half, LANES), b16),
            pltpu.VMEM((layers, layers - 1, half, LANES), b16),
            pltpu.VMEM((layers, slots, fw), b16),
            pltpu.VMEM((layers, slots, LANES), b16),
            pltpu.VMEM((layers, slots, LANES), f32),
            pltpu.VMEM((slots, fw), f32),
            pltpu.VMEM((slots, fw), f32),
            pltpu.VMEM((slots, LANES), f32),
            pltpu.VMEM((layers, rows, fw), b16),
            pltpu.VMEM((layers, rows, fw), b16),
            pltpu.VMEM((layers, 8, wide), f32),
            dma((2,)),
            dma,
            dma,
            dma,
            dma,
            dma((layers,)),
            dma((layers,)),
            dma,
            dma((2 * layers,)),
            dma,
            dma((2 * layers,)),
            dma,
            dma,
            dma,
            dma,
            dma,
            dma,
        ],
        compiler_params=pltpu.CompilerParams(
            collective_id=0, has_side_effects=True, vmem_limit_bytes=40 * 1024 * 1024
        ),
    )(
        owner_indices,
        own_row,
        choose_row,
        gains,
        down,
        jnp.asarray(compact, b16),
        tokens,
        cotangent,
        up,
    )
    grad_down = (grad_down.astype(f32) * gains.astype(f32)).astype(b16)
    own = owner_indices[:, 0]
    own_micro = own.reshape(micro, MTOK)
    same = own_micro[:, :, None] == own_micro[:, None, :]
    earlier = jnp.arange(MTOK)[:, None] > jnp.arange(MTOK)[None, :]
    rank_in = jnp.sum((same & earlier).astype(jnp.int32), 2).reshape(count)
    spot = lax.axis_index("dp") * each + jnp.arange(count) // MTOK * cap + rank_in
    here = (jnp.arange(groups)[None, :, None] == own[:, None, None]) & (
        jnp.arange(wide)[None, None, :] == spot[:, None, None]
    )
    slope = jnp.sum(jnp.where(here, slopes[None, :, 0, :], 0.0), (1, 2))
    shape = (1, adapters, rank, local)
    return (grad_down.reshape(shape), grad_up.reshape(shape), slope[None])


def solution(mesh):
    return jax.shard_map(
        on_device,
        mesh=mesh,
        in_specs=(
            P("dp", "tensor"),
            P("dp", None),
            P("dp"),
            P("section", "tensor"),
            P("section", "dp", None, "tensor"),
            P("section", "dp", None, "tensor"),
            P("dp", "tensor"),
        ),
        out_specs=(
            P("section", "dp", None, "tensor"),
            P("section", "dp", None, "tensor"),
            P("section", "dp"),
        ),
        check_vma=False,
    )
```

```python
import functools
import math

import jax
import jax.numpy as jnp
import numpy as np
from jax import lax
from jax.experimental import pallas as pl
from jax.experimental.pallas import tpu as pltpu
from jax.sharding import PartitionSpec as P

MTOK = 64
LANES = 128
TILE = 16
EPS = 1e-05
SCALE = 0.5
MESH = pl.DeviceIdType.MESH
NN = ((1,), (0,))
NT = ((1,), (1,))
TN = ((0,), (0,))


def round_up(value, unit):
    return -(-value // unit) * unit


def matmul(a, b, contract):
    return lax.dot_general(a, b, (contract, ((), ())), preferred_element_type=jnp.float32)


def drain(ref, sem):
    pltpu.make_async_copy(ref, ref, sem).wait()


def peers(axis):
    count, me = lax.axis_size(axis), lax.axis_index(axis)
    return [lax.rem(me + o, count) for o in range(1, count)]


def payload_rows(layers, half, rank):
    at, rows = {}, 0
    at["squares"], rows = rows, rows + TILE
    for name, count in (("p", layers), ("q", layers - 1), ("r", layers)):
        at[name], rows = rows, rows + count * half
    for k in range(layers - 1):
        for name, others in (("m", range(k + 1, layers)), ("u", range(k, layers - 1))):
            for other in others:
                at[name, k, other], rows = rows, rows + rank
    return at, rows


def kernel(
    cap,
    own,
    choose,
    gains,
    down,
    compact,
    tokens,
    cotangent,
    up,
    grad_down,
    grad_up,
    slope_out,
    own_v,
    choose_v,
    gains_v,
    down_v,
    compact_v,
    tokv,
    cotv,
    sendbuf,
    recvbuf,
    down_scaled,
    w_down,
    w_up,
    part,
    fin,
    got,
    got_y,
    acc_p,
    acc_q,
    acc_w,
    seen,
    big_m,
    big_u,
    xs,
    zs,
    rd,
    es,
    prods,
    first_x,
    first_cot,
    mask,
    back_d,
    back_u,
    slope_row,
    slopes,
    loc_sem,
    tok_s,
    tok_r,
    wd_s,
    wu_s,
    wd_r,
    wu_r,
    ar_s,
    ar_r,
    gd_s,
    gu_s,
    gd_r,
    gu_r,
    sl_s,
    sl_r,
):
    dp = lax.axis_index("dp")
    section = lax.axis_index("section")
    tensor = lax.axis_index("tensor")
    groups = lax.axis_size("dp")
    layers = lax.axis_size("section")
    ranks = lax.axis_size("tensor")
    bits = ranks.bit_length() - 1
    count = tokens.shape[0]
    fw = tokv.shape[1]
    width = tokens.shape[1] * ranks
    spad = sendbuf.shape[1]
    slots = xs.shape[1]
    half = slots // 2
    rank = LANES // 2
    each = slots // groups
    bf16, f32 = jnp.bfloat16, jnp.float32
    at, _ = payload_rows(layers, half, rank)

    barrier = pltpu.get_barrier_semaphore()
    greeted = 0
    for axis in ("tensor", "section", "dp"):
        for peer in peers(axis):
            pl.semaphore_signal(barrier, inc=1, device_id={axis: peer}, device_id_type=MESH)
            greeted += 1

    def columns(index):
        return pl.ds(pl.multiple_of(index * fw, LANES), fw)

    loads = [
        pltpu.make_async_copy(source, target, loc_sem.at[i])
        for i, (source, target) in enumerate(
            (
                (own, own_v),
                (choose, choose_v),
                (tokens.at[:, columns(section)], tokv),
                (cotangent.at[:, columns(section)], cotv),
                (gains, gains_v),
                (down, down_v),
                (compact, compact_v),
            )
        )
    ]
    for load in loads:
        load.start()

    early = lax.broadcasted_iota(jnp.int32, (count, count), 0)
    late = lax.broadcasted_iota(jnp.int32, (count, count), 1)
    diagonal = early == late
    shift = MTOK.bit_length() - 1
    loads[0].wait()
    loads[1].wait()
    own_row = own_v[...].astype(f32)
    own_col = jnp.sum(jnp.where(diagonal, own_row, 0.0), 1, keepdims=True)
    before = (own_col == own_row) & (early < late) & ((early >> shift) == (late >> shift))
    rank_in = jnp.sum(jnp.where(before, 1.0, 0.0), 0, keepdims=True)
    micro_of = (lax.broadcasted_iota(jnp.int32, (1, count), 1) >> shift).astype(f32)
    place = micro_of * cap + rank_in
    spots = lax.broadcasted_iota(jnp.int32, (spad, count), 0).astype(f32)
    fits = place == spots
    member = jnp.concatenate(
        [jnp.where(fits & (own_row == d), 1.0, 0.0) for d in range(groups)], 0
    )
    flag = jnp.sum(member * choose_v[...].astype(f32), 1, keepdims=True)
    member = member.astype(bf16)
    loads[2].wait()
    loads[3].wait()
    sendbuf[:, :, 0:fw] = matmul(member, tokv[...], NN).astype(bf16).reshape(groups, spad, fw)
    sendbuf[:, :, fw : 2 * fw] = (
        matmul(member, cotv[...], NN).astype(bf16).reshape(groups, spad, fw)
    )
    sendbuf[:, :, 2 * fw :] = (
        jnp.broadcast_to(flag, (groups * spad, LANES)).astype(bf16).reshape(groups, spad, LANES)
    )

    pl.semaphore_wait(barrier, greeted)

    for peer in peers("dp"):
        pltpu.make_async_remote_copy(
            sendbuf.at[peer], recvbuf.at[dp], tok_s, tok_r, {"dp": peer}, MESH
        ).start()
    recvbuf[dp] = sendbuf[dp]

    def spread(source, target, send, recv):
        for peer in peers("section"):
            pltpu.make_async_remote_copy(
                source.at[:, columns(peer)],
                target.at[section],
                send,
                recv.at[section],
                {"section": peer},
                MESH,
            ).start()
        pltpu.make_async_copy(
            source.at[:, columns(section)], target.at[section], recv.at[section]
        ).start()

    spread(up, w_up, wu_s, wu_r)
    for load in loads[4:]:
        load.wait()
    down_scaled[...] = (down_v[...].astype(f32) * gains_v[...].astype(f32)).astype(bf16)
    spread(down_scaled, w_down, wd_s, wd_r)

    drain(recvbuf.at[pl.ds(0, groups - 1)], tok_r)
    arrived = matmul(compact_v[...], recvbuf[...].reshape(groups * spad, 2 * fw + LANES), NN)
    x0 = arrived[:, 0:fw]
    first_x[...] = x0
    first_cot[...] = arrived[:, fw : 2 * fw]
    lane = lax.broadcasted_iota(jnp.int32, (slots, LANES), 1)
    second = arrived[:, 2 * fw :] > 0.5
    mask[...] = jnp.where(second == (lane >= rank), 1.0, 0.0)

    low = lax.broadcasted_iota(jnp.int32, (half, LANES), 1) < rank
    low_rank = lax.broadcasted_iota(jnp.int32, (rank, LANES), 1) < rank
    tall = lax.broadcasted_iota(jnp.int32, (TILE, LANES), 1)

    def packed(total):
        kept = total * mask[...]
        both = kept + pltpu.roll(kept, rank, 1)
        return jnp.where(low, both[0:half], both[half:])

    def unpacked(total):
        turned = pltpu.roll(total, rank, 1)
        both = jnp.concatenate([jnp.where(low, total, turned), jnp.where(low, turned, total)], 0)
        return both * mask[...]

    squares = jnp.sum(x0 * x0, 1, keepdims=True)
    folded = jnp.zeros((TILE, LANES), f32)
    for q in range(slots // TILE):
        folded = jnp.where(tall == q, squares[q * TILE : (q + 1) * TILE], folded)
    part[0:TILE] = folded.astype(bf16)

    for layer in range(layers):
        drain(w_up.at[layer], wu_r.at[layer])
    x_low = first_x[...].astype(bf16)
    cot_low = first_cot[...].astype(bf16)
    for layer in range(layers):
        weight = w_up[layer]
        if layer < layers - 1:
            row = at["q"] + layer * half
            part[row : row + half] = packed(matmul(x_low, weight, NT)).astype(bf16)
        row = at["r"] + layer * half
        part[row : row + half] = packed(matmul(cot_low, weight, NT)).astype(bf16)

    def pairs(name, k, others, weights):
        first, last = others[0], others[-1] + 1
        stacked = weights[first:last].reshape((last - first) * LANES, fw)
        product = matmul(w_up[k], stacked, NT)
        for i, other in enumerate(others):
            block = product[:, i * LANES : (i + 1) * LANES]
            row = at[name, k, other]
            part[row : row + rank] = jnp.where(low_rank, block[0:rank], block[rank:]).astype(bf16)

    for k in range(layers - 1):
        pairs("u", k, range(k, layers - 1), w_up)
    for layer in range(layers):
        drain(w_down.at[layer], wd_r.at[layer])
    for layer in range(layers):
        row = at["p"] + layer * half
        part[row : row + half] = packed(matmul(x_low, w_down[layer], NT)).astype(bf16)
    for k in range(layers - 1):
        pairs("m", k, range(k + 1, layers), w_down)

    total_rows = part.shape[0]
    piece = total_rows // (ranks * layers)

    def rows(first, size):
        return pl.ds(pl.multiple_of(first, TILE), size)

    base, size, stage, starts = 0, total_rows, 0, []
    for bit in range(bits):
        size //= 2
        mine = (tensor >> bit) & 1
        keep, give = base + mine * size, base + (1 - mine) * size
        peer = tensor ^ (1 << bit)
        spot = total_rows - 2 * size
        pltpu.make_async_remote_copy(
            part.at[rows(give, size)],
            got.at[pl.ds(spot, size)],
            ar_s.at[stage],
            ar_r.at[stage],
            {"tensor": peer},
            MESH,
        ).start()
        drain(got.at[pl.ds(spot, size)], ar_r.at[stage])
        part[rows(keep, size)] = (
            part[rows(keep, size)].astype(f32) + got[spot : spot + size].astype(f32)
        ).astype(bf16)
        starts.append((keep, size, peer))
        base, stage = keep, stage + 1
    for o, peer in enumerate(peers("section")):
        pltpu.make_async_remote_copy(
            part.at[rows(base + peer * piece, piece)],
            got_y.at[o],
            ar_s.at[stage],
            ar_r.at[stage],
            {"section": peer},
            MESH,
        ).start()
    drain(got_y, ar_r.at[stage])
    mine = base + section * piece
    total = part[rows(mine, piece)].astype(f32)
    for o in range(layers - 1):
        total += got_y[o].astype(f32)
    fin[rows(mine, piece)] = total.astype(bf16)
    stage += 1
    for peer in peers("section"):
        pltpu.make_async_remote_copy(
            fin.at[rows(mine, piece)],
            fin.at[rows(mine, piece)],
            ar_s.at[stage],
            ar_r.at[stage],
            {"section": peer},
            MESH,
        ).start()
    drain(fin.at[pl.ds(0, (layers - 1) * piece)], ar_r.at[stage])
    stage += 1
    for keep, size, peer in reversed(starts):
        pltpu.make_async_remote_copy(
            fin.at[rows(keep, size)],
            fin.at[rows(keep, size)],
            ar_s.at[stage],
            ar_r.at[stage],
            {"tensor": peer},
            MESH,
        ).start()
        drain(fin.at[pl.ds(0, size)], ar_r.at[stage])
        stage += 1

    def lanes(first, last=None):
        return slice(first * LANES, (first + 1 if last is None else last) * LANES)

    for name, target, number in (
        ("p", acc_p, layers),
        ("q", acc_q, layers - 1),
        ("r", acc_w, layers),
    ):
        for layer in range(number):
            row = at[name] + layer * half
            target[:, lanes(layer)] = unpacked(fin[row : row + half].astype(f32))
    for k in range(layers - 1):
        for name, target, others in (
            ("m", big_m, range(k + 1, layers)),
            ("u", big_u, range(k, layers - 1)),
        ):
            for other in others:
                row = at[name, k, other]
                block = fin[row : row + rank]
                zero = jnp.zeros_like(block)
                target[k, 0:rank, lanes(other)] = jnp.where(low_rank, block, zero)
                target[k, rank:, lanes(other)] = jnp.where(low_rank, zero, block)
    folded = fin[0:TILE].astype(f32)
    squares = jnp.concatenate(
        [
            jnp.sum(jnp.where(tall == q, folded, 0.0), 1, keepdims=True)
            for q in range(slots // TILE)
        ],
        0,
    )

    scales = []
    for k in range(layers):
        scale_rows = lax.rsqrt(squares / width + EPS)
        scales.append(scale_rows)
        latent = (acc_p[:, lanes(k)] * scale_rows).astype(bf16)
        zs[k] = latent
        if k == layers - 1:
            break
        if k < layers - 1:
            acc_p[:, lanes(k + 1, layers)] += SCALE * matmul(
                latent, big_m[k, :, lanes(k + 1, layers)], NN
            )
            inner = acc_q[:, lanes(k)]
            step = SCALE * matmul(latent, big_u[k, :, lanes(k, layers - 1)], NN)
            squares = jnp.maximum(
                squares
                + jnp.sum(
                    latent.astype(f32) * (inner + 0.5 * step[:, 0:LANES]), 1, keepdims=True
                ),
                0.0,
            )
            acc_q[:, lanes(k, layers - 1)] += step
            if k > 0:
                others = big_u[0:k, :, lanes(k)].reshape(k * LANES, LANES)
                acc_q[:, lanes(0, k)] += SCALE * matmul(latent, others, NT)
            seen[k + 1, :, lanes(0, k + 1)] = acc_q[:, lanes(0, k + 1)].astype(bf16)

    for m in reversed(range(layers)):
        rank_low = (SCALE * acc_w[:, lanes(m)]).astype(bf16)
        product = rank_low.astype(f32) * zs[m].astype(f32)
        prods[m] = product
        scale_rows = scales[m]
        scaled = (rank_low.astype(f32) * scale_rows).astype(bf16)
        rd[m] = scaled
        if m > 0:
            weight = scale_rows * scale_rows * jnp.sum(product, 1, keepdims=True) / width
            es[m] = jnp.broadcast_to(weight, (slots, LANES))
            others = big_m[0:m, :, lanes(m)].reshape(m * LANES, LANES)
            acc_w[:, lanes(0, m)] += matmul(scaled, others, NT) - weight * seen[
                m, :, lanes(0, m)
            ].astype(f32)

    slope_row[:, 0:slots] = lax.dot_general(
        jnp.full((8, LANES), 1.0 / math.sqrt(width), f32),
        prods[section],
        (NT, ((), ())),
        preferred_element_type=f32,
        precision=lax.Precision.HIGHEST,
    )
    for peer in peers("dp"):
        pltpu.make_async_remote_copy(
            slope_row, slopes.at[dp], sl_s, sl_r, {"dp": peer}, MESH
        ).start()
    slopes[dp] = slope_row[...]

    x = first_x[...]
    for layer in range(layers):
        xs[layer] = x.astype(bf16)
        if layer < layers - 1:
            x = x + SCALE * matmul(zs[layer], w_up[layer], NN)

    def give_back(layer, product, store, target, send, recv):
        store[layer] = product.astype(bf16)

        @pl.when(section == layer)
        def _():
            pltpu.make_async_copy(store.at[layer], target.at[:, columns(section)], recv).start()

        @pl.when(section != layer)
        def _():
            pltpu.make_async_remote_copy(
                store.at[layer],
                target.at[:, columns(section)],
                send,
                recv,
                {"section": layer},
                MESH,
            ).start()

    g = first_cot[...]
    for layer in reversed(range(layers)):
        g_low = g.astype(bf16)
        give_back(layer, SCALE * matmul(zs[layer], g_low, TN), back_u, grad_up, gu_s, gu_r)
        give_back(layer, matmul(rd[layer], xs[layer], TN), back_d, grad_down, gd_s, gd_r)
        if layer > 0:
            g = (
                g
                + matmul(rd[layer], w_down[layer], NN)
                - es[layer][:, 0:1] * xs[layer].astype(f32)
            )

    drain(recvbuf.at[pl.ds(0, groups - 1)], tok_s)
    drain(w_down.at[pl.ds(0, layers - 1)], wd_s)
    drain(w_up.at[pl.ds(0, layers - 1)], wu_s)
    stage = 0
    for _, size, _ in starts:
        drain(got.at[pl.ds(0, size)], ar_s.at[stage])
        stage += 1
    for _ in range(2):
        drain(got_y, ar_s.at[stage])
        stage += 1
    for _, size, _ in reversed(starts):
        drain(got.at[pl.ds(0, size)], ar_s.at[stage])
        stage += 1
    drain(back_d.at[pl.ds(0, layers - 1)], gd_s)
    drain(back_u.at[pl.ds(0, layers - 1)], gu_s)
    drain(slopes.at[pl.ds(0, groups - 1)], sl_s)

    drain(slopes.at[pl.ds(0, groups - 1)], sl_r)
    wide = slopes.shape[2]
    found = jnp.zeros((count, wide), f32)
    for d in range(groups):
        found = jnp.where(own_col == d, slopes[d, 0:1], found)
    first_slot = (dp * each).astype(f32)
    place_col = jnp.sum(jnp.where(diagonal, place, 0.0), 1, keepdims=True) + first_slot
    here = lax.broadcasted_iota(jnp.int32, (count, wide), 1).astype(f32) == place_col
    slope_col = jnp.sum(jnp.where(here, found, 0.0), 1, keepdims=True)
    slope_out[...] = jnp.sum(jnp.where(diagonal, slope_col, 0.0), 0, keepdims=True)

    drain(grad_up, gu_r)
    drain(grad_down, gd_r)


def on_device(
    tokens,
    owner_indices,
    local_adapter_index,
    gains,
    adapter_down_weights,
    adapter_up_weights,
    cotangent,
):
    groups, layers, ranks = (lax.axis_size(a) for a in ("dp", "section", "tensor"))
    count, local = tokens.shape
    micro = count // MTOK
    cap = 5 * MTOK // (4 * groups)
    each = micro * cap
    spad = round_up(each, TILE)
    slots = groups * each
    fw = local // layers
    adapters, rank = adapter_down_weights.shape[1:3]
    weight_rows = adapters * rank
    half = slots // 2
    slot_ids = np.arange(slots)
    compact = np.zeros((slots, groups * spad), np.float32)
    compact[slot_ids, slot_ids // each * spad + slot_ids % each] = 1.0
    wide = round_up(slots, LANES)
    _, rows = payload_rows(layers, half, rank)
    rows = round_up(rows, TILE * layers * ranks)
    piece = rows // (layers * ranks)
    stages = 2 * (ranks.bit_length() - 1) + 2
    vmem = pl.BlockSpec(memory_space=pltpu.VMEM)
    anywhere = pl.BlockSpec(memory_space=pl.ANY)
    b16, f32 = jnp.bfloat16, jnp.float32
    dma = pltpu.SemaphoreType.DMA
    grad_down, grad_up, slope = pl.pallas_call(
        functools.partial(kernel, cap),
        out_shape=(
            jax.ShapeDtypeStruct((weight_rows, local), b16),
            jax.ShapeDtypeStruct((weight_rows, local), b16),
            jax.ShapeDtypeStruct((1, count), f32),
        ),
        in_specs=[anywhere] * 8,
        out_specs=(vmem, vmem, vmem),
        scratch_shapes=[
            pltpu.VMEM((1, count), jnp.int32),
            pltpu.VMEM((1, count), jnp.int32),
            pltpu.VMEM((1, local), b16),
            pltpu.VMEM((weight_rows, local), b16),
            pltpu.VMEM(compact.shape, b16),
            pltpu.VMEM((count, fw), b16),
            pltpu.VMEM((count, fw), b16),
            pltpu.VMEM((groups, spad, 2 * fw + LANES), b16),
            pltpu.VMEM((groups, spad, 2 * fw + LANES), b16),
            pltpu.VMEM((weight_rows, local), b16),
            pltpu.VMEM((layers, weight_rows, fw), b16),
            pltpu.VMEM((layers, weight_rows, fw), b16),
            pltpu.VMEM((rows, LANES), b16),
            pltpu.VMEM((rows, LANES), b16),
            pltpu.VMEM((rows, LANES), b16),
            pltpu.VMEM((layers - 1, piece, LANES), b16),
            pltpu.VMEM((slots, layers * LANES), f32),
            pltpu.VMEM((slots, layers * LANES), f32),
            pltpu.VMEM((slots, layers * LANES), f32),
            pltpu.VMEM((layers, slots, layers * LANES), b16),
            pltpu.VMEM((layers, LANES, layers * LANES), b16),
            pltpu.VMEM((layers, LANES, layers * LANES), b16),
            pltpu.VMEM((layers, slots, fw), b16),
            pltpu.VMEM((layers, slots, LANES), b16),
            pltpu.VMEM((layers, slots, LANES), b16),
            pltpu.VMEM((layers, slots, LANES), f32),
            pltpu.VMEM((layers, slots, LANES), f32),
            pltpu.VMEM((slots, fw), f32),
            pltpu.VMEM((slots, fw), f32),
            pltpu.VMEM((slots, LANES), f32),
            pltpu.VMEM((layers, weight_rows, fw), b16),
            pltpu.VMEM((layers, weight_rows, fw), b16),
            pltpu.VMEM((8, wide), f32),
            pltpu.VMEM((groups, 8, wide), f32),
            dma((7,)),
            dma,
            dma,
            dma,
            dma,
            dma((layers,)),
            dma((layers,)),
            dma((stages,)),
            dma((stages,)),
            dma,
            dma,
            dma,
            dma,
            dma,
            dma,
        ],
        compiler_params=pltpu.CompilerParams(
            collective_id=0, has_side_effects=True, vmem_limit_bytes=48 * 1024 * 1024
        ),
    )(
        owner_indices.reshape(1, count),
        local_adapter_index.reshape(1, count),
        gains,
        adapter_down_weights.reshape(weight_rows, local),
        jnp.asarray(compact, b16),
        tokens,
        cotangent,
        adapter_up_weights.reshape(weight_rows, local),
    )
    grad_down = (grad_down.astype(f32) * gains.astype(f32)).astype(b16)
    shape = (1, adapters, rank, local)
    return (grad_down.reshape(shape), grad_up.reshape(shape), slope)


def solution(mesh):
    return jax.shard_map(
        on_device,
        mesh=mesh,
        in_specs=(
            P("dp", "tensor"),
            P("dp", None),
            P("dp"),
            P("section", "tensor"),
            P("section", "dp", None, "tensor"),
            P("section", "dp", None, "tensor"),
            P("dp", "tensor"),
        ),
        out_specs=(
            P("section", "dp", None, "tensor"),
            P("section", "dp", None, "tensor"),
            P("section", "dp"),
        ),
        check_vma=False,
    )
```

```python
import functools
import math

import jax
import jax.numpy as jnp
import numpy as np
from jax import lax
from jax.experimental import pallas as pl
from jax.experimental.pallas import tpu as pltpu
from jax.sharding import PartitionSpec as P

MTOK = 64
LANES = 128
TILE = 16
EPS = 1e-05
SCALE = 0.5
MESH = pl.DeviceIdType.MESH
NN = ((1,), (0,))
NT = ((1,), (1,))
TN = ((0,), (0,))


def round_up(value, unit):
    return -(-value // unit) * unit


def matmul(a, b, contract):
    return lax.dot_general(a, b, (contract, ((), ())), preferred_element_type=jnp.float32)


def drain(ref, sem):
    pltpu.make_async_copy(ref, ref, sem).wait()


def peers(axis):
    count, me = lax.axis_size(axis), lax.axis_index(axis)
    return [lax.rem(me + o, count) for o in range(1, count)]


def payload_rows(layers, half, rank, unit):
    at, ends = {}, []
    at["squares"], rows = 0, TILE
    for number, name, count in (("u", "q", layers - 1), ("m", "p", layers)):
        at[name], rows = rows, rows + count * half
        if number == "u":
            at["r"], rows = rows, rows + layers * half
        for k in range(layers - 1):
            for other in range(k, layers - 1) if number == "u" else range(k + 1, layers):
                at[number, k, other], rows = rows, rows + rank
        rows = round_up(rows, unit)
        ends.append(rows)
    return at, ends


def kernel(
    cap,
    own,
    choose,
    gains,
    down,
    compact,
    tokens,
    cotangent,
    up,
    grad_down,
    grad_up,
    slope_out,
    own_v,
    choose_v,
    gains_v,
    down_v,
    compact_v,
    tokv,
    cotv,
    sendbuf,
    recvbuf,
    down_scaled,
    w_down,
    w_up,
    part,
    fin,
    got,
    got_y,
    acc_p,
    acc_q,
    acc_w,
    seen,
    big_m,
    big_u,
    xs,
    gs,
    zs,
    rd,
    es,
    prods,
    first_x,
    first_cot,
    mask,
    back_d,
    back_u,
    slope_row,
    slopes,
    loc_sem,
    tok_s,
    tok_r,
    wd_s,
    wu_s,
    wd_r,
    wu_r,
    ar_s,
    ar_r,
    gd_s,
    gu_s,
    gd_r,
    gu_r,
    sl_s,
    sl_r,
):
    dp = lax.axis_index("dp")
    section = lax.axis_index("section")
    tensor = lax.axis_index("tensor")
    groups = lax.axis_size("dp")
    layers = lax.axis_size("section")
    ranks = lax.axis_size("tensor")
    bits = ranks.bit_length() - 1
    count = tokens.shape[0]
    fw = tokv.shape[1]
    width = tokens.shape[1] * ranks
    spad = sendbuf.shape[1]
    slots = xs.shape[1]
    half = slots // 2
    rank = LANES // 2
    each = slots // groups
    bf16, f32 = jnp.bfloat16, jnp.float32
    at, ends = payload_rows(layers, half, rank, TILE * layers * ranks)

    barrier = pltpu.get_barrier_semaphore()
    greeted = 0
    for axis in ("tensor", "section", "dp"):
        for peer in peers(axis):
            pl.semaphore_signal(barrier, inc=1, device_id={axis: peer}, device_id_type=MESH)
            greeted += 1

    def columns(index):
        return pl.ds(pl.multiple_of(index * fw, LANES), fw)

    loads = [
        pltpu.make_async_copy(source, target, loc_sem.at[i])
        for i, (source, target) in enumerate(
            (
                (own, own_v),
                (choose, choose_v),
                (tokens.at[:, columns(section)], tokv),
                (cotangent.at[:, columns(section)], cotv),
                (gains, gains_v),
                (down, down_v),
                (compact, compact_v),
            )
        )
    ]
    for load in loads:
        load.start()

    pl.semaphore_wait(barrier, greeted)

    def spread(source, target, send, recv):
        for peer in peers("section"):
            pltpu.make_async_remote_copy(
                source.at[:, columns(peer)],
                target.at[section],
                send,
                recv.at[section],
                {"section": peer},
                MESH,
            ).start()
        pltpu.make_async_copy(
            source.at[:, columns(section)], target.at[section], recv.at[section]
        ).start()

    spread(up, w_up, wu_s, wu_r)
    for load in loads[4:]:
        load.wait()
    down_scaled[...] = (down_v[...].astype(f32) * gains_v[...].astype(f32)).astype(bf16)
    spread(down_scaled, w_down, wd_s, wd_r)

    early = lax.broadcasted_iota(jnp.int32, (count, count), 0)
    late = lax.broadcasted_iota(jnp.int32, (count, count), 1)
    diagonal = early == late
    shift = MTOK.bit_length() - 1
    loads[0].wait()
    loads[1].wait()
    own_row = own_v[...].astype(f32)
    own_col = jnp.sum(jnp.where(diagonal, own_row, 0.0), 1, keepdims=True)
    before = (own_col == own_row) & (early < late) & ((early >> shift) == (late >> shift))
    rank_in = jnp.sum(jnp.where(before, 1.0, 0.0), 0, keepdims=True)
    micro_of = (lax.broadcasted_iota(jnp.int32, (1, count), 1) >> shift).astype(f32)
    place = micro_of * cap + rank_in
    spots = lax.broadcasted_iota(jnp.int32, (spad, count), 0).astype(f32)
    fits = place == spots
    member = jnp.concatenate(
        [jnp.where(fits & (own_row == d), 1.0, 0.0) for d in range(groups)], 0
    )
    flag = jnp.sum(member * choose_v[...].astype(f32), 1, keepdims=True)
    member = member.astype(bf16)
    loads[2].wait()
    loads[3].wait()
    sendbuf[:, :, 0:fw] = matmul(member, tokv[...], NN).astype(bf16).reshape(groups, spad, fw)
    sendbuf[:, :, fw : 2 * fw] = (
        matmul(member, cotv[...], NN).astype(bf16).reshape(groups, spad, fw)
    )
    sendbuf[:, :, 2 * fw :] = (
        jnp.broadcast_to(flag, (groups * spad, LANES)).astype(bf16).reshape(groups, spad, LANES)
    )

    for peer in peers("dp"):
        pltpu.make_async_remote_copy(
            sendbuf.at[peer], recvbuf.at[dp], tok_s, tok_r, {"dp": peer}, MESH
        ).start()
    recvbuf[dp] = sendbuf[dp]

    drain(recvbuf.at[pl.ds(0, groups - 1)], tok_r)
    arrived = matmul(compact_v[...], recvbuf[...].reshape(groups * spad, 2 * fw + LANES), NN)
    x0 = arrived[:, 0:fw]
    first_x[...] = x0
    first_cot[...] = arrived[:, fw : 2 * fw]
    lane = lax.broadcasted_iota(jnp.int32, (slots, LANES), 1)
    second = arrived[:, 2 * fw :] > 0.5
    mask[...] = jnp.where(second == (lane >= rank), 1.0, 0.0)

    low = lax.broadcasted_iota(jnp.int32, (half, LANES), 1) < rank
    low_rank = lax.broadcasted_iota(jnp.int32, (rank, LANES), 1) < rank
    tall = lax.broadcasted_iota(jnp.int32, (TILE, LANES), 1)

    def packed(total):
        kept = total * mask[...]
        both = kept + pltpu.roll(kept, rank, 1)
        return jnp.where(low, both[0:half], both[half:])

    def unpacked(total):
        turned = pltpu.roll(total, rank, 1)
        both = jnp.concatenate([jnp.where(low, total, turned), jnp.where(low, turned, total)], 0)
        return both * mask[...]

    squares = jnp.sum(x0 * x0, 1, keepdims=True)
    folded = jnp.zeros((TILE, LANES), f32)
    for q in range(slots // TILE):
        folded = jnp.where(tall == q, squares[q * TILE : (q + 1) * TILE], folded)
    part[0:TILE] = folded.astype(bf16)

    for layer in range(layers):
        drain(w_up.at[layer], wu_r.at[layer])
    x_low = first_x[...].astype(bf16)
    cot_low = first_cot[...].astype(bf16)
    for layer in range(layers):
        weight = w_up[layer]
        if layer < layers - 1:
            row = at["q"] + layer * half
            part[row : row + half] = packed(matmul(x_low, weight, NT)).astype(bf16)
        row = at["r"] + layer * half
        part[row : row + half] = packed(matmul(cot_low, weight, NT)).astype(bf16)

    def pairs(name, k, others, weights):
        first, last = others[0], others[-1] + 1
        stacked = weights[first:last].reshape((last - first) * LANES, fw)
        product = matmul(w_up[k], stacked, NT)
        for i, other in enumerate(others):
            block = product[:, i * LANES : (i + 1) * LANES]
            row = at[name, k, other]
            part[row : row + rank] = jnp.where(low_rank, block[0:rank], block[rank:]).astype(bf16)

    for k in range(layers - 1):
        pairs("u", k, range(k, layers - 1), w_up)

    def rows(first, size):
        return pl.ds(pl.multiple_of(first, TILE), size)

    def all_reduce(chunk):
        first = ends[chunk - 1] if chunk else 0
        size = ends[chunk] - first
        whole, piece, y_first = size, size // (ranks * layers), first // (ranks * layers)
        base, stage, starts = first, 0, []
        sends, arrivals = ar_s.at[chunk], ar_r.at[chunk]

        def send(source, target, device):
            pltpu.make_async_remote_copy(
                source, target, sends.at[stage], arrivals.at[stage], device, MESH
            ).start()

        for bit in range(bits):
            size //= 2
            mine = (tensor >> bit) & 1
            keep, give = base + mine * size, base + (1 - mine) * size
            peer = tensor ^ (1 << bit)
            spot = first + whole - 2 * size
            send(part.at[rows(give, size)], got.at[pl.ds(spot, size)], {"tensor": peer})
            yield
            drain(got.at[pl.ds(spot, size)], arrivals.at[stage])
            part[rows(keep, size)] = (
                part[rows(keep, size)].astype(f32) + got[spot : spot + size].astype(f32)
            ).astype(bf16)
            starts.append((keep, size, peer))
            base, stage = keep, stage + 1
        for o, peer in enumerate(peers("section")):
            send(
                part.at[rows(base + peer * piece, piece)],
                got_y.at[o, pl.ds(y_first, piece)],
                {"section": peer},
            )
        yield
        drain(fin.at[pl.ds(first, (layers - 1) * piece)], arrivals.at[stage])
        stage += 1
        mine = base + section * piece
        total = part[rows(mine, piece)].astype(f32)
        for o in range(layers - 1):
            total += got_y[o, y_first : y_first + piece].astype(f32)
        fin[rows(mine, piece)] = total.astype(bf16)
        for peer in peers("section"):
            send(fin.at[rows(mine, piece)], fin.at[rows(mine, piece)], {"section": peer})
        yield
        drain(fin.at[pl.ds(first, (layers - 1) * piece)], arrivals.at[stage])
        stage += 1
        for keep, size, peer in reversed(starts):
            send(fin.at[rows(keep, size)], fin.at[rows(keep, size)], {"tensor": peer})
            yield
            drain(fin.at[pl.ds(first, size)], arrivals.at[stage])
            stage += 1
        sizes = [size for _, size, _ in starts]
        y_size = (layers - 1) * piece
        for i, size in enumerate([*sizes, y_size, y_size, *reversed(sizes)]):
            sent.append((first, size, sends.at[i]))

    sent = []
    early_half, late_half = all_reduce(0), all_reduce(1)

    def advance(*halves):
        for chunk in halves:
            next(chunk, None)

    for _ in range(bits + 1):
        advance(early_half)
    for layer in range(layers):
        drain(w_down.at[layer], wd_r.at[layer])
    for layer in range(layers):
        row = at["p"] + layer * half
        part[row : row + half] = packed(matmul(x_low, w_down[layer], NT)).astype(bf16)
    for k in range(layers - 1):
        pairs("m", k, range(k + 1, layers), w_down)
    for _ in range(bits):
        advance(late_half)
    for _ in range(2):
        advance(early_half, late_half)
    for _ in range(bits):
        advance(early_half, late_half)
    advance(late_half)

    def lanes(first, last=None):
        return slice(first * LANES, (first + 1 if last is None else last) * LANES)

    for name, target, number in (
        ("p", acc_p, layers),
        ("q", acc_q, layers - 1),
        ("r", acc_w, layers),
    ):
        for layer in range(number):
            row = at[name] + layer * half
            target[:, lanes(layer)] = unpacked(fin[row : row + half].astype(f32))
    for k in range(layers - 1):
        for name, target, others in (
            ("m", big_m, range(k + 1, layers)),
            ("u", big_u, range(k, layers - 1)),
        ):
            for other in others:
                row = at[name, k, other]
                block = fin[row : row + rank]
                zero = jnp.zeros_like(block)
                target[k, 0:rank, lanes(other)] = jnp.where(low_rank, block, zero)
                target[k, rank:, lanes(other)] = jnp.where(low_rank, zero, block)
    folded = fin[0:TILE].astype(f32)
    squares = jnp.concatenate(
        [
            jnp.sum(jnp.where(tall == q, folded, 0.0), 1, keepdims=True)
            for q in range(slots // TILE)
        ],
        0,
    )

    scales = []
    for k in range(layers):
        scale_rows = lax.rsqrt(squares / width + EPS)
        scales.append(scale_rows)
        latent = (acc_p[:, lanes(k)] * scale_rows).astype(bf16)
        zs[k] = latent
        if k == layers - 1:
            break
        if k < layers - 1:
            acc_p[:, lanes(k + 1, layers)] += SCALE * matmul(
                latent, big_m[k, :, lanes(k + 1, layers)], NN
            )
            inner = acc_q[:, lanes(k)]
            step = SCALE * matmul(latent, big_u[k, :, lanes(k, layers - 1)], NN)
            squares = jnp.maximum(
                squares
                + jnp.sum(
                    latent.astype(f32) * (inner + 0.5 * step[:, 0:LANES]), 1, keepdims=True
                ),
                0.0,
            )
            acc_q[:, lanes(k, layers - 1)] += step
            if k > 0:
                others = big_u[0:k, :, lanes(k)].reshape(k * LANES, LANES)
                acc_q[:, lanes(0, k)] += SCALE * matmul(latent, others, NT)
            seen[k + 1, :, lanes(0, k + 1)] = acc_q[:, lanes(0, k + 1)].astype(bf16)

    for m in reversed(range(layers)):
        rank_low = (SCALE * acc_w[:, lanes(m)]).astype(bf16)
        product = rank_low.astype(f32) * zs[m].astype(f32)
        prods[m] = product
        scale_rows = scales[m]
        scaled = (rank_low.astype(f32) * scale_rows).astype(bf16)
        rd[m] = scaled
        if m > 0:
            weight = scale_rows * scale_rows * jnp.sum(product, 1, keepdims=True) / width
            es[m] = jnp.broadcast_to(weight, (slots, LANES))
            others = big_m[0:m, :, lanes(m)].reshape(m * LANES, LANES)
            acc_w[:, lanes(0, m)] += matmul(scaled, others, NT) - weight * seen[
                m, :, lanes(0, m)
            ].astype(f32)

    slope_row[:, 0:slots] = lax.dot_general(
        jnp.full((8, LANES), 1.0 / math.sqrt(width), f32),
        prods[section],
        (NT, ((), ())),
        preferred_element_type=f32,
        precision=lax.Precision.HIGHEST,
    )
    for peer in peers("dp"):
        pltpu.make_async_remote_copy(
            slope_row, slopes.at[dp], sl_s, sl_r, {"dp": peer}, MESH
        ).start()
    slopes[dp] = slope_row[...]

    x = first_x[...]
    for layer in range(layers):
        xs[layer] = x.astype(bf16)
        if layer < layers - 1:
            x = x + SCALE * matmul(zs[layer], w_up[layer], NN)

    def give_back(product, store, target, send, recv):
        store[section] = product(section).astype(bf16)
        pltpu.make_async_copy(store.at[section], target.at[:, columns(section)], recv).start()
        for layer in peers("section"):
            store[layer] = product(layer).astype(bf16)
            pltpu.make_async_remote_copy(
                store.at[layer],
                target.at[:, columns(section)],
                send,
                recv,
                {"section": layer},
                MESH,
            ).start()

    give_back(lambda layer: matmul(rd[layer], xs[layer], TN), back_d, grad_down, gd_s, gd_r)
    g = first_cot[...]
    for layer in reversed(range(layers)):
        gs[layer] = g.astype(bf16)
        if layer > 0:
            g = (
                g
                + matmul(rd[layer], w_down[layer], NN)
                - es[layer][:, 0:1] * xs[layer].astype(f32)
            )
    give_back(lambda layer: SCALE * matmul(zs[layer], gs[layer], TN), back_u, grad_up, gu_s, gu_r)

    drain(recvbuf.at[pl.ds(0, groups - 1)], tok_s)
    drain(w_down.at[pl.ds(0, layers - 1)], wd_s)
    drain(w_up.at[pl.ds(0, layers - 1)], wu_s)
    for first, size, sem in sent:
        drain(fin.at[pl.ds(first, size)], sem)
    drain(back_d.at[pl.ds(0, layers - 1)], gd_s)
    drain(back_u.at[pl.ds(0, layers - 1)], gu_s)
    drain(slopes.at[pl.ds(0, groups - 1)], sl_s)

    drain(slopes.at[pl.ds(0, groups - 1)], sl_r)
    wide = slopes.shape[2]
    found = jnp.zeros((count, wide), f32)
    for d in range(groups):
        found = jnp.where(own_col == d, slopes[d, 0:1], found)
    first_slot = (dp * each).astype(f32)
    place_col = jnp.sum(jnp.where(diagonal, place, 0.0), 1, keepdims=True) + first_slot
    here = lax.broadcasted_iota(jnp.int32, (count, wide), 1).astype(f32) == place_col
    slope_col = jnp.sum(jnp.where(here, found, 0.0), 1, keepdims=True)
    slope_out[...] = jnp.sum(jnp.where(diagonal, slope_col, 0.0), 0, keepdims=True)

    drain(grad_up, gu_r)
    drain(grad_down, gd_r)


def on_device(
    tokens,
    owner_indices,
    local_adapter_index,
    gains,
    adapter_down_weights,
    adapter_up_weights,
    cotangent,
):
    groups, layers, ranks = (lax.axis_size(a) for a in ("dp", "section", "tensor"))
    count, local = tokens.shape
    micro = count // MTOK
    cap = 5 * MTOK // (4 * groups)
    each = micro * cap
    spad = round_up(each, TILE)
    slots = groups * each
    fw = local // layers
    adapters, rank = adapter_down_weights.shape[1:3]
    weight_rows = adapters * rank
    half = slots // 2
    slot_ids = np.arange(slots)
    compact = np.zeros((slots, groups * spad), np.float32)
    compact[slot_ids, slot_ids // each * spad + slot_ids % each] = 1.0
    wide = round_up(slots, LANES)
    _, ends = payload_rows(layers, half, rank, TILE * layers * ranks)
    rows = ends[-1]
    piece = rows // (layers * ranks)
    stages = 2 * (ranks.bit_length() - 1) + 2
    vmem = pl.BlockSpec(memory_space=pltpu.VMEM)
    anywhere = pl.BlockSpec(memory_space=pltpu.HBM)
    b16, f32 = jnp.bfloat16, jnp.float32
    dma = pltpu.SemaphoreType.DMA
    grad_down, grad_up, slope = pl.pallas_call(
        functools.partial(kernel, cap),
        out_shape=(
            jax.ShapeDtypeStruct((weight_rows, local), b16),
            jax.ShapeDtypeStruct((weight_rows, local), b16),
            jax.ShapeDtypeStruct((1, count), f32),
        ),
        in_specs=[anywhere] * 8,
        out_specs=(vmem, vmem, vmem),
        scratch_shapes=[
            pltpu.VMEM((1, count), jnp.int32),
            pltpu.VMEM((1, count), jnp.int32),
            pltpu.VMEM((1, local), b16),
            pltpu.VMEM((weight_rows, local), b16),
            pltpu.VMEM(compact.shape, b16),
            pltpu.VMEM((count, fw), b16),
            pltpu.VMEM((count, fw), b16),
            pltpu.VMEM((groups, spad, 2 * fw + LANES), b16),
            pltpu.VMEM((groups, spad, 2 * fw + LANES), b16),
            pltpu.VMEM((weight_rows, local), b16),
            pltpu.VMEM((layers, weight_rows, fw), b16),
            pltpu.VMEM((layers, weight_rows, fw), b16),
            pltpu.VMEM((rows, LANES), b16),
            pltpu.VMEM((rows, LANES), b16),
            pltpu.VMEM((rows, LANES), b16),
            pltpu.VMEM((layers - 1, piece, LANES), b16),
            pltpu.VMEM((slots, layers * LANES), f32),
            pltpu.VMEM((slots, layers * LANES), f32),
            pltpu.VMEM((slots, layers * LANES), f32),
            pltpu.VMEM((layers, slots, layers * LANES), b16),
            pltpu.VMEM((layers, LANES, layers * LANES), b16),
            pltpu.VMEM((layers, LANES, layers * LANES), b16),
            pltpu.VMEM((layers, slots, fw), b16),
            pltpu.VMEM((layers, slots, fw), b16),
            pltpu.VMEM((layers, slots, LANES), b16),
            pltpu.VMEM((layers, slots, LANES), b16),
            pltpu.VMEM((layers, slots, LANES), f32),
            pltpu.VMEM((layers, slots, LANES), f32),
            pltpu.VMEM((slots, fw), f32),
            pltpu.VMEM((slots, fw), f32),
            pltpu.VMEM((slots, LANES), f32),
            pltpu.VMEM((layers, weight_rows, fw), b16),
            pltpu.VMEM((layers, weight_rows, fw), b16),
            pltpu.VMEM((8, wide), f32),
            pltpu.VMEM((groups, 8, wide), f32),
            dma((7,)),
            dma,
            dma,
            dma,
            dma,
            dma((layers,)),
            dma((layers,)),
            dma((2, stages)),
            dma((2, stages)),
            dma,
            dma,
            dma,
            dma,
            dma,
            dma,
        ],
        compiler_params=pltpu.CompilerParams(
            collective_id=0, has_side_effects=True, vmem_limit_bytes=48 * 1024 * 1024
        ),
    )(
        owner_indices.reshape(1, count),
        local_adapter_index.reshape(1, count),
        gains,
        adapter_down_weights.reshape(weight_rows, local),
        jnp.asarray(compact, b16),
        tokens,
        cotangent,
        adapter_up_weights.reshape(weight_rows, local),
    )
    grad_down = (grad_down.astype(f32) * gains.astype(f32)).astype(b16)
    shape = (1, adapters, rank, local)
    return (grad_down.reshape(shape), grad_up.reshape(shape), slope)


def solution(mesh):
    return jax.shard_map(
        on_device,
        mesh=mesh,
        in_specs=(
            P("dp", "tensor"),
            P("dp", None),
            P("dp"),
            P("section", "tensor"),
            P("section", "dp", None, "tensor"),
            P("section", "dp", None, "tensor"),
            P("dp", "tensor"),
        ),
        out_specs=(
            P("section", "dp", None, "tensor"),
            P("section", "dp", None, "tensor"),
            P("section", "dp"),
        ),
        check_vma=False,
    )
```

```python
import functools
import math

import jax
import jax.numpy as jnp
from jax import lax
from jax.experimental import pallas as pl
from jax.experimental.pallas import tpu as pltpu
from jax.sharding import PartitionSpec as P

MTOK = 64
LANES = 128
TILE = 16
EPS = 1e-05
SCALE = 0.5
MESH = pl.DeviceIdType.MESH
NN = ((1,), (0,))
NT = ((1,), (1,))
TN = ((0,), (0,))


def round_up(value, unit):
    return -(-value // unit) * unit


def matmul(a, b, contract):
    return lax.dot_general(a, b, (contract, ((), ())), preferred_element_type=jnp.float32)


def drain(ref, sem):
    pltpu.make_async_copy(ref, ref, sem).wait()


def peers(axis):
    count, me = lax.axis_size(axis), lax.axis_index(axis)
    return [lax.rem(me + o, count) for o in range(1, count)]


def payload_rows(layers, half, rank, unit):
    at, ends = {}, []
    at["squares"], rows = 0, TILE
    for number, name, count in (("u", "q", layers - 1), ("m", "p", layers)):
        at[name], rows = rows, rows + count * half
        if number == "u":
            at["r"], rows = rows, rows + layers * half
        for k in range(layers - 1):
            for other in range(k, layers - 1) if number == "u" else range(k + 1, layers):
                at[number, k, other], rows = rows, rows + rank
        rows = round_up(rows, unit)
        ends.append(rows)
    return at, ends


def kernel(
    cap,
    own,
    choose,
    gains,
    down,
    tokens,
    cotangent,
    up,
    grad_down,
    grad_up,
    slope_out,
    own_v,
    choose_v,
    gains_v,
    down_v,
    tokv,
    cotv,
    sendbuf,
    recvbuf,
    gains_wide,
    w_gain,
    down_scaled,
    w_down,
    w_up,
    part,
    fin,
    got,
    got_y,
    acc_p,
    acc_q,
    acc_w,
    seen,
    big_m,
    big_u,
    xs,
    gs,
    zs,
    rd,
    es,
    prods,
    first_x,
    first_cot,
    mask,
    back_d,
    back_u,
    slope_row,
    slopes,
    loc_sem,
    tok_s,
    tok_r,
    wd_s,
    wu_s,
    wg_s,
    wd_r,
    wu_r,
    wg_r,
    ar_s,
    ar_r,
    gd_s,
    gu_s,
    gd_r,
    gu_r,
    sl_s,
    sl_r,
):
    dp = lax.axis_index("dp")
    section = lax.axis_index("section")
    tensor = lax.axis_index("tensor")
    groups = lax.axis_size("dp")
    layers = lax.axis_size("section")
    ranks = lax.axis_size("tensor")
    bits = ranks.bit_length() - 1
    count = tokens.shape[0]
    fw = tokv.shape[1]
    width = tokens.shape[1] * ranks
    spad = sendbuf.shape[1]
    slots = xs.shape[1]
    half = slots // 2
    rank = LANES // 2
    each = slots // groups
    bf16, f32 = jnp.bfloat16, jnp.float32
    at, ends = payload_rows(layers, half, rank, TILE * layers * ranks)

    barrier = pltpu.get_barrier_semaphore()
    greeted = 0
    for axis in ("tensor", "section", "dp"):
        for peer in peers(axis):
            pl.semaphore_signal(barrier, inc=1, device_id={axis: peer}, device_id_type=MESH)
            greeted += 1

    def columns(index):
        return pl.ds(pl.multiple_of(index * fw, LANES), fw)

    loads = [
        pltpu.make_async_copy(source, target, loc_sem.at[i])
        for i, (source, target) in enumerate(
            (
                (own, own_v),
                (choose, choose_v),
                (tokens.at[:, columns(section)], tokv),
                (cotangent.at[:, columns(section)], cotv),
                (gains, gains_v),
                (down, down_v),
            )
        )
    ]
    for load in loads:
        load.start()

    pl.semaphore_wait(barrier, greeted)

    def spread(source, target, send, recv):
        for peer in peers("section"):
            pltpu.make_async_remote_copy(
                source.at[:, columns(peer)],
                target.at[section],
                send,
                recv.at[section],
                {"section": peer},
                MESH,
            ).start()
        pltpu.make_async_copy(
            source.at[:, columns(section)], target.at[section], recv.at[section]
        ).start()

    spread(up, w_up, wu_s, wu_r)
    for load in loads[4:]:
        load.wait()
    down_scaled[...] = (down_v[...].astype(f32) * gains_v[...].astype(f32)).astype(bf16)
    spread(down_scaled, w_down, wd_s, wd_r)
    gains_wide[...] = jnp.broadcast_to(gains_v[...], gains_wide.shape)
    spread(gains_wide, w_gain, wg_s, wg_r)

    early = lax.broadcasted_iota(jnp.int32, (count, count), 0)
    late = lax.broadcasted_iota(jnp.int32, (count, count), 1)
    diagonal = early == late
    shift = MTOK.bit_length() - 1
    loads[0].wait()
    loads[1].wait()
    own_row = own_v[...].astype(f32)
    own_col = jnp.sum(jnp.where(diagonal, own_row, 0.0), 1, keepdims=True)
    before = (own_col == own_row) & (early < late) & ((early >> shift) == (late >> shift))
    rank_in = jnp.sum(jnp.where(before, 1.0, 0.0), 0, keepdims=True)
    micro_of = (lax.broadcasted_iota(jnp.int32, (1, count), 1) >> shift).astype(f32)
    place = micro_of * cap + rank_in
    spots = lax.broadcasted_iota(jnp.int32, (spad, count), 0).astype(f32)
    fits = place == spots
    member = jnp.concatenate(
        [jnp.where(fits & (own_row == d), 1.0, 0.0) for d in range(groups)], 0
    )
    flag = jnp.sum(member * choose_v[...].astype(f32), 1, keepdims=True)
    member = member.astype(bf16)
    loads[2].wait()
    loads[3].wait()
    sendbuf[:, :, 0:fw] = matmul(member, tokv[...], NN).astype(bf16).reshape(groups, spad, fw)
    sendbuf[:, :, fw : 2 * fw] = (
        matmul(member, cotv[...], NN).astype(bf16).reshape(groups, spad, fw)
    )
    sendbuf[:, :, 2 * fw :] = (
        jnp.broadcast_to(flag, (groups * spad, LANES)).astype(bf16).reshape(groups, spad, LANES)
    )

    for peer in peers("dp"):
        pltpu.make_async_remote_copy(
            sendbuf.at[peer], recvbuf.at[dp], tok_s, tok_r, {"dp": peer}, MESH
        ).start()
    recvbuf[dp] = sendbuf[dp]

    cell = lax.broadcasted_iota(jnp.int32, (1, groups * spad), 1)
    source = sum((cell >= d * spad).astype(jnp.int32) for d in range(1, groups))
    within = cell - source * spad
    wanted = jnp.where(within < each, source * each + within, -1)
    slot_ids = lax.broadcasted_iota(jnp.int32, (slots, groups * spad), 0)
    compact = jnp.where(slot_ids == wanted, 1.0, 0.0).astype(bf16)
    drain(recvbuf.at[pl.ds(0, groups - 1)], tok_r)
    arrived = matmul(compact, recvbuf[...].reshape(groups * spad, 2 * fw + LANES), NN)
    x0 = arrived[:, 0:fw]
    first_x[...] = x0
    first_cot[...] = arrived[:, fw : 2 * fw]
    lane = lax.broadcasted_iota(jnp.int32, (slots, LANES), 1)
    second = arrived[:, 2 * fw :] > 0.5
    mask[...] = jnp.where(second == (lane >= rank), 1.0, 0.0)

    low = lax.broadcasted_iota(jnp.int32, (half, LANES), 1) < rank
    low_rank = lax.broadcasted_iota(jnp.int32, (rank, LANES), 1) < rank
    tall = lax.broadcasted_iota(jnp.int32, (TILE, LANES), 1)

    def packed(total):
        kept = total * mask[...]
        both = kept + pltpu.roll(kept, rank, 1)
        return jnp.where(low, both[0:half], both[half:])

    def unpacked(total):
        turned = pltpu.roll(total, rank, 1)
        both = jnp.concatenate([jnp.where(low, total, turned), jnp.where(low, turned, total)], 0)
        return both * mask[...]

    squares = jnp.sum(x0 * x0, 1, keepdims=True)
    folded = jnp.zeros((TILE, LANES), f32)
    for q in range(slots // TILE):
        folded = jnp.where(tall == q, squares[q * TILE : (q + 1) * TILE], folded)
    part[0:TILE] = folded.astype(bf16)

    for layer in range(layers):
        drain(w_up.at[layer], wu_r.at[layer])
    x_low = first_x[...].astype(bf16)
    cot_low = first_cot[...].astype(bf16)
    for layer in range(layers):
        weight = w_up[layer]
        if layer < layers - 1:
            row = at["q"] + layer * half
            part[row : row + half] = packed(matmul(x_low, weight, NT)).astype(bf16)
        row = at["r"] + layer * half
        part[row : row + half] = packed(matmul(cot_low, weight, NT)).astype(bf16)

    def pairs(name, k, others, weights):
        first, last = others[0], others[-1] + 1
        stacked = weights[first:last].reshape((last - first) * LANES, fw)
        product = matmul(w_up[k], stacked, NT)
        for i, other in enumerate(others):
            block = product[:, i * LANES : (i + 1) * LANES]
            row = at[name, k, other]
            part[row : row + rank] = jnp.where(low_rank, block[0:rank], block[rank:]).astype(bf16)

    for k in range(layers - 1):
        pairs("u", k, range(k, layers - 1), w_up)

    def rows(first, size):
        return pl.ds(pl.multiple_of(first, TILE), size)

    def all_reduce(chunk):
        first = ends[chunk - 1] if chunk else 0
        size = ends[chunk] - first
        whole, piece, y_first = size, size // (ranks * layers), first // (ranks * layers)
        base, stage, starts = first, 0, []
        sends, arrivals = ar_s.at[chunk], ar_r.at[chunk]

        def send(source, target, device):
            pltpu.make_async_remote_copy(
                source, target, sends.at[stage], arrivals.at[stage], device, MESH
            ).start()

        for bit in range(bits):
            size //= 2
            mine = (tensor >> bit) & 1
            keep, give = base + mine * size, base + (1 - mine) * size
            peer = tensor ^ (1 << bit)
            spot = first + whole - 2 * size
            send(part.at[rows(give, size)], got.at[pl.ds(spot, size)], {"tensor": peer})
            yield
            drain(got.at[pl.ds(spot, size)], arrivals.at[stage])
            part[rows(keep, size)] = (
                part[rows(keep, size)].astype(f32) + got[spot : spot + size].astype(f32)
            ).astype(bf16)
            starts.append((keep, size, peer))
            base, stage = keep, stage + 1
        for o, peer in enumerate(peers("section")):
            send(
                part.at[rows(base + peer * piece, piece)],
                got_y.at[o, pl.ds(y_first, piece)],
                {"section": peer},
            )
        yield
        drain(fin.at[pl.ds(first, (layers - 1) * piece)], arrivals.at[stage])
        stage += 1
        mine = base + section * piece
        total = part[rows(mine, piece)].astype(f32)
        for o in range(layers - 1):
            total += got_y[o, y_first : y_first + piece].astype(f32)
        fin[rows(mine, piece)] = total.astype(bf16)
        for peer in peers("section"):
            send(fin.at[rows(mine, piece)], fin.at[rows(mine, piece)], {"section": peer})
        yield
        drain(fin.at[pl.ds(first, (layers - 1) * piece)], arrivals.at[stage])
        stage += 1
        for keep, size, peer in reversed(starts):
            send(fin.at[rows(keep, size)], fin.at[rows(keep, size)], {"tensor": peer})
            yield
            drain(fin.at[pl.ds(first, size)], arrivals.at[stage])
            stage += 1
        sizes = [size for _, size, _ in starts]
        y_size = (layers - 1) * piece
        for i, size in enumerate([*sizes, y_size, y_size, *reversed(sizes)]):
            sent.append((first, size, sends.at[i]))

    sent = []
    early_half, late_half = all_reduce(0), all_reduce(1)

    def advance(*halves):
        for chunk in halves:
            next(chunk, None)

    for _ in range(bits + 1):
        advance(early_half)
    for layer in range(layers):
        drain(w_down.at[layer], wd_r.at[layer])
    for layer in range(layers):
        row = at["p"] + layer * half
        part[row : row + half] = packed(matmul(x_low, w_down[layer], NT)).astype(bf16)
    for k in range(layers - 1):
        pairs("m", k, range(k + 1, layers), w_down)
    for _ in range(bits):
        advance(late_half)
    for _ in range(2):
        advance(early_half, late_half)
    for _ in range(bits):
        advance(early_half, late_half)
    advance(late_half)

    def lanes(first, last=None):
        return slice(first * LANES, (first + 1 if last is None else last) * LANES)

    for name, target, number in (
        ("p", acc_p, layers),
        ("q", acc_q, layers - 1),
        ("r", acc_w, layers),
    ):
        for layer in range(number):
            row = at[name] + layer * half
            target[:, lanes(layer)] = unpacked(fin[row : row + half].astype(f32))
    for k in range(layers - 1):
        for name, target, others in (
            ("m", big_m, range(k + 1, layers)),
            ("u", big_u, range(k, layers - 1)),
        ):
            for other in others:
                row = at[name, k, other]
                block = fin[row : row + rank]
                zero = jnp.zeros_like(block)
                target[k, 0:rank, lanes(other)] = jnp.where(low_rank, block, zero)
                target[k, rank:, lanes(other)] = jnp.where(low_rank, zero, block)
    folded = fin[0:TILE].astype(f32)
    squares = jnp.concatenate(
        [
            jnp.sum(jnp.where(tall == q, folded, 0.0), 1, keepdims=True)
            for q in range(slots // TILE)
        ],
        0,
    )

    scales = []
    for k in range(layers):
        scale_rows = lax.rsqrt(squares / width + EPS)
        scales.append(scale_rows)
        latent = (acc_p[:, lanes(k)] * scale_rows).astype(bf16)
        zs[k] = latent
        if k == layers - 1:
            break
        if k < layers - 1:
            acc_p[:, lanes(k + 1, layers)] += SCALE * matmul(
                latent, big_m[k, :, lanes(k + 1, layers)], NN
            )
            inner = acc_q[:, lanes(k)]
            step = SCALE * matmul(latent, big_u[k, :, lanes(k, layers - 1)], NN)
            squares = jnp.maximum(
                squares
                + jnp.sum(
                    latent.astype(f32) * (inner + 0.5 * step[:, 0:LANES]), 1, keepdims=True
                ),
                0.0,
            )
            acc_q[:, lanes(k, layers - 1)] += step
            if k > 0:
                others = big_u[0:k, :, lanes(k)].reshape(k * LANES, LANES)
                acc_q[:, lanes(0, k)] += SCALE * matmul(latent, others, NT)
            seen[k + 1, :, lanes(0, k + 1)] = acc_q[:, lanes(0, k + 1)].astype(bf16)

    for m in reversed(range(layers)):
        rank_low = (SCALE * acc_w[:, lanes(m)]).astype(bf16)
        product = rank_low.astype(f32) * zs[m].astype(f32)
        prods[m] = product
        scale_rows = scales[m]
        scaled = (rank_low.astype(f32) * scale_rows).astype(bf16)
        rd[m] = scaled
        if m > 0:
            weight = scale_rows * scale_rows * jnp.sum(product, 1, keepdims=True) / width
            es[m] = jnp.broadcast_to(weight, (slots, LANES))
            others = big_m[0:m, :, lanes(m)].reshape(m * LANES, LANES)
            acc_w[:, lanes(0, m)] += matmul(scaled, others, NT) - weight * seen[
                m, :, lanes(0, m)
            ].astype(f32)

    slope_row[:, 0:slots] = lax.dot_general(
        jnp.full((8, LANES), 1.0 / math.sqrt(width), f32),
        prods[section],
        (NT, ((), ())),
        preferred_element_type=f32,
        precision=lax.Precision.HIGHEST,
    )
    for peer in peers("dp"):
        pltpu.make_async_remote_copy(
            slope_row, slopes.at[dp], sl_s, sl_r, {"dp": peer}, MESH
        ).start()
    slopes[dp] = slope_row[...]

    x = first_x[...]
    for layer in range(layers):
        xs[layer] = x.astype(bf16)
        if layer < layers - 1:
            x = x + SCALE * matmul(zs[layer], w_up[layer], NN)

    def give_back(product, store, target, send, recv):
        store[section] = product(section).astype(bf16)
        pltpu.make_async_copy(store.at[section], target.at[:, columns(section)], recv).start()
        for layer in peers("section"):
            store[layer] = product(layer).astype(bf16)
            pltpu.make_async_remote_copy(
                store.at[layer],
                target.at[:, columns(section)],
                send,
                recv,
                {"section": layer},
                MESH,
            ).start()

    for layer in range(layers):
        drain(w_gain.at[layer], wg_r.at[layer])
    give_back(
        lambda layer: matmul(rd[layer], xs[layer], TN) * w_gain[layer, 0:1].astype(f32),
        back_d,
        grad_down,
        gd_s,
        gd_r,
    )
    g = first_cot[...]
    for layer in reversed(range(layers)):
        gs[layer] = g.astype(bf16)
        if layer > 0:
            g = (
                g
                + matmul(rd[layer], w_down[layer], NN)
                - es[layer][:, 0:1] * xs[layer].astype(f32)
            )
    give_back(lambda layer: SCALE * matmul(zs[layer], gs[layer], TN), back_u, grad_up, gu_s, gu_r)

    drain(recvbuf.at[pl.ds(0, groups - 1)], tok_s)
    drain(w_down.at[pl.ds(0, layers - 1)], wd_s)
    drain(w_up.at[pl.ds(0, layers - 1)], wu_s)
    drain(w_gain.at[pl.ds(0, layers - 1)], wg_s)
    for first, size, sem in sent:
        drain(fin.at[pl.ds(first, size)], sem)
    drain(back_d.at[pl.ds(0, layers - 1)], gd_s)
    drain(back_u.at[pl.ds(0, layers - 1)], gu_s)
    drain(slopes.at[pl.ds(0, groups - 1)], sl_s)

    drain(slopes.at[pl.ds(0, groups - 1)], sl_r)
    wide = slopes.shape[2]
    found = jnp.zeros((count, wide), f32)
    for d in range(groups):
        found = jnp.where(own_col == d, slopes[d, 0:1], found)
    first_slot = (dp * each).astype(f32)
    place_col = jnp.sum(jnp.where(diagonal, place, 0.0), 1, keepdims=True) + first_slot
    here = lax.broadcasted_iota(jnp.int32, (count, wide), 1).astype(f32) == place_col
    slope_col = jnp.sum(jnp.where(here, found, 0.0), 1, keepdims=True)
    slope_out[...] = jnp.sum(jnp.where(diagonal, slope_col, 0.0), 0, keepdims=True)

    drain(grad_up, gu_r)
    drain(grad_down, gd_r)


def finish(raw_down, raw_up, raw_slope, grad_down, grad_up, slope, v_down, v_up, v_slope, loads, stores):
    parts = (loads.shape[0] - 1) // 2
    rows = grad_up.shape[0] // parts
    pieces = [(raw_slope, v_slope, slope)]
    for i in range(parts):
        some = pl.ds(i * rows, rows)
        pieces.append((raw_up.at[some], v_up.at[some], grad_up.at[some]))
        pieces.append((raw_down.at[some], v_down.at[some], grad_down.at[some]))
    reads = [
        pltpu.make_async_copy(source, through, loads.at[i])
        for i, (source, through, _) in enumerate(pieces)
    ]
    writes = [
        pltpu.make_async_copy(through, target, stores.at[i])
        for i, (_, through, target) in enumerate(pieces)
    ]
    for read in reads:
        read.start()
    for read, write in zip(reads, writes):
        read.wait()
        write.start()
    for write in writes:
        write.wait()


def on_device(
    tokens,
    owner_indices,
    local_adapter_index,
    gains,
    adapter_down_weights,
    adapter_up_weights,
    cotangent,
):
    groups, layers, ranks = (lax.axis_size(a) for a in ("dp", "section", "tensor"))
    count, local = tokens.shape
    micro = count // MTOK
    cap = 5 * MTOK // (4 * groups)
    each = micro * cap
    spad = round_up(each, TILE)
    slots = groups * each
    fw = local // layers
    adapters, rank = adapter_down_weights.shape[1:3]
    weight_rows = adapters * rank
    half = slots // 2
    wide = round_up(slots, LANES)
    _, ends = payload_rows(layers, half, rank, TILE * layers * ranks)
    rows = ends[-1]
    piece = rows // (layers * ranks)
    stages = 2 * (ranks.bit_length() - 1) + 2
    vmem = pl.BlockSpec(memory_space=pltpu.VMEM)
    anywhere = pl.BlockSpec(memory_space=pltpu.HBM)
    b16, f32 = jnp.bfloat16, jnp.float32
    dma = pltpu.SemaphoreType.DMA
    raw = pl.pallas_call(
        functools.partial(kernel, cap),
        out_shape=(
            jax.ShapeDtypeStruct((weight_rows, local), b16),
            jax.ShapeDtypeStruct((weight_rows, local), b16),
            jax.ShapeDtypeStruct((1, count), f32),
        ),
        in_specs=[anywhere] * 7,
        out_specs=(anywhere, anywhere, vmem),
        scratch_shapes=[
            pltpu.VMEM((1, count), jnp.int32),
            pltpu.VMEM((1, count), jnp.int32),
            pltpu.VMEM((1, local), b16),
            pltpu.VMEM((weight_rows, local), b16),
            pltpu.VMEM((count, fw), b16),
            pltpu.VMEM((count, fw), b16),
            pltpu.VMEM((groups, spad, 2 * fw + LANES), b16),
            pltpu.VMEM((groups, spad, 2 * fw + LANES), b16),
            pltpu.VMEM((TILE, local), b16),
            pltpu.VMEM((layers, TILE, fw), b16),
            pltpu.VMEM((weight_rows, local), b16),
            pltpu.VMEM((layers, weight_rows, fw), b16),
            pltpu.VMEM((layers, weight_rows, fw), b16),
            pltpu.VMEM((rows, LANES), b16),
            pltpu.VMEM((rows, LANES), b16),
            pltpu.VMEM((rows, LANES), b16),
            pltpu.VMEM((layers - 1, piece, LANES), b16),
            pltpu.VMEM((slots, layers * LANES), f32),
            pltpu.VMEM((slots, layers * LANES), f32),
            pltpu.VMEM((slots, layers * LANES), f32),
            pltpu.VMEM((layers, slots, layers * LANES), b16),
            pltpu.VMEM((layers, LANES, layers * LANES), b16),
            pltpu.VMEM((layers, LANES, layers * LANES), b16),
            pltpu.VMEM((layers, slots, fw), b16),
            pltpu.VMEM((layers, slots, fw), b16),
            pltpu.VMEM((layers, slots, LANES), b16),
            pltpu.VMEM((layers, slots, LANES), b16),
            pltpu.VMEM((layers, slots, LANES), f32),
            pltpu.VMEM((layers, slots, LANES), f32),
            pltpu.VMEM((slots, fw), f32),
            pltpu.VMEM((slots, fw), f32),
            pltpu.VMEM((slots, LANES), f32),
            pltpu.VMEM((layers, weight_rows, fw), b16),
            pltpu.VMEM((layers, weight_rows, fw), b16),
            pltpu.VMEM((8, wide), f32),
            pltpu.VMEM((groups, 8, wide), f32),
            dma((6,)),
            dma,
            dma,
            dma,
            dma,
            dma,
            dma((layers,)),
            dma((layers,)),
            dma((layers,)),
            dma((2, stages)),
            dma((2, stages)),
            dma,
            dma,
            dma,
            dma,
            dma,
            dma,
        ],
        compiler_params=pltpu.CompilerParams(
            collective_id=0, has_side_effects=True, vmem_limit_bytes=62 * 1024 * 1024
        ),
    )(
        owner_indices.reshape(1, count),
        local_adapter_index.reshape(1, count),
        gains,
        adapter_down_weights.reshape(weight_rows, local),
        tokens,
        cotangent,
        adapter_up_weights.reshape(weight_rows, local),
    )
    grad_down, grad_up, slope = pl.pallas_call(
        finish,
        out_shape=tuple(jax.ShapeDtypeStruct(r.shape, r.dtype) for r in raw),
        in_specs=[anywhere] * 3,
        out_specs=(anywhere,) * 3,
        scratch_shapes=[pltpu.VMEM(r.shape, r.dtype) for r in raw] + [dma((9,)), dma((9,))],
        compiler_params=pltpu.CompilerParams(vmem_limit_bytes=62 * 1024 * 1024),
    )(*raw)
    shape = (1, adapters, rank, local)
    return (grad_down.reshape(shape), grad_up.reshape(shape), slope)


def solution(mesh):
    return jax.shard_map(
        on_device,
        mesh=mesh,
        in_specs=(
            P("dp", "tensor"),
            P("dp", None),
            P("dp"),
            P("section", "tensor"),
            P("section", "dp", None, "tensor"),
            P("section", "dp", None, "tensor"),
            P("dp", "tensor"),
        ),
        out_specs=(
            P("section", "dp", None, "tensor"),
            P("section", "dp", None, "tensor"),
            P("section", "dp"),
        ),
        check_vma=False,
    )
```

```python
import functools
import math

import jax
import jax.numpy as jnp
from jax import lax
from jax.experimental import pallas as pl
from jax.experimental.pallas import tpu as pltpu
from jax.sharding import PartitionSpec as P

MTOK = 64
LANES = 128
TILE = 16
JOINT = True
EPS = 1e-05
SCALE = 0.5
MESH = pl.DeviceIdType.MESH
NN = ((1,), (0,))
NT = ((1,), (1,))
TN = ((0,), (0,))


def round_up(value, unit):
    return -(-value // unit) * unit


def matmul(a, b, contract):
    return lax.dot_general(a, b, (contract, ((), ())), preferred_element_type=jnp.float32)


def drain(ref, sem):
    pltpu.make_async_copy(ref, ref, sem).wait()


def peers(axis):
    count, me = lax.axis_size(axis), lax.axis_index(axis)
    offsets = sorted(range(1, count), key=lambda o: (-min(o, count - o), o))
    return [lax.rem(me + o, count) for o in offsets]


def payload_rows(layers, half, rank, unit):
    at, ends = {}, []
    at["squares"], rows = 0, TILE
    for name, count in (("q", layers - 1), ("r", layers)):
        at[name], rows = rows, rows + count * half
    for k in range(layers - 1):
        for other in range(k, layers - 1):
            at["u", k, other], rows = rows, rows + rank
    rows = round_up(rows, unit)
    ends.append(rows)
    for part in range(2):
        at["p", part], rows = rows, rows + layers // 2 * half
        for k in range(layers - 1):
            for pair in range((k + 1) // 2, layers // 2):
                at["m", part, k, pair], rows = rows, rows + rank
        rows = round_up(rows, unit)
        ends.append(rows)
    return at, ends


def kernel(
    cap,
    own,
    choose,
    gains,
    down,
    tokens,
    cotangent,
    up,
    grad_down,
    grad_up,
    slope_out,
    own_v,
    choose_v,
    gains_v,
    up_v,
    down_v,
    tokv,
    cotv,
    sendbuf,
    recvbuf,
    gains_wide,
    w_gain,
    down_scaled,
    w_down,
    w_up,
    part,
    fin,
    got,
    got_y,
    acc_p,
    acc_q,
    acc_w,
    seen,
    big_m,
    big_u,
    xs,
    gs,
    zs,
    rd,
    prods,
    cur,
    first_x,
    first_cot,
    mask,
    back_d,
    back_u,
    slope_row,
    slopes,
    loc_sem,
    tok_s,
    tok_r,
    wd_s,
    wu_s,
    wg_s,
    wd_r,
    wu_r,
    wg_r,
    ar_s,
    ar_r,
    gd_s,
    gu_s,
    gd_r,
    gu_r,
    sl_s,
    sl_r,
):
    dp = lax.axis_index("dp")
    section = lax.axis_index("section")
    tensor = lax.axis_index("tensor")
    groups = lax.axis_size("dp")
    layers = lax.axis_size("section")
    ranks = lax.axis_size("tensor")
    bits = ranks.bit_length() - 1
    count = tokens.shape[0]
    fw = tokv.shape[1]
    width = tokens.shape[1] * ranks
    spad = sendbuf.shape[1]
    slots = xs.shape[1]
    half = slots // 2
    rank = LANES // 2
    each = slots // groups
    bf16, f32 = jnp.bfloat16, jnp.float32
    at, ends = payload_rows(layers, half, rank, TILE * layers * ranks)

    barrier = pltpu.get_barrier_semaphore()
    greeted = 0
    greet = [{axis: peer} for axis in ("tensor", "section", "dp") for peer in peers(axis)]
    if bits > 1:
        greet += [{"tensor": tensor ^ 2, "section": peer} for peer in peers("section")]
    for device in greet:
        pl.semaphore_signal(barrier, inc=1, device_id=device, device_id_type=MESH)
        greeted += 1

    def columns(index):
        return pl.ds(pl.multiple_of(index * fw, LANES), fw)

    quarter = rank // 2
    blocks = [
        (pl.ds((2 * a + h) * quarter, quarter), pl.ds((2 * h + a) * quarter, quarter))
        for a in range(2)
        for h in range(2)
    ]
    loads = [
        pltpu.make_async_copy(source, target, loc_sem.at[i])
        for i, (source, target) in enumerate(
            [
                (own, own_v),
                (choose, choose_v),
                (tokens.at[:, columns(section)], tokv),
                (cotangent.at[:, columns(section)], cotv),
                (gains, gains_v),
            ]
            + [(up.at[there], up_v.at[here]) for there, here in blocks]
            + [(down.at[there], down_v.at[here]) for there, here in blocks]
        )
    ]
    for load in loads:
        load.start()

    pl.semaphore_wait(barrier, greeted)

    def spread(source, target, send, recv, some=None):
        def rows_of(ref):
            return ref if some is None else ref.at[some]

        for peer in peers("section"):
            pltpu.make_async_remote_copy(
                rows_of(source).at[:, columns(peer)],
                rows_of(target.at[section]),
                send,
                recv.at[section],
                {"section": peer},
                MESH,
            ).start()
        pltpu.make_async_copy(
            rows_of(source).at[:, columns(section)], rows_of(target.at[section]), recv.at[section]
        ).start()

    for load in loads[5:9]:
        load.wait()
    spread(up_v, w_up, wu_s, wu_r)
    for load in loads[4:5] + loads[9:]:
        load.wait()
    down_scaled[...] = (down_v[...].astype(f32) * gains_v[...].astype(f32)).astype(bf16)
    for part_of in range(2):
        spread(
            down_scaled,
            w_down,
            wd_s,
            wd_r.at[part_of],
            pl.ds(part_of * rank, rank),
        )
    gains_wide[...] = jnp.broadcast_to(gains_v[...], gains_wide.shape)
    spread(gains_wide, w_gain, wg_s, wg_r)

    early = lax.broadcasted_iota(jnp.int32, (count, count), 0)
    late = lax.broadcasted_iota(jnp.int32, (count, count), 1)
    diagonal = early == late
    shift = MTOK.bit_length() - 1
    loads[0].wait()
    loads[1].wait()
    own_row = own_v[...].astype(f32)
    own_col = jnp.sum(jnp.where(diagonal, own_row, 0.0), 1, keepdims=True)
    before = (own_col == own_row) & (early < late) & ((early >> shift) == (late >> shift))
    rank_in = jnp.sum(jnp.where(before, 1.0, 0.0), 0, keepdims=True)
    micro_of = (lax.broadcasted_iota(jnp.int32, (1, count), 1) >> shift).astype(f32)
    place = micro_of * cap + rank_in
    spots = lax.broadcasted_iota(jnp.int32, (spad, count), 0).astype(f32)
    fits = place == spots
    member = jnp.concatenate(
        [jnp.where(fits & (own_row == d), 1.0, 0.0) for d in range(groups)], 0
    )
    flag = jnp.sum(member * choose_v[...].astype(f32), 1, keepdims=True)
    member = member.astype(bf16)
    loads[2].wait()
    loads[3].wait()
    sendbuf[:, :, 0:fw] = matmul(member, tokv[...], NN).astype(bf16).reshape(groups, spad, fw)
    sendbuf[:, :, fw : 2 * fw] = (
        matmul(member, cotv[...], NN).astype(bf16).reshape(groups, spad, fw)
    )
    sendbuf[:, :, 2 * fw :] = (
        jnp.broadcast_to(flag, (groups * spad, LANES)).astype(bf16).reshape(groups, spad, LANES)
    )

    for peer in peers("dp"):
        pltpu.make_async_remote_copy(
            sendbuf.at[peer], recvbuf.at[dp], tok_s, tok_r, {"dp": peer}, MESH
        ).start()
    recvbuf[dp] = sendbuf[dp]

    cell = lax.broadcasted_iota(jnp.int32, (1, groups * spad), 1)
    source = sum((cell >= d * spad).astype(jnp.int32) for d in range(1, groups))
    within = cell - source * spad
    wanted = jnp.where(within < each, source * each + within, -1)
    slot_ids = lax.broadcasted_iota(jnp.int32, (slots, groups * spad), 0)
    compact = jnp.where(slot_ids == wanted, 1.0, 0.0).astype(bf16)
    drain(recvbuf.at[pl.ds(0, groups - 1)], tok_r)
    arrived = matmul(compact, recvbuf[...].reshape(groups * spad, 2 * fw + LANES), NN)
    x0 = arrived[:, 0:fw]
    first_x[...] = x0
    first_cot[...] = arrived[:, fw : 2 * fw]
    lane = lax.broadcasted_iota(jnp.int32, (slots, LANES), 1)
    second = arrived[:, 2 * fw :] > 0.5
    mask[...] = jnp.where(second == ((lane & quarter) > 0), 1.0, 0.0)

    even = (lax.broadcasted_iota(jnp.int32, (half, LANES), 1) & quarter) == 0
    even_rank = (lax.broadcasted_iota(jnp.int32, (rank, LANES), 1) & quarter) == 0
    left = lane < rank
    left_rank = lax.broadcasted_iota(jnp.int32, (rank, LANES), 1) < rank
    tall = lax.broadcasted_iota(jnp.int32, (TILE, LANES), 1)

    def packed(total):
        kept = total * mask[...]
        first = kept[0:half] + pltpu.roll(kept[0:half], LANES - quarter, 1)
        last = kept[half:] + pltpu.roll(kept[half:], quarter, 1)
        return jnp.where(even, first, last).astype(bf16)

    def unpacked(total):
        total = total.astype(f32)
        first = jnp.where(even, total, pltpu.roll(total, quarter, 1))
        last = jnp.where(even, pltpu.roll(total, LANES - quarter, 1), total)
        return jnp.concatenate([first, last], 0) * mask[...]

    def thinned(block):
        first, second, third, fourth = (
            block[i * quarter : (i + 1) * quarter] for i in range(4)
        )
        return jnp.where(
            even_rank,
            jnp.concatenate([first, third], 0),
            jnp.concatenate([second, fourth], 0),
        ).astype(bf16)

    def widened(block):
        block = block.astype(f32)
        evens, odds = jnp.where(even_rank, block, 0.0), jnp.where(even_rank, 0.0, block)
        return jnp.concatenate(
            [evens[0:quarter], odds[0:quarter], evens[quarter:], odds[quarter:]], 0
        ).astype(bf16)

    def layer_of(first, last, which, keep_left):
        if which == 0:
            return jnp.where(keep_left, first, pltpu.roll(last, rank, 1))
        return jnp.where(keep_left, pltpu.roll(first, rank, 1), last)

    squares = jnp.sum(x0 * x0, 1, keepdims=True)
    folded = jnp.zeros((TILE, LANES), f32)
    for q in range(slots // TILE):
        folded = jnp.where(tall == q, squares[q * TILE : (q + 1) * TILE], folded)
    part[0:TILE] = folded.astype(bf16)

    for layer in range(layers):
        drain(w_up.at[layer], wu_r.at[layer])
    x_low = first_x[...].astype(bf16)
    cot_low = first_cot[...].astype(bf16)
    for layer in range(layers):
        weight = w_up[layer]
        if layer < layers - 1:
            row = at["q"] + layer * half
            part[row : row + half] = packed(matmul(x_low, weight, NT))
        row = at["r"] + layer * half
        part[row : row + half] = packed(matmul(cot_low, weight, NT))
    for k in range(layers - 1):
        stacked = w_up[k : layers - 1].reshape((layers - 1 - k) * LANES, fw)
        product = matmul(w_up[k], stacked, NT)
        for i, other in enumerate(range(k, layers - 1)):
            row = at["u", k, other]
            part[row : row + rank] = thinned(product[:, i * LANES : (i + 1) * LANES])

    def down_products(h):
        for layer in range(layers):
            drain(w_down.at[layer, pl.ds(h * rank, rank)], wd_r.at[h, layer])
        weights = w_down[:, h * rank : (h + 1) * rank].reshape(layers * rank, fw)
        product = matmul(x_low, weights, NT)
        for pair in range(layers // 2):
            row = at["p", h] + pair * half
            part[row : row + half] = packed(product[:, pair * LANES : (pair + 1) * LANES])
        for k in range(layers - 1):
            skip = (k + 1) // 2
            product = matmul(w_up[k], weights[skip * LANES :], NT)
            for pair in range(skip, layers // 2):
                row = at["m", h, k, pair]
                i = pair - skip
                part[row : row + rank] = thinned(product[:, i * LANES : (i + 1) * LANES])

    def rows(first, size):
        return pl.ds(pl.multiple_of(first, TILE), size)

    def all_reduce(chunk, joint):
        first = ends[chunk - 1] if chunk else 0
        size = ends[chunk] - first
        halvings = bits - 1 if joint and bits > 1 else bits
        strides = [] if halvings == bits else [1 << halvings]
        whole, piece = size, (size >> halvings) // (layers << len(strides))
        base, stage, starts = first, 0, []
        sends, arrivals = ar_s.at[chunk], ar_r.at[chunk]
        others = [({"section": peer}, peer, 0) for peer in peers("section")]
        high = 0
        for stride in strides:
            high = (tensor // stride) & 1
            away = tensor ^ stride
            others = (
                [({"section": peer, "tensor": away}, peer, 1) for peer in peers("section")]
                + others
                + [({"tensor": away}, section, 1)]
            )

        def index_of(peer, crossed):
            return peer + layers * (high + crossed - 2 * high * crossed)

        def send(source, target, device):
            pltpu.make_async_remote_copy(
                source, target, sends.at[stage], arrivals.at[stage], device, MESH
            ).start()

        for bit in range(halvings):
            size //= 2
            mine = (tensor >> bit) & 1
            keep, give = base + mine * size, base + (1 - mine) * size
            peer = tensor ^ (1 << bit)
            spot = first + whole - 2 * size
            send(part.at[rows(give, size)], got.at[pl.ds(spot, size)], {"tensor": peer})
            yield
            drain(got.at[pl.ds(spot, size)], arrivals.at[stage])
            part[rows(keep, size)] = (
                part[rows(keep, size)].astype(f32) + got[spot : spot + size].astype(f32)
            ).astype(bf16)
            starts.append((keep, size, peer))
            base, stage = keep, stage + 1
        landed = got_y.at[chunk]
        for o, (device, peer, crossed) in enumerate(others):
            send(
                part.at[rows(base + index_of(peer, crossed) * piece, piece)],
                landed.at[pl.ds(o * piece, piece)],
                device,
            )
        yield
        filled = len(others) * piece
        drain(landed.at[pl.ds(0, filled)], arrivals.at[stage])
        stage += 1
        mine = base + index_of(section, 0) * piece
        total = part[rows(mine, piece)].astype(f32)
        for o in range(len(others)):
            total += got_y[chunk, o * piece : (o + 1) * piece].astype(f32)
        fin[rows(mine, piece)] = total.astype(bf16)
        for device, _, _ in others:
            send(fin.at[rows(mine, piece)], fin.at[rows(mine, piece)], device)
        yield
        drain(fin.at[pl.ds(first, filled)], arrivals.at[stage])
        stage += 1
        for keep, size, peer in reversed(starts):
            send(fin.at[rows(keep, size)], fin.at[rows(keep, size)], {"tensor": peer})
            yield
            drain(fin.at[pl.ds(first, size)], arrivals.at[stage])
            stage += 1
        sizes = [size for _, size, _ in starts]
        for i, size in enumerate([*sizes, filled, filled, *reversed(sizes)]):
            sent.append((first, size, sends.at[i]))

    sent = []
    chunks = [all_reduce(0, False), all_reduce(1, False), all_reduce(2, JOINT)]

    def advance(order):
        for chunk in order:
            next(chunks[chunk], None)

    advance([0, 0])
    down_products(0)
    advance([1])
    advance([0, 1] if bits > 1 else [1])
    down_products(1)
    advance([2])
    advance([1, 2, 0, 1, 2, 0, 1, 2, 0, 1, 2, 0, 1, 2, 0, 1, 2])

    def lanes(first, last=None):
        return slice(first * LANES, (first + 1 if last is None else last) * LANES)

    for name, target, number in (("q", acc_q, layers - 1), ("r", acc_w, layers)):
        for layer in range(number):
            row = at[name] + layer * half
            target[:, lanes(layer)] = unpacked(fin[row : row + half])
    for pair in range(layers // 2):
        row, last_row = (at["p", h] + pair * half for h in range(2))
        first = unpacked(fin[row : row + half])
        last = unpacked(fin[last_row : last_row + half])
        for which in range(2):
            acc_p[:, lanes(2 * pair + which)] = layer_of(first, last, which, left)
    for k in range(layers - 1):
        for other in range(k, layers - 1):
            row = at["u", k, other]
            big_u[k, :, lanes(other)] = widened(fin[row : row + rank])
        for pair in range((k + 1) // 2, layers // 2):
            first, last = (
                fin[row : row + rank].astype(f32)
                for row in (at["m", h, k, pair] for h in range(2))
            )
            for which in range(2):
                if 2 * pair + which > k:
                    block = layer_of(first, last, which, left_rank)
                    big_m[k, :, lanes(2 * pair + which)] = widened(block)
    folded = fin[0:TILE].astype(f32)
    squares = jnp.concatenate(
        [
            jnp.sum(jnp.where(tall == q, folded, 0.0), 1, keepdims=True)
            for q in range(slots // TILE)
        ],
        0,
    )

    scales = []
    for k in range(layers):
        scale_rows = lax.rsqrt(squares / width + EPS)
        scales.append(scale_rows)
        latent = (acc_p[:, lanes(k)] * scale_rows).astype(bf16)
        zs[k] = latent
        x = first_x[...] if k == 0 else cur[...]
        xs[k] = x.astype(bf16)
        if k < layers - 1:
            cur[...] = x + SCALE * matmul(latent, w_up[k], NN)
            acc_p[:, lanes(k + 1, layers)] += SCALE * matmul(
                latent, big_m[k, :, lanes(k + 1, layers)], NN
            )
            inner = acc_q[:, lanes(k)]
            step = SCALE * matmul(latent, big_u[k, :, lanes(k, layers - 1)], NN)
            squares = jnp.maximum(
                squares
                + jnp.sum(
                    latent.astype(f32) * (inner + 0.5 * step[:, 0:LANES]), 1, keepdims=True
                ),
                0.0,
            )
            acc_q[:, lanes(k, layers - 1)] += step
            if k > 0:
                others = big_u[0:k, :, lanes(k)].reshape(k * LANES, LANES)
                acc_q[:, lanes(0, k)] += SCALE * matmul(latent, others, NT)
            seen[k + 1, :, lanes(0, k + 1)] = acc_q[:, lanes(0, k + 1)].astype(bf16)

    for m in reversed(range(layers)):
        rank_low = (SCALE * acc_w[:, lanes(m)]).astype(bf16)
        product = rank_low.astype(f32) * zs[m].astype(f32)
        prods[m] = product
        scale_rows = scales[m]
        scaled = (rank_low.astype(f32) * scale_rows).astype(bf16)
        rd[m] = scaled
        g = first_cot[...] if m == layers - 1 else cur[...]
        gs[m] = g.astype(bf16)
        if m > 0:
            weight = scale_rows * scale_rows * jnp.sum(product, 1, keepdims=True) / width
            cur[...] = (
                g + matmul(scaled, w_down[m], NN) - weight * xs[m].astype(f32)
            )
            others = big_m[0:m, :, lanes(m)].reshape(m * LANES, LANES)
            acc_w[:, lanes(0, m)] += matmul(scaled, others, NT) - weight * seen[
                m, :, lanes(0, m)
            ].astype(f32)

    for layer in range(layers):
        drain(w_gain.at[layer], wg_r.at[layer])

    def down_grad(layer):
        gain = w_gain[layer, 0:1].astype(f32)
        back_d[layer] = (matmul(rd[layer], xs[layer], TN) * gain).astype(bf16)
        return back_d.at[layer], grad_down.at[:, columns(section)], gd_s, gd_r

    def up_grad(layer):
        back_u[layer] = (SCALE * matmul(zs[layer], gs[layer], TN)).astype(bf16)
        return back_u.at[layer], grad_up.at[:, columns(section)], gu_s, gu_r

    for make in (down_grad, up_grad):
        for layer in peers("section"):
            source, target, send, recv = make(layer)
            pltpu.make_async_remote_copy(
                source, target, send, recv, {"section": layer}, MESH
            ).start()
    for make in (down_grad, up_grad):
        source, target, _, recv = make(section)
        pltpu.make_async_copy(source, target, recv).start()

    slope_row[:, 0:slots] = lax.dot_general(
        jnp.full((8, LANES), 1.0 / math.sqrt(width), f32),
        prods[section],
        (NT, ((), ())),
        preferred_element_type=f32,
        precision=lax.Precision.HIGHEST,
    )
    for peer in peers("dp"):
        pltpu.make_async_remote_copy(
            slope_row, slopes.at[dp], sl_s, sl_r, {"dp": peer}, MESH
        ).start()
    slopes[dp] = slope_row[...]

    drain(recvbuf.at[pl.ds(0, groups - 1)], tok_s)
    drain(w_down.at[pl.ds(0, layers - 1)], wd_s)
    drain(w_up.at[pl.ds(0, layers - 1)], wu_s)
    drain(w_gain.at[pl.ds(0, layers - 1)], wg_s)
    for first, size, sem in sent:
        drain(fin.at[pl.ds(first, size)], sem)
    drain(back_d.at[pl.ds(0, layers - 1)], gd_s)
    drain(back_u.at[pl.ds(0, layers - 1)], gu_s)
    drain(slopes.at[pl.ds(0, groups - 1)], sl_s)

    drain(slopes.at[pl.ds(0, groups - 1)], sl_r)
    wide = slopes.shape[2]
    found = jnp.zeros((count, wide), f32)
    for d in range(groups):
        found = jnp.where(own_col == d, slopes[d, 0:1], found)
    first_slot = (dp * each).astype(f32)
    place_col = jnp.sum(jnp.where(diagonal, place, 0.0), 1, keepdims=True) + first_slot
    here = lax.broadcasted_iota(jnp.int32, (count, wide), 1).astype(f32) == place_col
    slope_col = jnp.sum(jnp.where(here, found, 0.0), 1, keepdims=True)
    slope_out[...] = jnp.sum(jnp.where(diagonal, slope_col, 0.0), 0, keepdims=True)

    drain(grad_up, gu_r)
    drain(grad_down, gd_r)


def finish(raw_down, raw_up, raw_slope, grad_down, grad_up, slope, v_down, v_up, v_slope, loads, stores):
    parts = (loads.shape[0] - 1) // 2
    rows = grad_up.shape[0] // parts
    pieces = [(raw_slope, v_slope, slope)]
    for i, block in enumerate((0, 2, 1, 3)):
        some, home = pl.ds(i * rows, rows), pl.ds(block * rows, rows)
        pieces.append((raw_up.at[some], v_up.at[some], grad_up.at[home]))
        pieces.append((raw_down.at[some], v_down.at[some], grad_down.at[home]))
    reads = [
        pltpu.make_async_copy(source, through, loads.at[i])
        for i, (source, through, _) in enumerate(pieces)
    ]
    writes = [
        pltpu.make_async_copy(through, target, stores.at[i])
        for i, (_, through, target) in enumerate(pieces)
    ]
    for read in reads:
        read.start()
    for read, write in zip(reads, writes):
        read.wait()
        write.start()
    for write in writes:
        write.wait()


def on_device(
    tokens,
    owner_indices,
    local_adapter_index,
    gains,
    adapter_down_weights,
    adapter_up_weights,
    cotangent,
):
    groups, layers, ranks = (lax.axis_size(a) for a in ("dp", "section", "tensor"))
    count, local = tokens.shape
    micro = count // MTOK
    cap = 5 * MTOK // (4 * groups)
    each = micro * cap
    spad = round_up(each, TILE)
    slots = groups * each
    fw = local // layers
    adapters, rank = adapter_down_weights.shape[1:3]
    weight_rows = adapters * rank
    half = slots // 2
    wide = round_up(slots, LANES)
    _, ends = payload_rows(layers, half, rank, TILE * layers * ranks)
    rows = ends[-1]
    most = max(b - a for a, b in zip([0] + ends, ends))
    stages = 2 * (ranks.bit_length() - 1) + 2
    vmem = pl.BlockSpec(memory_space=pltpu.VMEM)
    anywhere = pl.BlockSpec(memory_space=pltpu.HBM)
    b16, f32 = jnp.bfloat16, jnp.float32
    dma = pltpu.SemaphoreType.DMA
    raw = pl.pallas_call(
        functools.partial(kernel, cap),
        out_shape=(
            jax.ShapeDtypeStruct((weight_rows, local), b16),
            jax.ShapeDtypeStruct((weight_rows, local), b16),
            jax.ShapeDtypeStruct((1, count), f32),
        ),
        in_specs=[anywhere] * 7,
        out_specs=(anywhere, anywhere, vmem),
        scratch_shapes=[
            pltpu.VMEM((1, count), jnp.int32),
            pltpu.VMEM((1, count), jnp.int32),
            pltpu.VMEM((1, local), b16),
            pltpu.VMEM((weight_rows, local), b16),
            pltpu.VMEM((weight_rows, local), b16),
            pltpu.VMEM((count, fw), b16),
            pltpu.VMEM((count, fw), b16),
            pltpu.VMEM((groups, spad, 2 * fw + LANES), b16),
            pltpu.VMEM((groups, spad, 2 * fw + LANES), b16),
            pltpu.VMEM((TILE, local), b16),
            pltpu.VMEM((layers, TILE, fw), b16),
            pltpu.VMEM((weight_rows, local), b16),
            pltpu.VMEM((layers, weight_rows, fw), b16),
            pltpu.VMEM((layers, weight_rows, fw), b16),
            pltpu.VMEM((rows, LANES), b16),
            pltpu.VMEM((rows, LANES), b16),
            pltpu.VMEM((rows, LANES), b16),
            pltpu.VMEM((3, most, LANES), b16),
            pltpu.VMEM((slots, layers * LANES), f32),
            pltpu.VMEM((slots, layers * LANES), f32),
            pltpu.VMEM((slots, layers * LANES), f32),
            pltpu.VMEM((layers, slots, layers * LANES), b16),
            pltpu.VMEM((layers, LANES, layers * LANES), b16),
            pltpu.VMEM((layers, LANES, layers * LANES), b16),
            pltpu.VMEM((layers, slots, fw), b16),
            pltpu.VMEM((layers, slots, fw), b16),
            pltpu.VMEM((layers, slots, LANES), b16),
            pltpu.VMEM((layers, slots, LANES), b16),
            pltpu.VMEM((layers, slots, LANES), f32),
            pltpu.VMEM((slots, fw), f32),
            pltpu.VMEM((slots, fw), f32),
            pltpu.VMEM((slots, fw), f32),
            pltpu.VMEM((slots, LANES), f32),
            pltpu.VMEM((layers, weight_rows, fw), b16),
            pltpu.VMEM((layers, weight_rows, fw), b16),
            pltpu.VMEM((8, wide), f32),
            pltpu.VMEM((groups, 8, wide), f32),
            dma((13,)),
            dma,
            dma,
            dma,
            dma,
            dma,
            dma((2, layers)),
            dma((layers,)),
            dma((layers,)),
            dma((3, stages)),
            dma((3, stages)),
            dma,
            dma,
            dma,
            dma,
            dma,
            dma,
        ],
        compiler_params=pltpu.CompilerParams(
            collective_id=0, has_side_effects=True, vmem_limit_bytes=62 * 1024 * 1024
        ),
    )(
        owner_indices.reshape(1, count),
        local_adapter_index.reshape(1, count),
        gains,
        adapter_down_weights.reshape(weight_rows, local),
        tokens,
        cotangent,
        adapter_up_weights.reshape(weight_rows, local),
    )
    grad_down, grad_up, slope = pl.pallas_call(
        finish,
        out_shape=tuple(jax.ShapeDtypeStruct(r.shape, r.dtype) for r in raw),
        in_specs=[anywhere] * 3,
        out_specs=(anywhere,) * 3,
        scratch_shapes=[pltpu.VMEM(r.shape, r.dtype) for r in raw] + [dma((9,)), dma((9,))],
        compiler_params=pltpu.CompilerParams(vmem_limit_bytes=62 * 1024 * 1024),
    )(*raw)
    shape = (1, adapters, rank, local)
    return (grad_down.reshape(shape), grad_up.reshape(shape), slope)


def solution(mesh):
    return jax.shard_map(
        on_device,
        mesh=mesh,
        in_specs=(
            P("dp", "tensor"),
            P("dp", None),
            P("dp"),
            P("section", "tensor"),
            P("section", "dp", None, "tensor"),
            P("section", "dp", None, "tensor"),
            P("dp", "tensor"),
        ),
        out_specs=(
            P("section", "dp", None, "tensor"),
            P("section", "dp", None, "tensor"),
            P("section", "dp"),
        ),
        check_vma=False,
    )
```

```python
import functools
import math

import jax
import jax.numpy as jnp
from jax import lax
from jax.experimental import pallas as pl
from jax.experimental.pallas import tpu as pltpu
from jax.sharding import PartitionSpec as P

MTOK = 64
LANES = 128
TILE = 16
JOINT = True
EPS = 1e-05
SCALE = 0.5
MESH = pl.DeviceIdType.MESH
NN = ((1,), (0,))
NT = ((1,), (1,))
TN = ((0,), (0,))


def round_up(value, unit):
    return -(-value // unit) * unit


def matmul(a, b, contract):
    return lax.dot_general(a, b, (contract, ((), ())), preferred_element_type=jnp.float32)


def drain(ref, sem):
    pltpu.make_async_copy(ref, ref, sem).wait()


def peers(axis):
    count, me = lax.axis_size(axis), lax.axis_index(axis)
    offsets = sorted(range(1, count), key=lambda o: (-min(o, count - o), o))
    return [lax.rem(me + o, count) for o in offsets]


def payload_rows(layers, half, rank, unit):
    at, ends = {}, []
    at["squares"], rows = 0, TILE
    for name, count in (("q", layers - 1), ("r", layers)):
        at[name], rows = rows, rows + count * half
    for k in range(layers - 1):
        for other in range(k, layers - 1):
            at["u", k, other], rows = rows, rows + rank
    rows = round_up(rows, unit)
    ends.append(rows)
    for part in range(2):
        at["p", part], rows = rows, rows + layers // 2 * half
        for k in range(layers - 1):
            for pair in range((k + 1) // 2, layers // 2):
                at["m", part, k, pair], rows = rows, rows + rank
        rows = round_up(rows, unit)
        ends.append(rows)
    return at, ends


def kernel(
    cap,
    own,
    choose,
    gains,
    down,
    tokens,
    cotangent,
    up,
    grad_down,
    grad_up,
    slope_out,
    own_v,
    choose_v,
    gains_v,
    up_v,
    down_v,
    tokv,
    cotv,
    sendbuf,
    recvbuf,
    gains_wide,
    w_gain,
    down_scaled,
    w_down,
    w_up,
    part,
    fin,
    got,
    got_y,
    acc_p,
    acc_q,
    acc_w,
    seen,
    big_m,
    big_u,
    xs,
    gs,
    zs,
    rd,
    prods,
    cur,
    first_x,
    first_cot,
    mask,
    back_d,
    back_u,
    slope_row,
    slopes,
    group_sem,
    all_sem,
    loc_sem,
    tok_s,
    tok_r,
    wd_s,
    wu_s,
    wg_s,
    wd_r,
    wu_r,
    wg_r,
    ar_s,
    ar_r,
    gd_s,
    gu_s,
    gd_r,
    gu_r,
    sl_s,
    sl_r,
):
    dp = lax.axis_index("dp")
    section = lax.axis_index("section")
    tensor = lax.axis_index("tensor")
    groups = lax.axis_size("dp")
    layers = lax.axis_size("section")
    ranks = lax.axis_size("tensor")
    bits = ranks.bit_length() - 1
    count = tokens.shape[0]
    fw = tokv.shape[1]
    width = tokens.shape[1] * ranks
    spad = sendbuf.shape[1]
    slots = xs.shape[1]
    half = slots // 2
    rank = LANES // 2
    each = slots // groups
    bf16, f32 = jnp.bfloat16, jnp.float32
    at, ends = payload_rows(layers, half, rank, TILE * layers * ranks)

    barrier = pltpu.get_barrier_semaphore()
    core = tensor & 1
    sibling = {"tensor": tensor ^ 1}

    def greet(device):
        pl.semaphore_signal(barrier, inc=1, device_id=device, device_id_type=MESH)

    chips = ranks // 2
    for away in range(layers):
        for over in range(chips):
            chip = lax.rem((tensor >> 1) + over, chips)
            if away or over:
                greet({"section": lax.rem(section + away, layers), "tensor": 2 * chip + 1})
    pl.when(core == 0)(lambda: greet(sibling))
    for peer in peers("dp"):
        greet({"dp": peer, "tensor": tensor - core})

    def group_arrived():
        @pl.when(core == 1)
        def _():
            pl.semaphore_wait(barrier, layers * ranks - 1)
            pl.semaphore_signal(group_sem, inc=1, device_id=sibling, device_id_type=MESH)

        @pl.when(core == 0)
        def _():
            pl.semaphore_wait(group_sem, 1)

    def all_arrived():
        @pl.when(core == 0)
        def _():
            pl.semaphore_wait(barrier, 2 * (groups - 1))
            pl.semaphore_signal(all_sem, inc=1, device_id=sibling, device_id_type=MESH)

        @pl.when(core == 1)
        def _():
            pl.semaphore_wait(all_sem, 1)

    def columns(index):
        return pl.ds(pl.multiple_of(index * fw, LANES), fw)

    quarter = rank // 2
    blocks = [
        (pl.ds((2 * a + h) * quarter, quarter), pl.ds((2 * h + a) * quarter, quarter))
        for a in range(2)
        for h in range(2)
    ]
    loads = [
        pltpu.make_async_copy(source, target, loc_sem.at[i])
        for i, (source, target) in enumerate(
            [
                (own, own_v),
                (choose, choose_v),
                (tokens.at[:, columns(section)], tokv),
                (cotangent.at[:, columns(section)], cotv),
                (gains, gains_v),
            ]
            + [(up.at[there], up_v.at[here]) for there, here in blocks]
            + [(down.at[there], down_v.at[here]) for there, here in blocks]
        )
    ]
    for load in loads:
        load.start()

    early = lax.broadcasted_iota(jnp.int32, (count, count), 0)
    late = lax.broadcasted_iota(jnp.int32, (count, count), 1)
    diagonal = early == late
    shift = MTOK.bit_length() - 1
    loads[0].wait()
    loads[1].wait()
    own_row = own_v[...].astype(f32)
    own_col = jnp.sum(jnp.where(diagonal, own_row, 0.0), 1, keepdims=True)
    before = (own_col == own_row) & (early < late) & ((early >> shift) == (late >> shift))
    rank_in = jnp.sum(jnp.where(before, 1.0, 0.0), 0, keepdims=True)
    micro_of = (lax.broadcasted_iota(jnp.int32, (1, count), 1) >> shift).astype(f32)
    place = micro_of * cap + rank_in
    spots = lax.broadcasted_iota(jnp.int32, (spad, count), 0).astype(f32)
    fits = place == spots
    member = jnp.concatenate(
        [jnp.where(fits & (own_row == d), 1.0, 0.0) for d in range(groups)], 0
    )
    flag = jnp.sum(member * choose_v[...].astype(f32), 1, keepdims=True)
    member = member.astype(bf16)
    loads[2].wait()
    loads[3].wait()
    sendbuf[:, :, 0:fw] = matmul(member, tokv[...], NN).astype(bf16).reshape(groups, spad, fw)
    sendbuf[:, :, fw : 2 * fw] = (
        matmul(member, cotv[...], NN).astype(bf16).reshape(groups, spad, fw)
    )
    sendbuf[:, :, 2 * fw :] = (
        jnp.broadcast_to(flag, (groups * spad, LANES)).astype(bf16).reshape(groups, spad, LANES)
    )

    group_arrived()

    def spread(source, target, send, recv, some=None):
        def rows_of(ref):
            return ref if some is None else ref.at[some]

        for peer in peers("section"):
            pltpu.make_async_remote_copy(
                rows_of(source).at[:, columns(peer)],
                rows_of(target.at[section]),
                send,
                recv.at[section],
                {"section": peer},
                MESH,
            ).start()
        pltpu.make_async_copy(
            rows_of(source).at[:, columns(section)], rows_of(target.at[section]), recv.at[section]
        ).start()

    for load in loads[5:9]:
        load.wait()
    spread(up_v, w_up, wu_s, wu_r)
    for load in loads[4:5] + loads[9:]:
        load.wait()
    down_scaled[...] = (down_v[...].astype(f32) * gains_v[...].astype(f32)).astype(bf16)
    all_arrived()
    for peer in peers("dp"):
        pltpu.make_async_remote_copy(
            sendbuf.at[peer], recvbuf.at[dp], tok_s, tok_r, {"dp": peer}, MESH
        ).start()
    recvbuf[dp] = sendbuf[dp]

    for part_of in range(2):
        spread(
            down_scaled,
            w_down,
            wd_s,
            wd_r.at[part_of],
            pl.ds(part_of * rank, rank),
        )
    gains_wide[...] = jnp.broadcast_to(gains_v[...], gains_wide.shape)
    spread(gains_wide, w_gain, wg_s, wg_r)

    cell = lax.broadcasted_iota(jnp.int32, (1, groups * spad), 1)
    source = sum((cell >= d * spad).astype(jnp.int32) for d in range(1, groups))
    within = cell - source * spad
    wanted = jnp.where(within < each, source * each + within, -1)
    slot_ids = lax.broadcasted_iota(jnp.int32, (slots, groups * spad), 0)
    compact = jnp.where(slot_ids == wanted, 1.0, 0.0).astype(bf16)
    drain(recvbuf.at[pl.ds(0, groups - 1)], tok_r)
    arrived = matmul(compact, recvbuf[...].reshape(groups * spad, 2 * fw + LANES), NN)
    x0 = arrived[:, 0:fw]
    first_x[...] = x0
    first_cot[...] = arrived[:, fw : 2 * fw]
    lane = lax.broadcasted_iota(jnp.int32, (slots, LANES), 1)
    second = arrived[:, 2 * fw :] > 0.5
    mask[...] = jnp.where(second == ((lane & quarter) > 0), 1.0, 0.0)

    even = (lax.broadcasted_iota(jnp.int32, (half, LANES), 1) & quarter) == 0
    even_rank = (lax.broadcasted_iota(jnp.int32, (rank, LANES), 1) & quarter) == 0
    left = lane < rank
    left_rank = lax.broadcasted_iota(jnp.int32, (rank, LANES), 1) < rank
    tall = lax.broadcasted_iota(jnp.int32, (TILE, LANES), 1)

    def packed(total):
        kept = total * mask[...]
        first = kept[0:half] + pltpu.roll(kept[0:half], LANES - quarter, 1)
        last = kept[half:] + pltpu.roll(kept[half:], quarter, 1)
        return jnp.where(even, first, last).astype(bf16)

    def unpacked(total):
        total = total.astype(f32)
        first = jnp.where(even, total, pltpu.roll(total, quarter, 1))
        last = jnp.where(even, pltpu.roll(total, LANES - quarter, 1), total)
        return jnp.concatenate([first, last], 0) * mask[...]

    def thinned(block):
        first, second, third, fourth = (
            block[i * quarter : (i + 1) * quarter] for i in range(4)
        )
        return jnp.where(
            even_rank,
            jnp.concatenate([first, third], 0),
            jnp.concatenate([second, fourth], 0),
        ).astype(bf16)

    def widened(block):
        block = block.astype(f32)
        evens, odds = jnp.where(even_rank, block, 0.0), jnp.where(even_rank, 0.0, block)
        return jnp.concatenate(
            [evens[0:quarter], odds[0:quarter], evens[quarter:], odds[quarter:]], 0
        ).astype(bf16)

    def layer_of(first, last, which, keep_left):
        if which == 0:
            return jnp.where(keep_left, first, pltpu.roll(last, rank, 1))
        return jnp.where(keep_left, pltpu.roll(first, rank, 1), last)

    squares = jnp.sum(x0 * x0, 1, keepdims=True)
    folded = jnp.zeros((TILE, LANES), f32)
    for q in range(slots // TILE):
        folded = jnp.where(tall == q, squares[q * TILE : (q + 1) * TILE], folded)
    part[0:TILE] = folded.astype(bf16)

    for layer in range(layers):
        drain(w_up.at[layer], wu_r.at[layer])
    x_low = first_x[...].astype(bf16)
    cot_low = first_cot[...].astype(bf16)
    for layer in range(layers):
        weight = w_up[layer]
        if layer < layers - 1:
            row = at["q"] + layer * half
            part[row : row + half] = packed(matmul(x_low, weight, NT))
        row = at["r"] + layer * half
        part[row : row + half] = packed(matmul(cot_low, weight, NT))
    for k in range(layers - 1):
        stacked = w_up[k : layers - 1].reshape((layers - 1 - k) * LANES, fw)
        product = matmul(w_up[k], stacked, NT)
        for i, other in enumerate(range(k, layers - 1)):
            row = at["u", k, other]
            part[row : row + rank] = thinned(product[:, i * LANES : (i + 1) * LANES])

    def down_products(h):
        for layer in range(layers):
            drain(w_down.at[layer, pl.ds(h * rank, rank)], wd_r.at[h, layer])
        weights = w_down[:, h * rank : (h + 1) * rank].reshape(layers * rank, fw)
        product = matmul(x_low, weights, NT)
        for pair in range(layers // 2):
            row = at["p", h] + pair * half
            part[row : row + half] = packed(product[:, pair * LANES : (pair + 1) * LANES])
        for k in range(layers - 1):
            skip = (k + 1) // 2
            product = matmul(w_up[k], weights[skip * LANES :], NT)
            for pair in range(skip, layers // 2):
                row = at["m", h, k, pair]
                i = pair - skip
                part[row : row + rank] = thinned(product[:, i * LANES : (i + 1) * LANES])

    def rows(first, size):
        return pl.ds(pl.multiple_of(first, TILE), size)

    def all_reduce(chunk, joint):
        first = ends[chunk - 1] if chunk else 0
        size = ends[chunk] - first
        halvings = bits - 1 if joint and bits > 1 else bits
        strides = [] if halvings == bits else [1 << halvings]
        whole, piece = size, (size >> halvings) // (layers << len(strides))
        base, stage, starts = first, 0, []
        sends, arrivals = ar_s.at[chunk], ar_r.at[chunk]
        others = [({"section": peer}, peer, 0) for peer in peers("section")]
        high = 0
        for stride in strides:
            high = (tensor // stride) & 1
            away = tensor ^ stride
            others = (
                [({"section": peer, "tensor": away}, peer, 1) for peer in peers("section")]
                + others
                + [({"tensor": away}, section, 1)]
            )

        def index_of(peer, crossed):
            return peer + layers * (high + crossed - 2 * high * crossed)

        def send(source, target, device):
            pltpu.make_async_remote_copy(
                source, target, sends.at[stage], arrivals.at[stage], device, MESH
            ).start()

        for bit in range(halvings):
            size //= 2
            mine = (tensor >> bit) & 1
            keep, give = base + mine * size, base + (1 - mine) * size
            peer = tensor ^ (1 << bit)
            spot = first + whole - 2 * size
            send(part.at[rows(give, size)], got.at[pl.ds(spot, size)], {"tensor": peer})
            yield
            drain(got.at[pl.ds(spot, size)], arrivals.at[stage])
            part[rows(keep, size)] = (
                part[rows(keep, size)].astype(f32) + got[spot : spot + size].astype(f32)
            ).astype(bf16)
            starts.append((keep, size, peer))
            base, stage = keep, stage + 1
        landed = got_y.at[chunk]
        for o, (device, peer, crossed) in enumerate(others):
            send(
                part.at[rows(base + index_of(peer, crossed) * piece, piece)],
                landed.at[pl.ds(o * piece, piece)],
                device,
            )
        yield
        filled = len(others) * piece
        drain(landed.at[pl.ds(0, filled)], arrivals.at[stage])
        stage += 1
        mine = base + index_of(section, 0) * piece
        total = part[rows(mine, piece)].astype(f32)
        for o in range(len(others)):
            total += got_y[chunk, o * piece : (o + 1) * piece].astype(f32)
        fin[rows(mine, piece)] = total.astype(bf16)
        for device, _, _ in others:
            send(fin.at[rows(mine, piece)], fin.at[rows(mine, piece)], device)
        yield
        drain(fin.at[pl.ds(first, filled)], arrivals.at[stage])
        stage += 1
        for keep, size, peer in reversed(starts):
            send(fin.at[rows(keep, size)], fin.at[rows(keep, size)], {"tensor": peer})
            yield
            drain(fin.at[pl.ds(first, size)], arrivals.at[stage])
            stage += 1
        sizes = [size for _, size, _ in starts]
        for i, size in enumerate([*sizes, filled, filled, *reversed(sizes)]):
            sent.append((first, size, sends.at[i]))

    sent = []
    chunks = [all_reduce(0, False), all_reduce(1, False), all_reduce(2, JOINT)]

    def advance(order):
        for chunk in order:
            next(chunks[chunk], None)

    advance([0, 0])
    down_products(0)
    advance([1])
    advance([0, 1] if bits > 1 else [1])
    down_products(1)
    advance([2])
    advance([1, 2, 0, 1, 2, 0, 1, 2, 0, 1, 2, 0, 1, 2, 0, 1, 2])

    def lanes(first, last=None):
        return slice(first * LANES, (first + 1 if last is None else last) * LANES)

    for name, target, number in (("q", acc_q, layers - 1), ("r", acc_w, layers)):
        for layer in range(number):
            row = at[name] + layer * half
            target[:, lanes(layer)] = unpacked(fin[row : row + half])
    for pair in range(layers // 2):
        row, last_row = (at["p", h] + pair * half for h in range(2))
        first = unpacked(fin[row : row + half])
        last = unpacked(fin[last_row : last_row + half])
        for which in range(2):
            acc_p[:, lanes(2 * pair + which)] = layer_of(first, last, which, left)
    for k in range(layers - 1):
        for other in range(k, layers - 1):
            row = at["u", k, other]
            big_u[k, :, lanes(other)] = widened(fin[row : row + rank])
        for pair in range((k + 1) // 2, layers // 2):
            first, last = (
                fin[row : row + rank].astype(f32)
                for row in (at["m", h, k, pair] for h in range(2))
            )
            for which in range(2):
                if 2 * pair + which > k:
                    block = layer_of(first, last, which, left_rank)
                    big_m[k, :, lanes(2 * pair + which)] = widened(block)
    folded = fin[0:TILE].astype(f32)
    squares = jnp.concatenate(
        [
            jnp.sum(jnp.where(tall == q, folded, 0.0), 1, keepdims=True)
            for q in range(slots // TILE)
        ],
        0,
    )

    scales = []
    for k in range(layers):
        scale_rows = lax.rsqrt(squares / width + EPS)
        scales.append(scale_rows)
        latent = (acc_p[:, lanes(k)] * scale_rows).astype(bf16)
        zs[k] = latent
        x = first_x[...] if k == 0 else cur[...]
        xs[k] = x.astype(bf16)
        if k < layers - 1:
            cur[...] = x + SCALE * matmul(latent, w_up[k], NN)
            acc_p[:, lanes(k + 1, layers)] += SCALE * matmul(
                latent, big_m[k, :, lanes(k + 1, layers)], NN
            )
            inner = acc_q[:, lanes(k)]
            step = SCALE * matmul(latent, big_u[k, :, lanes(k, layers - 1)], NN)
            squares = jnp.maximum(
                squares
                + jnp.sum(
                    latent.astype(f32) * (inner + 0.5 * step[:, 0:LANES]), 1, keepdims=True
                ),
                0.0,
            )
            acc_q[:, lanes(k, layers - 1)] += step
            if k > 0:
                others = big_u[0:k, :, lanes(k)].reshape(k * LANES, LANES)
                acc_q[:, lanes(0, k)] += SCALE * matmul(latent, others, NT)
            seen[k + 1, :, lanes(0, k + 1)] = acc_q[:, lanes(0, k + 1)].astype(bf16)

    for m in reversed(range(layers)):
        rank_low = (SCALE * acc_w[:, lanes(m)]).astype(bf16)
        product = rank_low.astype(f32) * zs[m].astype(f32)
        prods[m] = product
        scale_rows = scales[m]
        scaled = (rank_low.astype(f32) * scale_rows).astype(bf16)
        rd[m] = scaled
        g = first_cot[...] if m == layers - 1 else cur[...]
        gs[m] = g.astype(bf16)
        if m > 0:
            weight = scale_rows * scale_rows * jnp.sum(product, 1, keepdims=True) / width
            cur[...] = (
                g + matmul(scaled, w_down[m], NN) - weight * xs[m].astype(f32)
            )
            others = big_m[0:m, :, lanes(m)].reshape(m * LANES, LANES)
            acc_w[:, lanes(0, m)] += matmul(scaled, others, NT) - weight * seen[
                m, :, lanes(0, m)
            ].astype(f32)

    for layer in range(layers):
        drain(w_gain.at[layer], wg_r.at[layer])

    def down_grad(layer):
        gain = w_gain[layer, 0:1].astype(f32)
        back_d[layer] = (matmul(rd[layer], xs[layer], TN) * gain).astype(bf16)
        return back_d.at[layer], grad_down.at[:, columns(section)], gd_s, gd_r

    def up_grad(layer):
        back_u[layer] = (SCALE * matmul(zs[layer], gs[layer], TN)).astype(bf16)
        return back_u.at[layer], grad_up.at[:, columns(section)], gu_s, gu_r

    for make in (down_grad, up_grad):
        for layer in peers("section"):
            source, target, send, recv = make(layer)
            pltpu.make_async_remote_copy(
                source, target, send, recv, {"section": layer}, MESH
            ).start()
    for make in (down_grad, up_grad):
        source, target, _, recv = make(section)
        pltpu.make_async_copy(source, target, recv).start()

    slope_row[:, 0:slots] = lax.dot_general(
        jnp.full((8, LANES), 1.0 / math.sqrt(width), f32),
        prods[section],
        (NT, ((), ())),
        preferred_element_type=f32,
        precision=lax.Precision.HIGHEST,
    )
    for peer in peers("dp"):
        pltpu.make_async_remote_copy(
            slope_row, slopes.at[dp], sl_s, sl_r, {"dp": peer}, MESH
        ).start()
    slopes[dp] = slope_row[...]

    drain(recvbuf.at[pl.ds(0, groups - 1)], tok_s)
    drain(w_down.at[pl.ds(0, layers - 1)], wd_s)
    drain(w_up.at[pl.ds(0, layers - 1)], wu_s)
    drain(w_gain.at[pl.ds(0, layers - 1)], wg_s)
    for first, size, sem in sent:
        drain(fin.at[pl.ds(first, size)], sem)
    drain(back_d.at[pl.ds(0, layers - 1)], gd_s)
    drain(back_u.at[pl.ds(0, layers - 1)], gu_s)
    drain(slopes.at[pl.ds(0, groups - 1)], sl_s)

    drain(slopes.at[pl.ds(0, groups - 1)], sl_r)
    wide = slopes.shape[2]
    found = jnp.zeros((count, wide), f32)
    for d in range(groups):
        found = jnp.where(own_col == d, slopes[d, 0:1], found)
    first_slot = (dp * each).astype(f32)
    place_col = jnp.sum(jnp.where(diagonal, place, 0.0), 1, keepdims=True) + first_slot
    here = lax.broadcasted_iota(jnp.int32, (count, wide), 1).astype(f32) == place_col
    slope_col = jnp.sum(jnp.where(here, found, 0.0), 1, keepdims=True)
    slope_out[...] = jnp.sum(jnp.where(diagonal, slope_col, 0.0), 0, keepdims=True)

    drain(grad_up, gu_r)
    drain(grad_down, gd_r)


def finish(raw_down, raw_up, raw_slope, grad_down, grad_up, slope, v_down, v_up, v_slope, loads, stores):
    parts = (loads.shape[0] - 1) // 2
    rows = grad_up.shape[0] // parts
    pieces = [(raw_slope, v_slope, slope)]
    for i, block in enumerate((0, 2, 1, 3)):
        some, home = pl.ds(i * rows, rows), pl.ds(block * rows, rows)
        pieces.append((raw_up.at[some], v_up.at[some], grad_up.at[home]))
        pieces.append((raw_down.at[some], v_down.at[some], grad_down.at[home]))
    reads = [
        pltpu.make_async_copy(source, through, loads.at[i])
        for i, (source, through, _) in enumerate(pieces)
    ]
    writes = [
        pltpu.make_async_copy(through, target, stores.at[i])
        for i, (_, through, target) in enumerate(pieces)
    ]
    for read in reads:
        read.start()
    for read, write in zip(reads, writes):
        read.wait()
        write.start()
    for write in writes:
        write.wait()


def on_device(
    tokens,
    owner_indices,
    local_adapter_index,
    gains,
    adapter_down_weights,
    adapter_up_weights,
    cotangent,
):
    groups, layers, ranks = (lax.axis_size(a) for a in ("dp", "section", "tensor"))
    count, local = tokens.shape
    micro = count // MTOK
    cap = 5 * MTOK // (4 * groups)
    each = micro * cap
    spad = round_up(each, TILE)
    slots = groups * each
    fw = local // layers
    adapters, rank = adapter_down_weights.shape[1:3]
    weight_rows = adapters * rank
    half = slots // 2
    wide = round_up(slots, LANES)
    _, ends = payload_rows(layers, half, rank, TILE * layers * ranks)
    rows = ends[-1]
    most = max(b - a for a, b in zip([0] + ends, ends))
    stages = 2 * (ranks.bit_length() - 1) + 2
    vmem = pl.BlockSpec(memory_space=pltpu.VMEM)
    anywhere = pl.BlockSpec(memory_space=pltpu.HBM)
    b16, f32 = jnp.bfloat16, jnp.float32
    dma = pltpu.SemaphoreType.DMA
    raw = pl.pallas_call(
        functools.partial(kernel, cap),
        out_shape=(
            jax.ShapeDtypeStruct((weight_rows, local), b16),
            jax.ShapeDtypeStruct((weight_rows, local), b16),
            jax.ShapeDtypeStruct((1, count), f32),
        ),
        in_specs=[anywhere] * 7,
        out_specs=(anywhere, anywhere, vmem),
        scratch_shapes=[
            pltpu.VMEM((1, count), jnp.int32),
            pltpu.VMEM((1, count), jnp.int32),
            pltpu.VMEM((1, local), b16),
            pltpu.VMEM((weight_rows, local), b16),
            pltpu.VMEM((weight_rows, local), b16),
            pltpu.VMEM((count, fw), b16),
            pltpu.VMEM((count, fw), b16),
            pltpu.VMEM((groups, spad, 2 * fw + LANES), b16),
            pltpu.VMEM((groups, spad, 2 * fw + LANES), b16),
            pltpu.VMEM((TILE, local), b16),
            pltpu.VMEM((layers, TILE, fw), b16),
            pltpu.VMEM((weight_rows, local), b16),
            pltpu.VMEM((layers, weight_rows, fw), b16),
            pltpu.VMEM((layers, weight_rows, fw), b16),
            pltpu.VMEM((rows, LANES), b16),
            pltpu.VMEM((rows, LANES), b16),
            pltpu.VMEM((rows, LANES), b16),
            pltpu.VMEM((3, most, LANES), b16),
            pltpu.VMEM((slots, layers * LANES), f32),
            pltpu.VMEM((slots, layers * LANES), f32),
            pltpu.VMEM((slots, layers * LANES), f32),
            pltpu.VMEM((layers, slots, layers * LANES), b16),
            pltpu.VMEM((layers, LANES, layers * LANES), b16),
            pltpu.VMEM((layers, LANES, layers * LANES), b16),
            pltpu.VMEM((layers, slots, fw), b16),
            pltpu.VMEM((layers, slots, fw), b16),
            pltpu.VMEM((layers, slots, LANES), b16),
            pltpu.VMEM((layers, slots, LANES), b16),
            pltpu.VMEM((layers, slots, LANES), f32),
            pltpu.VMEM((slots, fw), f32),
            pltpu.VMEM((slots, fw), f32),
            pltpu.VMEM((slots, fw), f32),
            pltpu.VMEM((slots, LANES), f32),
            pltpu.VMEM((layers, weight_rows, fw), b16),
            pltpu.VMEM((layers, weight_rows, fw), b16),
            pltpu.VMEM((8, wide), f32),
            pltpu.VMEM((groups, 8, wide), f32),
            pltpu.SemaphoreType.REGULAR,
            pltpu.SemaphoreType.REGULAR,
            dma((13,)),
            dma,
            dma,
            dma,
            dma,
            dma,
            dma((2, layers)),
            dma((layers,)),
            dma((layers,)),
            dma((3, stages)),
            dma((3, stages)),
            dma,
            dma,
            dma,
            dma,
            dma,
            dma,
        ],
        compiler_params=pltpu.CompilerParams(
            collective_id=0, has_side_effects=True, vmem_limit_bytes=62 * 1024 * 1024
        ),
    )(
        owner_indices.reshape(1, count),
        local_adapter_index.reshape(1, count),
        gains,
        adapter_down_weights.reshape(weight_rows, local),
        tokens,
        cotangent,
        adapter_up_weights.reshape(weight_rows, local),
    )
    grad_down, grad_up, slope = pl.pallas_call(
        finish,
        out_shape=tuple(jax.ShapeDtypeStruct(r.shape, r.dtype) for r in raw),
        in_specs=[anywhere] * 3,
        out_specs=(anywhere,) * 3,
        scratch_shapes=[pltpu.VMEM(r.shape, r.dtype) for r in raw] + [dma((9,)), dma((9,))],
        compiler_params=pltpu.CompilerParams(vmem_limit_bytes=62 * 1024 * 1024),
    )(*raw)
    shape = (1, adapters, rank, local)
    return (grad_down.reshape(shape), grad_up.reshape(shape), slope)


def solution(mesh):
    return jax.shard_map(
        on_device,
        mesh=mesh,
        in_specs=(
            P("dp", "tensor"),
            P("dp", None),
            P("dp"),
            P("section", "tensor"),
            P("section", "dp", None, "tensor"),
            P("section", "dp", None, "tensor"),
            P("dp", "tensor"),
        ),
        out_specs=(
            P("section", "dp", None, "tensor"),
            P("section", "dp", None, "tensor"),
            P("section", "dp"),
        ),
        check_vma=False,
    )
```

```python
import functools
import math

import jax
import jax.numpy as jnp
from jax import lax
from jax.experimental import pallas as pl
from jax.experimental.pallas import tpu as pltpu
from jax.sharding import PartitionSpec as P

MTOK = 64
LANES = 128
TILE = 16
JOINT = True
EPS = 1e-05
SCALE = 0.5
MESH = pl.DeviceIdType.MESH
NN = ((1,), (0,))
NT = ((1,), (1,))
TN = ((0,), (0,))


def round_up(value, unit):
    return -(-value // unit) * unit


def matmul(a, b, contract):
    return lax.dot_general(a, b, (contract, ((), ())), preferred_element_type=jnp.float32)


def drain(ref, sem):
    pltpu.make_async_copy(ref, ref, sem).wait()


def peers(axis):
    count, me = lax.axis_size(axis), lax.axis_index(axis)
    offsets = sorted(range(1, count), key=lambda o: (-min(o, count - o), o))
    return [lax.rem(me + o, count) for o in offsets]


def payload_rows(layers, half, rank, unit):
    at, ends = {}, []
    at["squares"], rows = 0, TILE
    for name, count in (("q", layers - 1), ("r", layers)):
        at[name], rows = rows, rows + count * half
    for k in range(layers - 1):
        for other in range(k, layers - 1):
            at["u", k, other], rows = rows, rows + rank
    rows = round_up(rows, unit)
    ends.append(rows)
    for part in range(2):
        at["p", part], rows = rows, rows + layers // 2 * half
        for k in range(layers - 1):
            for pair in range((k + 1) // 2, layers // 2):
                at["m", part, k, pair], rows = rows, rows + rank
        rows = round_up(rows, unit)
        ends.append(rows)
    return at, ends


def kernel(
    cap,
    own,
    choose,
    gains,
    down,
    tokens,
    cotangent,
    up,
    grad_down,
    grad_up,
    slope_out,
    own_v,
    choose_v,
    gains_v,
    up_v,
    down_v,
    tokv,
    cotv,
    sendbuf,
    recvbuf,
    gains_wide,
    w_gain,
    down_scaled,
    w_down,
    w_up,
    part,
    fin,
    got,
    got_y,
    acc_p,
    acc_q,
    acc_w,
    seen,
    big_m,
    big_u,
    xs,
    gs,
    zs,
    rd,
    prods,
    cur,
    first_x,
    first_cot,
    mask,
    back_d,
    back_u,
    slope_row,
    slopes,
    group_sem,
    all_sem,
    loc_sem,
    tok_s,
    tok_r,
    wd_s,
    wu_s,
    wg_s,
    wd_r,
    wu_r,
    wg_r,
    ar_s,
    ar_r,
    gd_s,
    gu_s,
    gd_r,
    gu_r,
    sl_s,
    sl_r,
):
    dp = lax.axis_index("dp")
    section = lax.axis_index("section")
    tensor = lax.axis_index("tensor")
    groups = lax.axis_size("dp")
    layers = lax.axis_size("section")
    ranks = lax.axis_size("tensor")
    bits = ranks.bit_length() - 1
    count = tokens.shape[0]
    fw = tokv.shape[1]
    width = tokens.shape[1] * ranks
    spad = sendbuf.shape[1]
    slots = xs.shape[1]
    half = slots // 2
    rank = LANES // 2
    each = slots // groups
    bf16, f32 = jnp.bfloat16, jnp.float32
    at, ends = payload_rows(layers, half, rank, TILE * layers * ranks)

    barrier = pltpu.get_barrier_semaphore()
    core = tensor & 1
    sibling = {"tensor": tensor ^ 1}

    def greet(device):
        pl.semaphore_signal(barrier, inc=1, device_id=device, device_id_type=MESH)

    chips = ranks // 2
    for away in range(layers):
        for over in range(chips):
            chip = lax.rem((tensor >> 1) + over, chips)
            if away or over:
                greet({"section": lax.rem(section + away, layers), "tensor": 2 * chip + 1})
    pl.when(core == 0)(lambda: greet(sibling))
    for peer in peers("dp"):
        greet({"dp": peer, "tensor": tensor - core})

    def group_arrived():
        @pl.when(core == 1)
        def _():
            pl.semaphore_wait(barrier, layers * ranks - 1)
            pl.semaphore_signal(group_sem, inc=1, device_id=sibling, device_id_type=MESH)

        @pl.when(core == 0)
        def _():
            pl.semaphore_wait(group_sem, 1)

    def all_arrived():
        @pl.when(core == 0)
        def _():
            pl.semaphore_wait(barrier, 2 * (groups - 1))
            pl.semaphore_signal(all_sem, inc=1, device_id=sibling, device_id_type=MESH)

        @pl.when(core == 1)
        def _():
            pl.semaphore_wait(all_sem, 1)

    def columns(index):
        return pl.ds(pl.multiple_of(index * fw, LANES), fw)

    quarter = rank // 2
    blocks = [
        (pl.ds((2 * a + h) * quarter, quarter), pl.ds((2 * h + a) * quarter, quarter))
        for a in range(2)
        for h in range(2)
    ]
    loads = [
        pltpu.make_async_copy(source, target, loc_sem.at[i])
        for i, (source, target) in enumerate(
            [
                (own, own_v),
                (choose, choose_v),
                (tokens.at[:, columns(section)], tokv),
                (cotangent.at[:, columns(section)], cotv),
                (gains, gains_v),
            ]
            + [(up.at[there], up_v.at[here]) for there, here in blocks]
            + [(down.at[there], down_v.at[here]) for there, here in blocks]
        )
    ]
    for load in loads:
        load.start()

    early = lax.broadcasted_iota(jnp.int32, (count, count), 0)
    late = lax.broadcasted_iota(jnp.int32, (count, count), 1)
    diagonal = early == late
    shift = MTOK.bit_length() - 1
    loads[0].wait()
    loads[1].wait()
    own_row = own_v[...].astype(f32)
    own_col = jnp.sum(jnp.where(diagonal, own_row, 0.0), 1, keepdims=True)
    before = (own_col == own_row) & (early < late) & ((early >> shift) == (late >> shift))
    rank_in = jnp.sum(jnp.where(before, 1.0, 0.0), 0, keepdims=True)
    micro_of = (lax.broadcasted_iota(jnp.int32, (1, count), 1) >> shift).astype(f32)
    place = micro_of * cap + rank_in
    spots = lax.broadcasted_iota(jnp.int32, (spad, count), 0).astype(f32)
    fits = place == spots
    member = jnp.concatenate(
        [jnp.where(fits & (own_row == d), 1.0, 0.0) for d in range(groups)], 0
    )
    flag = jnp.sum(member * choose_v[...].astype(f32), 1, keepdims=True)
    member = member.astype(bf16)
    loads[2].wait()
    loads[3].wait()
    sendbuf[:, :, 0:fw] = matmul(member, tokv[...], NN).astype(bf16).reshape(groups, spad, fw)
    sendbuf[:, :, fw : 2 * fw] = (
        matmul(member, cotv[...], NN).astype(bf16).reshape(groups, spad, fw)
    )
    sendbuf[:, :, 2 * fw :] = (
        jnp.broadcast_to(flag, (groups * spad, LANES)).astype(bf16).reshape(groups, spad, LANES)
    )

    group_arrived()

    def spread(source, target, send, recv, some=None):
        def rows_of(ref):
            return ref if some is None else ref.at[some]

        for peer in peers("section"):
            pltpu.make_async_remote_copy(
                rows_of(source).at[:, columns(peer)],
                rows_of(target.at[section]),
                send,
                recv.at[section],
                {"section": peer},
                MESH,
            ).start()
        pltpu.make_async_copy(
            rows_of(source).at[:, columns(section)], rows_of(target.at[section]), recv.at[section]
        ).start()

    for load in loads[5:9]:
        load.wait()
    spread(up_v, w_up, wu_s, wu_r)
    for load in loads[4:5] + loads[9:]:
        load.wait()
    down_scaled[...] = (down_v[...].astype(f32) * gains_v[...].astype(f32)).astype(bf16)
    all_arrived()
    for peer in peers("dp"):
        pltpu.make_async_remote_copy(
            sendbuf.at[peer], recvbuf.at[dp], tok_s, tok_r, {"dp": peer}, MESH
        ).start()
    recvbuf[dp] = sendbuf[dp]

    for part_of in range(2):
        spread(
            down_scaled,
            w_down,
            wd_s,
            wd_r.at[part_of],
            pl.ds(part_of * rank, rank),
        )
    gains_wide[...] = jnp.broadcast_to(gains_v[...], gains_wide.shape)
    spread(gains_wide, w_gain, wg_s, wg_r)

    cell = lax.broadcasted_iota(jnp.int32, (1, groups * spad), 1)
    source = sum((cell >= d * spad).astype(jnp.int32) for d in range(1, groups))
    within = cell - source * spad
    wanted = jnp.where(within < each, source * each + within, -1)
    slot_ids = lax.broadcasted_iota(jnp.int32, (slots, groups * spad), 0)
    compact = jnp.where(slot_ids == wanted, 1.0, 0.0).astype(bf16)
    drain(recvbuf.at[pl.ds(0, groups - 1)], tok_r)
    arrived = matmul(compact, recvbuf[...].reshape(groups * spad, 2 * fw + LANES), NN)
    x0 = arrived[:, 0:fw]
    first_x[...] = x0
    first_cot[...] = arrived[:, fw : 2 * fw]
    lane = lax.broadcasted_iota(jnp.int32, (slots, LANES), 1)
    second = arrived[:, 2 * fw :] > 0.5
    mask[...] = jnp.where(second == ((lane & quarter) > 0), 1.0, 0.0)

    even = (lax.broadcasted_iota(jnp.int32, (half, LANES), 1) & quarter) == 0
    even_rank = (lax.broadcasted_iota(jnp.int32, (rank, LANES), 1) & quarter) == 0
    left = lane < rank
    left_rank = lax.broadcasted_iota(jnp.int32, (rank, LANES), 1) < rank
    tall = lax.broadcasted_iota(jnp.int32, (TILE, LANES), 1)

    def packed(total):
        kept = total * mask[...]
        first = kept[0:half] + pltpu.roll(kept[0:half], LANES - quarter, 1)
        last = kept[half:] + pltpu.roll(kept[half:], quarter, 1)
        return jnp.where(even, first, last).astype(bf16)

    def unpacked(total):
        total = total.astype(f32)
        first = jnp.where(even, total, pltpu.roll(total, quarter, 1))
        last = jnp.where(even, pltpu.roll(total, LANES - quarter, 1), total)
        return jnp.concatenate([first, last], 0) * mask[...]

    def thinned(block):
        first, second, third, fourth = (
            block[i * quarter : (i + 1) * quarter] for i in range(4)
        )
        return jnp.where(
            even_rank,
            jnp.concatenate([first, third], 0),
            jnp.concatenate([second, fourth], 0),
        ).astype(bf16)

    def widened(block):
        block = block.astype(f32)
        evens, odds = jnp.where(even_rank, block, 0.0), jnp.where(even_rank, 0.0, block)
        return jnp.concatenate(
            [evens[0:quarter], odds[0:quarter], evens[quarter:], odds[quarter:]], 0
        ).astype(bf16)

    def layer_of(first, last, which, keep_left):
        if which == 0:
            return jnp.where(keep_left, first, pltpu.roll(last, rank, 1))
        return jnp.where(keep_left, pltpu.roll(first, rank, 1), last)

    squares = jnp.sum(x0 * x0, 1, keepdims=True)
    folded = jnp.zeros((TILE, LANES), f32)
    for q in range(slots // TILE):
        folded = jnp.where(tall == q, squares[q * TILE : (q + 1) * TILE], folded)
    part[0:TILE] = folded.astype(bf16)

    for layer in range(layers):
        drain(w_up.at[layer], wu_r.at[layer])
    x_low = first_x[...].astype(bf16)
    cot_low = first_cot[...].astype(bf16)
    for layer in range(layers):
        weight = w_up[layer]
        if layer < layers - 1:
            row = at["q"] + layer * half
            part[row : row + half] = packed(matmul(x_low, weight, NT))
        row = at["r"] + layer * half
        part[row : row + half] = packed(matmul(cot_low, weight, NT))
    for k in range(layers - 1):
        stacked = w_up[k : layers - 1].reshape((layers - 1 - k) * LANES, fw)
        product = matmul(w_up[k], stacked, NT)
        for i, other in enumerate(range(k, layers - 1)):
            row = at["u", k, other]
            part[row : row + rank] = thinned(product[:, i * LANES : (i + 1) * LANES])

    def down_products(h):
        for layer in range(layers):
            drain(w_down.at[layer, pl.ds(h * rank, rank)], wd_r.at[h, layer])
        weights = w_down[:, h * rank : (h + 1) * rank].reshape(layers * rank, fw)
        product = matmul(x_low, weights, NT)
        for pair in range(layers // 2):
            row = at["p", h] + pair * half
            part[row : row + half] = packed(product[:, pair * LANES : (pair + 1) * LANES])
        for k in range(layers - 1):
            skip = (k + 1) // 2
            product = matmul(w_up[k], weights[skip * LANES :], NT)
            for pair in range(skip, layers // 2):
                row = at["m", h, k, pair]
                i = pair - skip
                part[row : row + rank] = thinned(product[:, i * LANES : (i + 1) * LANES])

    def rows(first, size):
        return pl.ds(pl.multiple_of(first, TILE), size)

    def all_reduce(chunk, joint):
        first = ends[chunk - 1] if chunk else 0
        size = ends[chunk] - first
        halvings = bits - 1 if joint and bits > 1 else bits
        strides = [] if halvings == bits else [1 << halvings]
        whole, piece = size, (size >> halvings) // (layers << len(strides))
        base, stage, starts = first, 0, []
        sends, arrivals = ar_s.at[chunk], ar_r.at[chunk]
        others = [({"section": peer}, peer, 0) for peer in peers("section")]
        high = 0
        for stride in strides:
            high = (tensor // stride) & 1
            away = tensor ^ stride
            others = (
                [({"section": peer, "tensor": away}, peer, 1) for peer in peers("section")]
                + others
                + [({"tensor": away}, section, 1)]
            )

        def index_of(peer, crossed):
            return peer + layers * (high + crossed - 2 * high * crossed)

        def send(source, target, device):
            pltpu.make_async_remote_copy(
                source, target, sends.at[stage], arrivals.at[stage], device, MESH
            ).start()

        for bit in range(halvings):
            size //= 2
            mine = (tensor >> bit) & 1
            keep, give = base + mine * size, base + (1 - mine) * size
            peer = tensor ^ (1 << bit)
            spot = first + whole - 2 * size
            send(part.at[rows(give, size)], got.at[pl.ds(spot, size)], {"tensor": peer})
            yield
            drain(got.at[pl.ds(spot, size)], arrivals.at[stage])
            part[rows(keep, size)] = (
                part[rows(keep, size)].astype(f32) + got[spot : spot + size].astype(f32)
            ).astype(bf16)
            starts.append((keep, size, peer))
            base, stage = keep, stage + 1
        landed = got_y.at[chunk]
        for o, (device, peer, crossed) in enumerate(others):
            send(
                part.at[rows(base + index_of(peer, crossed) * piece, piece)],
                landed.at[pl.ds(o * piece, piece)],
                device,
            )
        yield
        filled = len(others) * piece
        drain(landed.at[pl.ds(0, filled)], arrivals.at[stage])
        stage += 1
        mine = base + index_of(section, 0) * piece
        total = part[rows(mine, piece)].astype(f32)
        for o in range(len(others)):
            total += got_y[chunk, o * piece : (o + 1) * piece].astype(f32)
        fin[rows(mine, piece)] = total.astype(bf16)
        for device, _, _ in others:
            send(fin.at[rows(mine, piece)], fin.at[rows(mine, piece)], device)
        yield
        drain(fin.at[pl.ds(first, filled)], arrivals.at[stage])
        stage += 1
        for keep, size, peer in reversed(starts):
            send(fin.at[rows(keep, size)], fin.at[rows(keep, size)], {"tensor": peer})
            yield
            drain(fin.at[pl.ds(first, size)], arrivals.at[stage])
            stage += 1
        sizes = [size for _, size, _ in starts]
        for i, size in enumerate([*sizes, filled, filled, *reversed(sizes)]):
            sent.append((first, size, sends.at[i]))

    sent = []
    chunks = [all_reduce(0, False), all_reduce(1, False), all_reduce(2, JOINT)]

    def advance(order):
        for chunk in order:
            next(chunks[chunk], None)

    advance([0, 0])
    down_products(0)
    advance([1])
    advance([0, 1] if bits > 1 else [1])
    down_products(1)
    advance([2])
    advance([1, 0, 2, 0, 1, 2, 0, 1, 2, 0, 1, 2, 0, 1, 2, 0, 1, 2])

    def lanes(first, last=None):
        return slice(first * LANES, (first + 1 if last is None else last) * LANES)

    for name, target, number in (("q", acc_q, layers - 1), ("r", acc_w, layers)):
        for layer in range(number):
            row = at[name] + layer * half
            target[:, lanes(layer)] = unpacked(fin[row : row + half])
    for pair in range(layers // 2):
        row, last_row = (at["p", h] + pair * half for h in range(2))
        first = unpacked(fin[row : row + half])
        last = unpacked(fin[last_row : last_row + half])
        for which in range(2):
            acc_p[:, lanes(2 * pair + which)] = layer_of(first, last, which, left)
    for k in range(layers - 1):
        for other in range(k, layers - 1):
            row = at["u", k, other]
            big_u[k, :, lanes(other)] = widened(fin[row : row + rank])
        for pair in range((k + 1) // 2, layers // 2):
            first, last = (
                fin[row : row + rank].astype(f32)
                for row in (at["m", h, k, pair] for h in range(2))
            )
            for which in range(2):
                if 2 * pair + which > k:
                    block = layer_of(first, last, which, left_rank)
                    big_m[k, :, lanes(2 * pair + which)] = widened(block)
    folded = fin[0:TILE].astype(f32)
    squares = jnp.concatenate(
        [
            jnp.sum(jnp.where(tall == q, folded, 0.0), 1, keepdims=True)
            for q in range(slots // TILE)
        ],
        0,
    )

    scales = []
    for k in range(layers):
        scale_rows = lax.rsqrt(squares / width + EPS)
        scales.append(scale_rows)
        latent = (acc_p[:, lanes(k)] * scale_rows).astype(bf16)
        zs[k] = latent
        x = first_x[...] if k == 0 else cur[...]
        xs[k] = x.astype(bf16)
        if k < layers - 1:
            cur[...] = x + SCALE * matmul(latent, w_up[k], NN)
            acc_p[:, lanes(k + 1, layers)] += SCALE * matmul(
                latent, big_m[k, :, lanes(k + 1, layers)], NN
            )
            inner = acc_q[:, lanes(k)]
            step = SCALE * matmul(latent, big_u[k, :, lanes(k, layers - 1)], NN)
            squares = jnp.maximum(
                squares
                + jnp.sum(
                    latent.astype(f32) * (inner + 0.5 * step[:, 0:LANES]), 1, keepdims=True
                ),
                0.0,
            )
            acc_q[:, lanes(k, layers - 1)] += step
            if k > 0:
                others = big_u[0:k, :, lanes(k)].reshape(k * LANES, LANES)
                acc_q[:, lanes(0, k)] += SCALE * matmul(latent, others, NT)
            seen[k + 1, :, lanes(0, k + 1)] = acc_q[:, lanes(0, k + 1)].astype(bf16)

    for m in reversed(range(layers)):
        rank_low = (SCALE * acc_w[:, lanes(m)]).astype(bf16)
        product = rank_low.astype(f32) * zs[m].astype(f32)
        prods[m] = product
        scale_rows = scales[m]
        scaled = (rank_low.astype(f32) * scale_rows).astype(bf16)
        rd[m] = scaled
        g = first_cot[...] if m == layers - 1 else cur[...]
        gs[m] = g.astype(bf16)
        if m > 0:
            weight = scale_rows * scale_rows * jnp.sum(product, 1, keepdims=True) / width
            cur[...] = (
                g + matmul(scaled, w_down[m], NN) - weight * xs[m].astype(f32)
            )
            others = big_m[0:m, :, lanes(m)].reshape(m * LANES, LANES)
            acc_w[:, lanes(0, m)] += matmul(scaled, others, NT) - weight * seen[
                m, :, lanes(0, m)
            ].astype(f32)

    for layer in range(layers):
        drain(w_gain.at[layer], wg_r.at[layer])

    def down_grad(layer):
        gain = w_gain[layer, 0:1].astype(f32)
        back_d[layer] = (matmul(rd[layer], xs[layer], TN) * gain).astype(bf16)
        return back_d.at[layer], grad_down.at[:, columns(section)], gd_s, gd_r

    def up_grad(layer):
        back_u[layer] = (SCALE * matmul(zs[layer], gs[layer], TN)).astype(bf16)
        return back_u.at[layer], grad_up.at[:, columns(section)], gu_s, gu_r

    for make in (down_grad, up_grad):
        for layer in peers("section"):
            source, target, send, recv = make(layer)
            pltpu.make_async_remote_copy(
                source, target, send, recv, {"section": layer}, MESH
            ).start()
    for make in (down_grad, up_grad):
        source, target, _, recv = make(section)
        pltpu.make_async_copy(source, target, recv).start()

    slope_row[:, 0:slots] = lax.dot_general(
        jnp.full((8, LANES), 1.0 / math.sqrt(width), f32),
        prods[section],
        (NT, ((), ())),
        preferred_element_type=f32,
        precision=lax.Precision.HIGHEST,
    )
    for peer in peers("dp"):
        pltpu.make_async_remote_copy(
            slope_row, slopes.at[dp], sl_s, sl_r, {"dp": peer}, MESH
        ).start()
    slopes[dp] = slope_row[...]

    drain(recvbuf.at[pl.ds(0, groups - 1)], tok_s)
    drain(w_down.at[pl.ds(0, layers - 1)], wd_s)
    drain(w_up.at[pl.ds(0, layers - 1)], wu_s)
    drain(w_gain.at[pl.ds(0, layers - 1)], wg_s)
    for first, size, sem in sent:
        drain(fin.at[pl.ds(first, size)], sem)
    drain(back_d.at[pl.ds(0, layers - 1)], gd_s)
    drain(back_u.at[pl.ds(0, layers - 1)], gu_s)
    drain(slopes.at[pl.ds(0, groups - 1)], sl_s)

    drain(slopes.at[pl.ds(0, groups - 1)], sl_r)
    wide = slopes.shape[2]
    found = jnp.zeros((count, wide), f32)
    for d in range(groups):
        found = jnp.where(own_col == d, slopes[d, 0:1], found)
    first_slot = (dp * each).astype(f32)
    place_col = jnp.sum(jnp.where(diagonal, place, 0.0), 1, keepdims=True) + first_slot
    here = lax.broadcasted_iota(jnp.int32, (count, wide), 1).astype(f32) == place_col
    slope_col = jnp.sum(jnp.where(here, found, 0.0), 1, keepdims=True)
    slope_out[...] = jnp.sum(jnp.where(diagonal, slope_col, 0.0), 0, keepdims=True)

    drain(grad_up, gu_r)
    drain(grad_down, gd_r)


def finish(raw_down, raw_up, raw_slope, grad_down, grad_up, slope, v_down, v_up, v_slope, loads, stores):
    parts = (loads.shape[0] - 1) // 2
    rows = grad_up.shape[0] // parts
    pieces = [(raw_slope, v_slope, slope)]
    for i, block in enumerate((0, 2, 1, 3)):
        some, home = pl.ds(i * rows, rows), pl.ds(block * rows, rows)
        pieces.append((raw_up.at[some], v_up.at[some], grad_up.at[home]))
        pieces.append((raw_down.at[some], v_down.at[some], grad_down.at[home]))
    reads = [
        pltpu.make_async_copy(source, through, loads.at[i])
        for i, (source, through, _) in enumerate(pieces)
    ]
    writes = [
        pltpu.make_async_copy(through, target, stores.at[i])
        for i, (_, through, target) in enumerate(pieces)
    ]
    for read in reads:
        read.start()
    for read, write in zip(reads, writes):
        read.wait()
        write.start()
    for write in writes:
        write.wait()


def on_device(
    tokens,
    owner_indices,
    local_adapter_index,
    gains,
    adapter_down_weights,
    adapter_up_weights,
    cotangent,
):
    groups, layers, ranks = (lax.axis_size(a) for a in ("dp", "section", "tensor"))
    count, local = tokens.shape
    micro = count // MTOK
    cap = 5 * MTOK // (4 * groups)
    each = micro * cap
    spad = round_up(each, TILE)
    slots = groups * each
    fw = local // layers
    adapters, rank = adapter_down_weights.shape[1:3]
    weight_rows = adapters * rank
    half = slots // 2
    wide = round_up(slots, LANES)
    _, ends = payload_rows(layers, half, rank, TILE * layers * ranks)
    rows = ends[-1]
    most = max(b - a for a, b in zip([0] + ends, ends))
    stages = 2 * (ranks.bit_length() - 1) + 2
    vmem = pl.BlockSpec(memory_space=pltpu.VMEM)
    anywhere = pl.BlockSpec(memory_space=pltpu.HBM)
    b16, f32 = jnp.bfloat16, jnp.float32
    dma = pltpu.SemaphoreType.DMA
    raw = pl.pallas_call(
        functools.partial(kernel, cap),
        out_shape=(
            jax.ShapeDtypeStruct((weight_rows, local), b16),
            jax.ShapeDtypeStruct((weight_rows, local), b16),
            jax.ShapeDtypeStruct((1, count), f32),
        ),
        in_specs=[anywhere] * 7,
        out_specs=(anywhere, anywhere, vmem),
        scratch_shapes=[
            pltpu.VMEM((1, count), jnp.int32),
            pltpu.VMEM((1, count), jnp.int32),
            pltpu.VMEM((1, local), b16),
            pltpu.VMEM((weight_rows, local), b16),
            pltpu.VMEM((weight_rows, local), b16),
            pltpu.VMEM((count, fw), b16),
            pltpu.VMEM((count, fw), b16),
            pltpu.VMEM((groups, spad, 2 * fw + LANES), b16),
            pltpu.VMEM((groups, spad, 2 * fw + LANES), b16),
            pltpu.VMEM((TILE, local), b16),
            pltpu.VMEM((layers, TILE, fw), b16),
            pltpu.VMEM((weight_rows, local), b16),
            pltpu.VMEM((layers, weight_rows, fw), b16),
            pltpu.VMEM((layers, weight_rows, fw), b16),
            pltpu.VMEM((rows, LANES), b16),
            pltpu.VMEM((rows, LANES), b16),
            pltpu.VMEM((rows, LANES), b16),
            pltpu.VMEM((3, most, LANES), b16),
            pltpu.VMEM((slots, layers * LANES), f32),
            pltpu.VMEM((slots, layers * LANES), f32),
            pltpu.VMEM((slots, layers * LANES), f32),
            pltpu.VMEM((layers, slots, layers * LANES), b16),
            pltpu.VMEM((layers, LANES, layers * LANES), b16),
            pltpu.VMEM((layers, LANES, layers * LANES), b16),
            pltpu.VMEM((layers, slots, fw), b16),
            pltpu.VMEM((layers, slots, fw), b16),
            pltpu.VMEM((layers, slots, LANES), b16),
            pltpu.VMEM((layers, slots, LANES), b16),
            pltpu.VMEM((layers, slots, LANES), f32),
            pltpu.VMEM((slots, fw), f32),
            pltpu.VMEM((slots, fw), f32),
            pltpu.VMEM((slots, fw), f32),
            pltpu.VMEM((slots, LANES), f32),
            pltpu.VMEM((layers, weight_rows, fw), b16),
            pltpu.VMEM((layers, weight_rows, fw), b16),
            pltpu.VMEM((8, wide), f32),
            pltpu.VMEM((groups, 8, wide), f32),
            pltpu.SemaphoreType.REGULAR,
            pltpu.SemaphoreType.REGULAR,
            dma((13,)),
            dma,
            dma,
            dma,
            dma,
            dma,
            dma((2, layers)),
            dma((layers,)),
            dma((layers,)),
            dma((3, stages)),
            dma((3, stages)),
            dma,
            dma,
            dma,
            dma,
            dma,
            dma,
        ],
        compiler_params=pltpu.CompilerParams(
            collective_id=0, has_side_effects=True, vmem_limit_bytes=62 * 1024 * 1024
        ),
    )(
        owner_indices.reshape(1, count),
        local_adapter_index.reshape(1, count),
        gains,
        adapter_down_weights.reshape(weight_rows, local),
        tokens,
        cotangent,
        adapter_up_weights.reshape(weight_rows, local),
    )
    grad_down, grad_up, slope = pl.pallas_call(
        finish,
        out_shape=tuple(jax.ShapeDtypeStruct(r.shape, r.dtype) for r in raw),
        in_specs=[anywhere] * 3,
        out_specs=(anywhere,) * 3,
        scratch_shapes=[pltpu.VMEM(r.shape, r.dtype) for r in raw] + [dma((9,)), dma((9,))],
        compiler_params=pltpu.CompilerParams(vmem_limit_bytes=62 * 1024 * 1024),
    )(*raw)
    shape = (1, adapters, rank, local)
    return (grad_down.reshape(shape), grad_up.reshape(shape), slope)


def solution(mesh):
    return jax.shard_map(
        on_device,
        mesh=mesh,
        in_specs=(
            P("dp", "tensor"),
            P("dp", None),
            P("dp"),
            P("section", "tensor"),
            P("section", "dp", None, "tensor"),
            P("section", "dp", None, "tensor"),
            P("dp", "tensor"),
        ),
        out_specs=(
            P("section", "dp", None, "tensor"),
            P("section", "dp", None, "tensor"),
            P("section", "dp"),
        ),
        check_vma=False,
    )
```

```python
import functools
import math

import jax
import jax.numpy as jnp
from jax import lax
from jax.experimental import pallas as pl
from jax.experimental.pallas import tpu as pltpu
from jax.sharding import PartitionSpec as P

MTOK = 64
LANES = 128
TILE = 16
JOINT = True
EPS = 1e-05
SCALE = 0.5
MESH = pl.DeviceIdType.MESH
NN = ((1,), (0,))
NT = ((1,), (1,))
TN = ((0,), (0,))


def round_up(value, unit):
    return -(-value // unit) * unit


def matmul(a, b, contract):
    return lax.dot_general(a, b, (contract, ((), ())), preferred_element_type=jnp.float32)


def drain(ref, sem):
    pltpu.make_async_copy(ref, ref, sem).wait()


def peers(axis):
    count, me = lax.axis_size(axis), lax.axis_index(axis)
    offsets = sorted(range(1, count), key=lambda o: (-min(o, count - o), o))
    return [lax.rem(me + o, count) for o in offsets]


def shared_blocks(layers):
    return (layers - 2, layers - 4) if layers >= 4 else (None, None)


def payload_rows(layers, half, rank, unit):
    at, ends = {}, []
    at["squares"], rows = 0, TILE
    for name, count in (("q", layers - 1), ("r", layers)):
        at[name], rows = rows, rows + count * half
    blocks = [("u", k, other) for k in range(layers - 1) for other in range(k, layers - 1)]
    left, right = shared_blocks(layers)
    later = []
    for part in range(2):
        parts = [(("p", part), layers // 2 * half)]
        for k in range(layers - 1):
            for pair in range((k + 1) // 2, layers // 2):
                if k != left:
                    parts.append((("m", part, k, pair), rank))
        later.append(parts)
    free = [-sum(size for _, size in parts) % unit // rank for parts in later]
    over = -(-((rows + len(blocks) * rank) % unit) // rank)
    if over <= sum(free):
        for parts, room in zip(later, free):
            take = min(room, over)
            over -= take
            for _ in range(take):
                parts.append((blocks.pop(), rank))
    for parts in [[(block, rank) for block in blocks], *later]:
        for name, size in parts:
            at[name], rows = rows, rows + size
        rows = round_up(rows, unit)
        ends.append(rows)
    for part in range(2):
        if left is not None:
            at["m", part, left, layers // 2 - 1] = at["m", part, right, layers // 2 - 2]
    return at, ends


def kernel(
    cap,
    own,
    choose,
    gains,
    down,
    tokens,
    cotangent,
    up,
    grad_down,
    grad_up,
    slope_out,
    own_v,
    choose_v,
    gains_v,
    up_v,
    down_v,
    tokv,
    cotv,
    sendbuf,
    recvbuf,
    gains_wide,
    w_gain,
    down_scaled,
    w_down,
    w_up,
    part,
    fin,
    got,
    got_y,
    acc_p,
    acc_q,
    acc_w,
    seen,
    big_m,
    big_u,
    xs,
    gs,
    zs,
    rd,
    prods,
    cur,
    first_x,
    first_cot,
    mask,
    back_d,
    back_u,
    slope_row,
    slopes,
    group_sem,
    all_sem,
    loc_sem,
    tok_s,
    tok_r,
    wd_s,
    wu_s,
    wg_s,
    wd_r,
    wu_r,
    wg_r,
    ar_s,
    ar_r,
    gd_s,
    gu_s,
    gd_r,
    gu_r,
    sl_s,
    sl_r,
):
    dp = lax.axis_index("dp")
    section = lax.axis_index("section")
    tensor = lax.axis_index("tensor")
    groups = lax.axis_size("dp")
    layers = lax.axis_size("section")
    ranks = lax.axis_size("tensor")
    bits = ranks.bit_length() - 1
    count = tokens.shape[0]
    fw = tokv.shape[1]
    width = tokens.shape[1] * ranks
    spad = sendbuf.shape[1]
    slots = xs.shape[1]
    half = slots // 2
    rank = LANES // 2
    each = slots // groups
    bf16, f32 = jnp.bfloat16, jnp.float32
    at, ends = payload_rows(layers, half, rank, TILE * layers * ranks)
    left_k, _ = shared_blocks(layers)

    barrier = pltpu.get_barrier_semaphore()
    core = tensor & 1
    sibling = {"tensor": tensor ^ 1}

    def greet(device):
        pl.semaphore_signal(barrier, inc=1, device_id=device, device_id_type=MESH)

    chips = ranks // 2
    for away in range(layers):
        for over in range(chips):
            chip = lax.rem((tensor >> 1) + over, chips)
            if away or over:
                greet({"section": lax.rem(section + away, layers), "tensor": 2 * chip + 1})
    pl.when(core == 0)(lambda: greet(sibling))
    for peer in peers("dp"):
        greet({"dp": peer, "tensor": tensor - core})

    def group_arrived():
        @pl.when(core == 1)
        def _():
            pl.semaphore_wait(barrier, layers * ranks - 1)
            pl.semaphore_signal(group_sem, inc=1, device_id=sibling, device_id_type=MESH)

        @pl.when(core == 0)
        def _():
            pl.semaphore_wait(group_sem, 1)

    def all_arrived():
        @pl.when(core == 0)
        def _():
            pl.semaphore_wait(barrier, 2 * (groups - 1))
            pl.semaphore_signal(all_sem, inc=1, device_id=sibling, device_id_type=MESH)

        @pl.when(core == 1)
        def _():
            pl.semaphore_wait(all_sem, 1)

    def columns(index):
        return pl.ds(pl.multiple_of(index * fw, LANES), fw)

    quarter = rank // 2
    blocks = [
        (pl.ds((2 * a + h) * quarter, quarter), pl.ds((2 * h + a) * quarter, quarter))
        for a in range(2)
        for h in range(2)
    ]
    loads = [
        pltpu.make_async_copy(source, target, loc_sem.at[i])
        for i, (source, target) in enumerate(
            [
                (own, own_v),
                (choose, choose_v),
                (tokens.at[:, columns(section)], tokv),
                (cotangent.at[:, columns(section)], cotv),
                (gains, gains_v),
            ]
            + [(up.at[there], up_v.at[here]) for there, here in blocks]
            + [(down.at[there], down_v.at[here]) for there, here in blocks]
        )
    ]
    for load in loads:
        load.start()

    early = lax.broadcasted_iota(jnp.int32, (count, count), 0)
    late = lax.broadcasted_iota(jnp.int32, (count, count), 1)
    diagonal = early == late
    shift = MTOK.bit_length() - 1
    loads[0].wait()
    loads[1].wait()
    own_row = own_v[...].astype(f32)
    own_col = jnp.sum(jnp.where(diagonal, own_row, 0.0), 1, keepdims=True)
    before = (own_col == own_row) & (early < late) & ((early >> shift) == (late >> shift))
    rank_in = jnp.sum(jnp.where(before, 1.0, 0.0), 0, keepdims=True)
    micro_of = (lax.broadcasted_iota(jnp.int32, (1, count), 1) >> shift).astype(f32)
    place = micro_of * cap + rank_in
    spots = lax.broadcasted_iota(jnp.int32, (spad, count), 0).astype(f32)
    fits = place == spots
    member = jnp.concatenate(
        [jnp.where(fits & (own_row == d), 1.0, 0.0) for d in range(groups)], 0
    )
    flag = jnp.sum(member * choose_v[...].astype(f32), 1, keepdims=True)
    member = member.astype(bf16)
    loads[2].wait()
    loads[3].wait()
    sendbuf[:, :, 0:fw] = matmul(member, tokv[...], NN).astype(bf16).reshape(groups, spad, fw)
    sendbuf[:, :, fw : 2 * fw] = (
        matmul(member, cotv[...], NN).astype(bf16).reshape(groups, spad, fw)
    )
    sendbuf[:, :, 2 * fw :] = (
        jnp.broadcast_to(flag, (groups * spad, LANES)).astype(bf16).reshape(groups, spad, LANES)
    )

    group_arrived()

    def spread(source, target, send, recv, some=None):
        def rows_of(ref):
            return ref if some is None else ref.at[some]

        for peer in peers("section"):
            pltpu.make_async_remote_copy(
                rows_of(source).at[:, columns(peer)],
                rows_of(target.at[section]),
                send,
                recv.at[section],
                {"section": peer},
                MESH,
            ).start()
        pltpu.make_async_copy(
            rows_of(source).at[:, columns(section)], rows_of(target.at[section]), recv.at[section]
        ).start()

    for load in loads[5:9]:
        load.wait()
    spread(up_v, w_up, wu_s, wu_r)
    for load in loads[4:5] + loads[9:]:
        load.wait()
    down_scaled[...] = (down_v[...].astype(f32) * gains_v[...].astype(f32)).astype(bf16)
    all_arrived()
    for peer in peers("dp"):
        pltpu.make_async_remote_copy(
            sendbuf.at[peer], recvbuf.at[dp], tok_s, tok_r, {"dp": peer}, MESH
        ).start()
    recvbuf[dp] = sendbuf[dp]

    for part_of in range(2):
        spread(
            down_scaled,
            w_down,
            wd_s,
            wd_r.at[part_of],
            pl.ds(part_of * rank, rank),
        )
    gains_wide[...] = jnp.broadcast_to(gains_v[...], gains_wide.shape)
    spread(gains_wide, w_gain, wg_s, wg_r)

    cell = lax.broadcasted_iota(jnp.int32, (1, groups * spad), 1)
    source = sum((cell >= d * spad).astype(jnp.int32) for d in range(1, groups))
    within = cell - source * spad
    wanted = jnp.where(within < each, source * each + within, -1)
    slot_ids = lax.broadcasted_iota(jnp.int32, (slots, groups * spad), 0)
    compact = jnp.where(slot_ids == wanted, 1.0, 0.0).astype(bf16)
    drain(recvbuf.at[pl.ds(0, groups - 1)], tok_r)
    arrived = matmul(compact, recvbuf[...].reshape(groups * spad, 2 * fw + LANES), NN)
    x0 = arrived[:, 0:fw]
    first_x[...] = x0
    first_cot[...] = arrived[:, fw : 2 * fw]
    lane = lax.broadcasted_iota(jnp.int32, (slots, LANES), 1)
    second = arrived[:, 2 * fw :] > 0.5
    mask[...] = jnp.where(second == ((lane & quarter) > 0), 1.0, 0.0)

    even = (lax.broadcasted_iota(jnp.int32, (half, LANES), 1) & quarter) == 0
    even_rank = (lax.broadcasted_iota(jnp.int32, (rank, LANES), 1) & quarter) == 0
    left = lane < rank
    left_rank = lax.broadcasted_iota(jnp.int32, (rank, LANES), 1) < rank
    tall = lax.broadcasted_iota(jnp.int32, (TILE, LANES), 1)

    def packed(total):
        kept = total * mask[...]
        first = kept[0:half] + pltpu.roll(kept[0:half], LANES - quarter, 1)
        last = kept[half:] + pltpu.roll(kept[half:], quarter, 1)
        return jnp.where(even, first, last).astype(bf16)

    def unpacked(total):
        total = total.astype(f32)
        first = jnp.where(even, total, pltpu.roll(total, quarter, 1))
        last = jnp.where(even, pltpu.roll(total, LANES - quarter, 1), total)
        return jnp.concatenate([first, last], 0) * mask[...]

    def thinned(block):
        first, second, third, fourth = (
            block[i * quarter : (i + 1) * quarter] for i in range(4)
        )
        return jnp.where(
            even_rank,
            jnp.concatenate([first, third], 0),
            jnp.concatenate([second, fourth], 0),
        ).astype(bf16)

    def widened(block):
        block = block.astype(f32)
        evens, odds = jnp.where(even_rank, block, 0.0), jnp.where(even_rank, 0.0, block)
        return jnp.concatenate(
            [evens[0:quarter], odds[0:quarter], evens[quarter:], odds[quarter:]], 0
        ).astype(bf16)

    def layer_of(first, last, which, keep_left):
        if which == 0:
            return jnp.where(keep_left, first, pltpu.roll(last, rank, 1))
        return jnp.where(keep_left, pltpu.roll(first, rank, 1), last)

    squares = jnp.sum(x0 * x0, 1, keepdims=True)
    folded = jnp.zeros((TILE, LANES), f32)
    for q in range(slots // TILE):
        folded = jnp.where(tall == q, squares[q * TILE : (q + 1) * TILE], folded)
    part[0:TILE] = folded.astype(bf16)

    for layer in range(layers):
        drain(w_up.at[layer], wu_r.at[layer])
    x_low = first_x[...].astype(bf16)
    cot_low = first_cot[...].astype(bf16)
    for layer in range(layers):
        weight = w_up[layer]
        if layer < layers - 1:
            row = at["q"] + layer * half
            part[row : row + half] = packed(matmul(x_low, weight, NT))
        row = at["r"] + layer * half
        part[row : row + half] = packed(matmul(cot_low, weight, NT))
    for k in range(layers - 1):
        stacked = w_up[k : layers - 1].reshape((layers - 1 - k) * LANES, fw)
        product = matmul(w_up[k], stacked, NT)
        for i, other in enumerate(range(k, layers - 1)):
            row = at["u", k, other]
            part[row : row + rank] = thinned(product[:, i * LANES : (i + 1) * LANES])

    def down_products(h):
        for layer in range(layers):
            drain(w_down.at[layer, pl.ds(h * rank, rank)], wd_r.at[h, layer])
        weights = w_down[:, h * rank : (h + 1) * rank].reshape(layers * rank, fw)
        product = matmul(x_low, weights, NT)
        for pair in range(layers // 2):
            row = at["p", h] + pair * half
            part[row : row + half] = packed(product[:, pair * LANES : (pair + 1) * LANES])
        for k in range(layers - 1):
            skip = (k + 1) // 2
            product = matmul(w_up[k], weights[skip * LANES :], NT)
            for pair in range(skip, layers // 2):
                row = at["m", h, k, pair]
                i = pair - skip
                block = thinned(product[:, i * LANES : (i + 1) * LANES])
                if k == left_k:
                    block = jnp.where(
                        left_rank, pltpu.roll(block.astype(f32), rank, 1), part[row : row + rank]
                    ).astype(bf16)
                part[row : row + rank] = block

    def rows(first, size):
        return pl.ds(pl.multiple_of(first, TILE), size)

    def all_reduce(chunk, joint):
        first = ends[chunk - 1] if chunk else 0
        size = ends[chunk] - first
        halvings = bits - 1 if joint and bits > 1 else bits
        strides = [] if halvings == bits else [1 << halvings]
        whole, piece = size, (size >> halvings) // (layers << len(strides))
        base, stage, starts = first, 0, []
        sends, arrivals = ar_s.at[chunk], ar_r.at[chunk]
        others = [({"section": peer}, peer, 0) for peer in peers("section")]
        high = 0
        for stride in strides:
            high = (tensor // stride) & 1
            away = tensor ^ stride
            others = (
                [({"section": peer, "tensor": away}, peer, 1) for peer in peers("section")]
                + others
                + [({"tensor": away}, section, 1)]
            )

        def index_of(peer, crossed):
            return peer + layers * (high + crossed - 2 * high * crossed)

        def send(source, target, device):
            pltpu.make_async_remote_copy(
                source, target, sends.at[stage], arrivals.at[stage], device, MESH
            ).start()

        for bit in range(halvings):
            size //= 2
            mine = (tensor >> bit) & 1
            keep, give = base + mine * size, base + (1 - mine) * size
            peer = tensor ^ (1 << bit)
            spot = first + whole - 2 * size
            send(part.at[rows(give, size)], got.at[pl.ds(spot, size)], {"tensor": peer})
            yield
            drain(got.at[pl.ds(spot, size)], arrivals.at[stage])
            part[rows(keep, size)] = (
                part[rows(keep, size)].astype(f32) + got[spot : spot + size].astype(f32)
            ).astype(bf16)
            starts.append((keep, size, peer))
            base, stage = keep, stage + 1
        landed = got_y.at[chunk]
        for o, (device, peer, crossed) in enumerate(others):
            send(
                part.at[rows(base + index_of(peer, crossed) * piece, piece)],
                landed.at[pl.ds(o * piece, piece)],
                device,
            )
        yield
        filled = len(others) * piece
        drain(landed.at[pl.ds(0, filled)], arrivals.at[stage])
        stage += 1
        mine = base + index_of(section, 0) * piece
        total = part[rows(mine, piece)].astype(f32)
        for o in range(len(others)):
            total += got_y[chunk, o * piece : (o + 1) * piece].astype(f32)
        fin[rows(mine, piece)] = total.astype(bf16)
        for device, _, _ in others:
            send(fin.at[rows(mine, piece)], fin.at[rows(mine, piece)], device)
        yield
        drain(fin.at[pl.ds(first, filled)], arrivals.at[stage])
        stage += 1
        for keep, size, peer in reversed(starts):
            send(fin.at[rows(keep, size)], fin.at[rows(keep, size)], {"tensor": peer})
            yield
            drain(fin.at[pl.ds(first, size)], arrivals.at[stage])
            stage += 1
        sizes = [size for _, size, _ in starts]
        for i, size in enumerate([*sizes, filled, filled, *reversed(sizes)]):
            sent.append((first, size, sends.at[i]))

    sent = []
    chunks = [all_reduce(0, False), all_reduce(1, False), all_reduce(2, JOINT)]

    def advance(order):
        for chunk in order:
            next(chunks[chunk], None)

    advance([0, 0])
    down_products(0)
    advance([1])
    advance([0, 1] if bits > 1 else [1])
    down_products(1)
    advance([2])
    advance([1, 0, 2, 0, 1, 2, 0, 1, 2, 0, 1, 2, 0, 1, 2, 0, 1, 2])

    def lanes(first, last=None):
        return slice(first * LANES, (first + 1 if last is None else last) * LANES)

    for name, target, number in (("q", acc_q, layers - 1), ("r", acc_w, layers)):
        for layer in range(number):
            row = at[name] + layer * half
            target[:, lanes(layer)] = unpacked(fin[row : row + half])
    for pair in range(layers // 2):
        row, last_row = (at["p", h] + pair * half for h in range(2))
        first = unpacked(fin[row : row + half])
        last = unpacked(fin[last_row : last_row + half])
        for which in range(2):
            acc_p[:, lanes(2 * pair + which)] = layer_of(first, last, which, left)
    for k in range(layers - 1):
        for other in range(k, layers - 1):
            row = at["u", k, other]
            big_u[k, :, lanes(other)] = widened(fin[row : row + rank])
        for pair in range((k + 1) // 2, layers // 2):
            first, last = (
                fin[row : row + rank].astype(f32)
                for row in (at["m", h, k, pair] for h in range(2))
            )
            for which in range(2):
                if 2 * pair + which > k:
                    block = layer_of(first, last, 0 if k == left_k else which, left_rank)
                    big_m[k, :, lanes(2 * pair + which)] = widened(block)
    folded = fin[0:TILE].astype(f32)
    squares = jnp.concatenate(
        [
            jnp.sum(jnp.where(tall == q, folded, 0.0), 1, keepdims=True)
            for q in range(slots // TILE)
        ],
        0,
    )

    scales = []
    for k in range(layers):
        scale_rows = lax.rsqrt(squares / width + EPS)
        scales.append(scale_rows)
        latent = (acc_p[:, lanes(k)] * scale_rows).astype(bf16)
        zs[k] = latent
        x = first_x[...] if k == 0 else cur[...]
        xs[k] = x.astype(bf16)
        if k < layers - 1:
            cur[...] = x + SCALE * matmul(latent, w_up[k], NN)
            acc_p[:, lanes(k + 1, layers)] += SCALE * matmul(
                latent, big_m[k, :, lanes(k + 1, layers)], NN
            )
            inner = acc_q[:, lanes(k)]
            step = SCALE * matmul(latent, big_u[k, :, lanes(k, layers - 1)], NN)
            squares = jnp.maximum(
                squares
                + jnp.sum(
                    latent.astype(f32) * (inner + 0.5 * step[:, 0:LANES]), 1, keepdims=True
                ),
                0.0,
            )
            acc_q[:, lanes(k, layers - 1)] += step
            if k > 0:
                others = big_u[0:k, :, lanes(k)].reshape(k * LANES, LANES)
                acc_q[:, lanes(0, k)] += SCALE * matmul(latent, others, NT)
            seen[k + 1, :, lanes(0, k + 1)] = acc_q[:, lanes(0, k + 1)].astype(bf16)

    for m in reversed(range(layers)):
        rank_low = (SCALE * acc_w[:, lanes(m)]).astype(bf16)
        product = rank_low.astype(f32) * zs[m].astype(f32)
        prods[m] = product
        scale_rows = scales[m]
        scaled = (rank_low.astype(f32) * scale_rows).astype(bf16)
        rd[m] = scaled
        g = first_cot[...] if m == layers - 1 else cur[...]
        gs[m] = g.astype(bf16)
        if m > 0:
            weight = scale_rows * scale_rows * jnp.sum(product, 1, keepdims=True) / width
            cur[...] = (
                g + matmul(scaled, w_down[m], NN) - weight * xs[m].astype(f32)
            )
            others = big_m[0:m, :, lanes(m)].reshape(m * LANES, LANES)
            acc_w[:, lanes(0, m)] += matmul(scaled, others, NT) - weight * seen[
                m, :, lanes(0, m)
            ].astype(f32)

    for layer in range(layers):
        drain(w_gain.at[layer], wg_r.at[layer])

    def down_grad(layer):
        gain = w_gain[layer, 0:1].astype(f32)
        back_d[layer] = (matmul(rd[layer], xs[layer], TN) * gain).astype(bf16)
        return back_d.at[layer], grad_down.at[:, columns(section)], gd_s, gd_r

    def up_grad(layer):
        back_u[layer] = (SCALE * matmul(zs[layer], gs[layer], TN)).astype(bf16)
        return back_u.at[layer], grad_up.at[:, columns(section)], gu_s, gu_r

    for make in (down_grad, up_grad):
        for layer in peers("section"):
            source, target, send, recv = make(layer)
            pltpu.make_async_remote_copy(
                source, target, send, recv, {"section": layer}, MESH
            ).start()
    for make in (down_grad, up_grad):
        source, target, _, recv = make(section)
        pltpu.make_async_copy(source, target, recv).start()

    slope_row[:, 0:slots] = lax.dot_general(
        jnp.full((8, LANES), 1.0 / math.sqrt(width), f32),
        prods[section],
        (NT, ((), ())),
        preferred_element_type=f32,
        precision=lax.Precision.HIGHEST,
    )
    for peer in peers("dp"):
        pltpu.make_async_remote_copy(
            slope_row, slopes.at[dp], sl_s, sl_r, {"dp": peer}, MESH
        ).start()
    slopes[dp] = slope_row[...]

    drain(recvbuf.at[pl.ds(0, groups - 1)], tok_s)
    drain(w_down.at[pl.ds(0, layers - 1)], wd_s)
    drain(w_up.at[pl.ds(0, layers - 1)], wu_s)
    drain(w_gain.at[pl.ds(0, layers - 1)], wg_s)
    for first, size, sem in sent:
        drain(fin.at[pl.ds(first, size)], sem)
    drain(back_d.at[pl.ds(0, layers - 1)], gd_s)
    drain(back_u.at[pl.ds(0, layers - 1)], gu_s)
    drain(slopes.at[pl.ds(0, groups - 1)], sl_s)

    drain(slopes.at[pl.ds(0, groups - 1)], sl_r)
    wide = slopes.shape[2]
    found = jnp.zeros((count, wide), f32)
    for d in range(groups):
        found = jnp.where(own_col == d, slopes[d, 0:1], found)
    first_slot = (dp * each).astype(f32)
    place_col = jnp.sum(jnp.where(diagonal, place, 0.0), 1, keepdims=True) + first_slot
    here = lax.broadcasted_iota(jnp.int32, (count, wide), 1).astype(f32) == place_col
    slope_col = jnp.sum(jnp.where(here, found, 0.0), 1, keepdims=True)
    slope_out[...] = jnp.sum(jnp.where(diagonal, slope_col, 0.0), 0, keepdims=True)

    drain(grad_up, gu_r)
    drain(grad_down, gd_r)


def finish(raw_down, raw_up, raw_slope, grad_down, grad_up, slope, v_down, v_up, v_slope, loads, stores):
    parts = (loads.shape[0] - 1) // 2
    rows = grad_up.shape[0] // parts
    pieces = [(raw_slope, v_slope, slope)]
    for i, block in enumerate((0, 2, 1, 3)):
        some, home = pl.ds(i * rows, rows), pl.ds(block * rows, rows)
        pieces.append((raw_up.at[some], v_up.at[some], grad_up.at[home]))
        pieces.append((raw_down.at[some], v_down.at[some], grad_down.at[home]))
    reads = [
        pltpu.make_async_copy(source, through, loads.at[i])
        for i, (source, through, _) in enumerate(pieces)
    ]
    writes = [
        pltpu.make_async_copy(through, target, stores.at[i])
        for i, (_, through, target) in enumerate(pieces)
    ]
    for read in reads:
        read.start()
    for read, write in zip(reads, writes):
        read.wait()
        write.start()
    for write in writes:
        write.wait()


def on_device(
    tokens,
    owner_indices,
    local_adapter_index,
    gains,
    adapter_down_weights,
    adapter_up_weights,
    cotangent,
):
    groups, layers, ranks = (lax.axis_size(a) for a in ("dp", "section", "tensor"))
    count, local = tokens.shape
    micro = count // MTOK
    cap = 5 * MTOK // (4 * groups)
    each = micro * cap
    spad = round_up(each, TILE)
    slots = groups * each
    fw = local // layers
    adapters, rank = adapter_down_weights.shape[1:3]
    weight_rows = adapters * rank
    half = slots // 2
    wide = round_up(slots, LANES)
    _, ends = payload_rows(layers, half, rank, TILE * layers * ranks)
    rows = ends[-1]
    most = max(b - a for a, b in zip([0] + ends, ends))
    stages = 2 * (ranks.bit_length() - 1) + 2
    vmem = pl.BlockSpec(memory_space=pltpu.VMEM)
    anywhere = pl.BlockSpec(memory_space=pltpu.HBM)
    b16, f32 = jnp.bfloat16, jnp.float32
    dma = pltpu.SemaphoreType.DMA
    raw = pl.pallas_call(
        functools.partial(kernel, cap),
        out_shape=(
            jax.ShapeDtypeStruct((weight_rows, local), b16),
            jax.ShapeDtypeStruct((weight_rows, local), b16),
            jax.ShapeDtypeStruct((1, count), f32),
        ),
        in_specs=[anywhere] * 7,
        out_specs=(anywhere, anywhere, vmem),
        scratch_shapes=[
            pltpu.VMEM((1, count), jnp.int32),
            pltpu.VMEM((1, count), jnp.int32),
            pltpu.VMEM((1, local), b16),
            pltpu.VMEM((weight_rows, local), b16),
            pltpu.VMEM((weight_rows, local), b16),
            pltpu.VMEM((count, fw), b16),
            pltpu.VMEM((count, fw), b16),
            pltpu.VMEM((groups, spad, 2 * fw + LANES), b16),
            pltpu.VMEM((groups, spad, 2 * fw + LANES), b16),
            pltpu.VMEM((TILE, local), b16),
            pltpu.VMEM((layers, TILE, fw), b16),
            pltpu.VMEM((weight_rows, local), b16),
            pltpu.VMEM((layers, weight_rows, fw), b16),
            pltpu.VMEM((layers, weight_rows, fw), b16),
            pltpu.VMEM((rows, LANES), b16),
            pltpu.VMEM((rows, LANES), b16),
            pltpu.VMEM((rows, LANES), b16),
            pltpu.VMEM((3, most, LANES), b16),
            pltpu.VMEM((slots, layers * LANES), f32),
            pltpu.VMEM((slots, layers * LANES), f32),
            pltpu.VMEM((slots, layers * LANES), f32),
            pltpu.VMEM((layers, slots, layers * LANES), b16),
            pltpu.VMEM((layers, LANES, layers * LANES), b16),
            pltpu.VMEM((layers, LANES, layers * LANES), b16),
            pltpu.VMEM((layers, slots, fw), b16),
            pltpu.VMEM((layers, slots, fw), b16),
            pltpu.VMEM((layers, slots, LANES), b16),
            pltpu.VMEM((layers, slots, LANES), b16),
            pltpu.VMEM((layers, slots, LANES), f32),
            pltpu.VMEM((slots, fw), f32),
            pltpu.VMEM((slots, fw), f32),
            pltpu.VMEM((slots, fw), f32),
            pltpu.VMEM((slots, LANES), f32),
            pltpu.VMEM((layers, weight_rows, fw), b16),
            pltpu.VMEM((layers, weight_rows, fw), b16),
            pltpu.VMEM((8, wide), f32),
            pltpu.VMEM((groups, 8, wide), f32),
            pltpu.SemaphoreType.REGULAR,
            pltpu.SemaphoreType.REGULAR,
            dma((13,)),
            dma,
            dma,
            dma,
            dma,
            dma,
            dma((2, layers)),
            dma((layers,)),
            dma((layers,)),
            dma((3, stages)),
            dma((3, stages)),
            dma,
            dma,
            dma,
            dma,
            dma,
            dma,
        ],
        compiler_params=pltpu.CompilerParams(
            collective_id=0, has_side_effects=True, vmem_limit_bytes=62 * 1024 * 1024
        ),
    )(
        owner_indices.reshape(1, count),
        local_adapter_index.reshape(1, count),
        gains,
        adapter_down_weights.reshape(weight_rows, local),
        tokens,
        cotangent,
        adapter_up_weights.reshape(weight_rows, local),
    )
    grad_down, grad_up, slope = pl.pallas_call(
        finish,
        out_shape=tuple(jax.ShapeDtypeStruct(r.shape, r.dtype) for r in raw),
        in_specs=[anywhere] * 3,
        out_specs=(anywhere,) * 3,
        scratch_shapes=[pltpu.VMEM(r.shape, r.dtype) for r in raw] + [dma((9,)), dma((9,))],
        compiler_params=pltpu.CompilerParams(vmem_limit_bytes=62 * 1024 * 1024),
    )(*raw)
    shape = (1, adapters, rank, local)
    return (grad_down.reshape(shape), grad_up.reshape(shape), slope)


def solution(mesh):
    return jax.shard_map(
        on_device,
        mesh=mesh,
        in_specs=(
            P("dp", "tensor"),
            P("dp", None),
            P("dp"),
            P("section", "tensor"),
            P("section", "dp", None, "tensor"),
            P("section", "dp", None, "tensor"),
            P("dp", "tensor"),
        ),
        out_specs=(
            P("section", "dp", None, "tensor"),
            P("section", "dp", None, "tensor"),
            P("section", "dp"),
        ),
        check_vma=False,
    )
```

```python
import functools
import math

import jax
import jax.numpy as jnp
from jax import lax
from jax.experimental import pallas as pl
from jax.experimental.pallas import tpu as pltpu
from jax.sharding import PartitionSpec as P

MTOK = 64
LANES = 128
TILE = 16
JOINT = True
EPS = 1e-05
SCALE = 0.5
MESH = pl.DeviceIdType.MESH
NN = ((1,), (0,))
NT = ((1,), (1,))
TN = ((0,), (0,))


def round_up(value, unit):
    return -(-value // unit) * unit


def matmul(a, b, contract):
    return lax.dot_general(a, b, (contract, ((), ())), preferred_element_type=jnp.float32)


def drain(ref, sem):
    pltpu.make_async_copy(ref, ref, sem).wait()


def peers(axis):
    count, me = lax.axis_size(axis), lax.axis_index(axis)
    offsets = sorted(range(1, count), key=lambda o: (-min(o, count - o), o))
    return [lax.rem(me + o, count) for o in offsets]


def shared_blocks(layers):
    return (layers - 2, layers - 4) if layers >= 4 else (None, None)


def payload_rows(layers, half, rank, unit):
    at, ends = {}, []
    at["squares"], rows = 0, TILE
    for name, count in (("q", layers - 1), ("r", layers)):
        at[name], rows = rows, rows + count * half
    blocks = [("u", k, other) for k in range(layers - 1) for other in range(k, layers - 1)]
    left, right = shared_blocks(layers)
    later = []
    for part in range(2):
        parts = [(("p", part), layers // 2 * half)]
        for k in range(layers - 1):
            for pair in range((k + 1) // 2, layers // 2):
                if k != left:
                    parts.append((("m", part, k, pair), rank))
        later.append(parts)
    free = [-sum(size for _, size in parts) % unit // rank for parts in later]
    over = -(-((rows + len(blocks) * rank) % unit) // rank)
    if over <= sum(free):
        for parts, room in zip(later, free):
            take = min(room, over)
            over -= take
            for _ in range(take):
                parts.append((blocks.pop(), rank))
    for parts in [[(block, rank) for block in blocks], *later]:
        for name, size in parts:
            at[name], rows = rows, rows + size
        rows = round_up(rows, unit)
        ends.append(rows)
    for part in range(2):
        if left is not None:
            at["m", part, left, layers // 2 - 1] = at["m", part, right, layers // 2 - 2]
    return at, ends


def kernel(
    cap,
    own,
    choose,
    gains,
    down,
    tokens,
    cotangent,
    up,
    grad_down,
    grad_up,
    slope_out,
    own_v,
    choose_v,
    gains_v,
    up_v,
    down_v,
    tokv,
    cotv,
    sendbuf,
    recvbuf,
    gains_wide,
    w_gain,
    down_scaled,
    w_down,
    w_up,
    part,
    fin,
    got,
    got_y,
    acc_p,
    acc_q,
    acc_w,
    seen,
    big_m,
    big_u,
    xs,
    gs,
    zs,
    rd,
    prods,
    cur,
    first_x,
    first_cot,
    mask,
    back_d,
    back_u,
    slope_row,
    slopes,
    group_sem,
    all_sem,
    loc_sem,
    tok_s,
    tok_r,
    wd_s,
    wu_s,
    wg_s,
    wd_r,
    wu_r,
    wg_r,
    ar_s,
    ar_r,
    gd_s,
    gu_s,
    gd_r,
    gu_r,
    sl_s,
    sl_r,
):
    dp = lax.axis_index("dp")
    section = lax.axis_index("section")
    tensor = lax.axis_index("tensor")
    groups = lax.axis_size("dp")
    layers = lax.axis_size("section")
    ranks = lax.axis_size("tensor")
    bits = ranks.bit_length() - 1
    count = tokens.shape[0]
    fw = tokv.shape[1]
    width = tokens.shape[1] * ranks
    spad = sendbuf.shape[1]
    slots = xs.shape[1]
    half = slots // 2
    rank = LANES // 2
    each = slots // groups
    bf16, f32 = jnp.bfloat16, jnp.float32
    at, ends = payload_rows(layers, half, rank, TILE * layers * ranks)
    left_k, _ = shared_blocks(layers)

    barrier = pltpu.get_barrier_semaphore()
    core = tensor & 1
    sibling = {"tensor": tensor ^ 1}

    def greet(device):
        pl.semaphore_signal(barrier, inc=1, device_id=device, device_id_type=MESH)

    chips = ranks // 2
    for away in range(layers):
        for over in range(chips):
            chip = lax.rem((tensor >> 1) + over, chips)
            if away or over:
                greet({"section": lax.rem(section + away, layers), "tensor": 2 * chip + 1})
    pl.when(core == 0)(lambda: greet(sibling))
    for peer in peers("dp"):
        greet({"dp": peer, "tensor": tensor - core})

    def group_arrived():
        @pl.when(core == 1)
        def _():
            pl.semaphore_wait(barrier, layers * ranks - 1)
            pl.semaphore_signal(group_sem, inc=1, device_id=sibling, device_id_type=MESH)

        @pl.when(core == 0)
        def _():
            pl.semaphore_wait(group_sem, 1)

    def all_arrived():
        @pl.when(core == 0)
        def _():
            pl.semaphore_wait(barrier, 2 * (groups - 1))
            pl.semaphore_signal(all_sem, inc=1, device_id=sibling, device_id_type=MESH)

        @pl.when(core == 1)
        def _():
            pl.semaphore_wait(all_sem, 1)

    def columns(index):
        return pl.ds(pl.multiple_of(index * fw, LANES), fw)

    quarter = rank // 2
    blocks = [
        (pl.ds((2 * a + h) * quarter, quarter), pl.ds((2 * h + a) * quarter, quarter))
        for a in range(2)
        for h in range(2)
    ]
    loads = [
        pltpu.make_async_copy(source, target, loc_sem.at[i])
        for i, (source, target) in enumerate(
            [
                (own, own_v),
                (choose, choose_v),
                (tokens.at[:, columns(section)], tokv),
                (cotangent.at[:, columns(section)], cotv),
                (gains, gains_v),
            ]
            + [(up.at[there], up_v.at[here]) for there, here in blocks]
            + [(down.at[there], down_v.at[here]) for there, here in blocks]
        )
    ]
    for load in loads:
        load.start()

    early = lax.broadcasted_iota(jnp.int32, (count, count), 0)
    late = lax.broadcasted_iota(jnp.int32, (count, count), 1)
    diagonal = early == late
    shift = MTOK.bit_length() - 1
    loads[0].wait()
    loads[1].wait()
    own_row = own_v[...].astype(f32)
    own_col = jnp.sum(jnp.where(diagonal, own_row, 0.0), 1, keepdims=True)
    before = (own_col == own_row) & (early < late) & ((early >> shift) == (late >> shift))
    rank_in = jnp.sum(jnp.where(before, 1.0, 0.0), 0, keepdims=True)
    micro_of = (lax.broadcasted_iota(jnp.int32, (1, count), 1) >> shift).astype(f32)
    place = micro_of * cap + rank_in
    spots = lax.broadcasted_iota(jnp.int32, (spad, count), 0).astype(f32)
    fits = place == spots
    member = jnp.concatenate(
        [jnp.where(fits & (own_row == d), 1.0, 0.0) for d in range(groups)], 0
    )
    flag = jnp.sum(member * choose_v[...].astype(f32), 1, keepdims=True)
    member = member.astype(bf16)
    loads[2].wait()
    loads[3].wait()
    sendbuf[:, :, 0:fw] = matmul(member, tokv[...], NN).astype(bf16).reshape(groups, spad, fw)
    sendbuf[:, :, fw : 2 * fw] = (
        matmul(member, cotv[...], NN).astype(bf16).reshape(groups, spad, fw)
    )
    sendbuf[:, :, 2 * fw :] = (
        jnp.broadcast_to(flag, (groups * spad, LANES)).astype(bf16).reshape(groups, spad, LANES)
    )

    group_arrived()

    def spread(source, target, send, recv, some=None):
        def rows_of(ref):
            return ref if some is None else ref.at[some]

        for peer in peers("section"):
            pltpu.make_async_remote_copy(
                rows_of(source).at[:, columns(peer)],
                rows_of(target.at[section]),
                send,
                recv.at[section],
                {"section": peer},
                MESH,
            ).start()
        pltpu.make_async_copy(
            rows_of(source).at[:, columns(section)], rows_of(target.at[section]), recv.at[section]
        ).start()

    for load in loads[5:9]:
        load.wait()
    spread(up_v, w_up, wu_s, wu_r)
    for load in loads[4:5] + loads[9:]:
        load.wait()
    down_scaled[...] = (down_v[...].astype(f32) * gains_v[...].astype(f32)).astype(bf16)
    all_arrived()
    for peer in peers("dp"):
        pltpu.make_async_remote_copy(
            sendbuf.at[peer], recvbuf.at[dp], tok_s, tok_r, {"dp": peer}, MESH
        ).start()
    recvbuf[dp] = sendbuf[dp]

    for part_of in range(2):
        spread(
            down_scaled,
            w_down,
            wd_s,
            wd_r.at[part_of],
            pl.ds(part_of * rank, rank),
        )
    gains_wide[...] = jnp.broadcast_to(gains_v[...], gains_wide.shape)
    spread(gains_wide, w_gain, wg_s, wg_r)

    cell = lax.broadcasted_iota(jnp.int32, (1, groups * spad), 1)
    source = sum((cell >= d * spad).astype(jnp.int32) for d in range(1, groups))
    within = cell - source * spad
    wanted = jnp.where(within < each, source * each + within, -1)
    slot_ids = lax.broadcasted_iota(jnp.int32, (slots, groups * spad), 0)
    compact = jnp.where(slot_ids == wanted, 1.0, 0.0).astype(bf16)
    drain(recvbuf.at[pl.ds(0, groups - 1)], tok_r)
    arrived = matmul(compact, recvbuf[...].reshape(groups * spad, 2 * fw + LANES), NN)
    x0 = arrived[:, 0:fw]
    first_x[...] = x0
    first_cot[...] = arrived[:, fw : 2 * fw]
    lane = lax.broadcasted_iota(jnp.int32, (slots, LANES), 1)
    second = arrived[:, 2 * fw :] > 0.5
    mask[...] = jnp.where(second == ((lane & quarter) > 0), 1.0, 0.0)

    even = (lax.broadcasted_iota(jnp.int32, (half, LANES), 1) & quarter) == 0
    even_rank = (lax.broadcasted_iota(jnp.int32, (rank, LANES), 1) & quarter) == 0
    left = lane < rank
    left_rank = lax.broadcasted_iota(jnp.int32, (rank, LANES), 1) < rank
    tall = lax.broadcasted_iota(jnp.int32, (TILE, LANES), 1)

    def packed(total):
        kept = total * mask[...]
        first = kept[0:half] + pltpu.roll(kept[0:half], LANES - quarter, 1)
        last = kept[half:] + pltpu.roll(kept[half:], quarter, 1)
        return jnp.where(even, first, last).astype(bf16)

    def unpacked(total):
        total = total.astype(f32)
        first = jnp.where(even, total, pltpu.roll(total, quarter, 1))
        last = jnp.where(even, pltpu.roll(total, LANES - quarter, 1), total)
        return jnp.concatenate([first, last], 0) * mask[...]

    def thinned(block):
        first, second, third, fourth = (
            block[i * quarter : (i + 1) * quarter] for i in range(4)
        )
        return jnp.where(
            even_rank,
            jnp.concatenate([first, third], 0),
            jnp.concatenate([second, fourth], 0),
        ).astype(bf16)

    def widened(block):
        block = block.astype(f32)
        evens, odds = jnp.where(even_rank, block, 0.0), jnp.where(even_rank, 0.0, block)
        return jnp.concatenate(
            [evens[0:quarter], odds[0:quarter], evens[quarter:], odds[quarter:]], 0
        ).astype(bf16)

    def layer_of(first, last, which, keep_left):
        if which == 0:
            return jnp.where(keep_left, first, pltpu.roll(last, rank, 1))
        return jnp.where(keep_left, pltpu.roll(first, rank, 1), last)

    squares = jnp.sum(x0 * x0, 1, keepdims=True)
    folded = jnp.zeros((TILE, LANES), f32)
    for q in range(slots // TILE):
        folded = jnp.where(tall == q, squares[q * TILE : (q + 1) * TILE], folded)
    part[0:TILE] = folded.astype(bf16)

    for layer in range(layers):
        drain(w_up.at[layer], wu_r.at[layer])
    x_low = first_x[...].astype(bf16)
    cot_low = first_cot[...].astype(bf16)
    for layer in range(layers):
        weight = w_up[layer]
        if layer < layers - 1:
            row = at["q"] + layer * half
            part[row : row + half] = packed(matmul(x_low, weight, NT))
        row = at["r"] + layer * half
        part[row : row + half] = packed(matmul(cot_low, weight, NT))
    for k in range(layers - 1):
        stacked = w_up[k : layers - 1].reshape((layers - 1 - k) * LANES, fw)
        product = matmul(w_up[k], stacked, NT)
        for i, other in enumerate(range(k, layers - 1)):
            row = at["u", k, other]
            part[row : row + rank] = thinned(product[:, i * LANES : (i + 1) * LANES])

    def down_products(h):
        for layer in range(layers):
            drain(w_down.at[layer, pl.ds(h * rank, rank)], wd_r.at[h, layer])
        weights = w_down[:, h * rank : (h + 1) * rank].reshape(layers * rank, fw)
        product = matmul(x_low, weights, NT)
        for pair in range(layers // 2):
            row = at["p", h] + pair * half
            part[row : row + half] = packed(product[:, pair * LANES : (pair + 1) * LANES])
        for k in range(layers - 1):
            skip = (k + 1) // 2
            product = matmul(w_up[k], weights[skip * LANES :], NT)
            for pair in range(skip, layers // 2):
                row = at["m", h, k, pair]
                i = pair - skip
                block = thinned(product[:, i * LANES : (i + 1) * LANES])
                if k == left_k:
                    block = jnp.where(
                        left_rank, pltpu.roll(block.astype(f32), rank, 1), part[row : row + rank]
                    ).astype(bf16)
                part[row : row + rank] = block

    def rows(first, size):
        return pl.ds(pl.multiple_of(first, TILE), size)

    def all_reduce(chunk, joint):
        first = ends[chunk - 1] if chunk else 0
        size = ends[chunk] - first
        halvings = bits - 1 if joint and bits > 1 else bits
        strides = [] if halvings == bits else [1 << halvings]
        whole, piece = size, (size >> halvings) // (layers << len(strides))
        base, stage, starts = first, 0, []
        sends, arrivals = ar_s.at[chunk], ar_r.at[chunk]
        others = [({"section": peer}, peer, 0) for peer in peers("section")]
        high = 0
        for stride in strides:
            high = (tensor // stride) & 1
            away = tensor ^ stride
            others = (
                [({"section": peer, "tensor": away}, peer, 1) for peer in peers("section")]
                + others
                + [({"tensor": away}, section, 1)]
            )

        def index_of(peer, crossed):
            return peer + layers * (high + crossed - 2 * high * crossed)

        def send(source, target, device):
            pltpu.make_async_remote_copy(
                source, target, sends.at[stage], arrivals.at[stage], device, MESH
            ).start()

        for bit in range(halvings):
            size //= 2
            mine = (tensor >> bit) & 1
            keep, give = base + mine * size, base + (1 - mine) * size
            peer = tensor ^ (1 << bit)
            spot = first + whole - 2 * size
            send(part.at[rows(give, size)], got.at[pl.ds(spot, size)], {"tensor": peer})
            yield
            drain(got.at[pl.ds(spot, size)], arrivals.at[stage])
            part[rows(keep, size)] = (
                part[rows(keep, size)].astype(f32) + got[spot : spot + size].astype(f32)
            ).astype(bf16)
            starts.append((keep, size, peer))
            base, stage = keep, stage + 1
        landed = got_y.at[chunk]
        for o, (device, peer, crossed) in enumerate(others):
            send(
                part.at[rows(base + index_of(peer, crossed) * piece, piece)],
                landed.at[pl.ds(o * piece, piece)],
                device,
            )
        yield
        filled = len(others) * piece
        drain(landed.at[pl.ds(0, filled)], arrivals.at[stage])
        stage += 1
        mine = base + index_of(section, 0) * piece
        total = part[rows(mine, piece)].astype(f32)
        for o in range(len(others)):
            total += got_y[chunk, o * piece : (o + 1) * piece].astype(f32)
        fin[rows(mine, piece)] = total.astype(bf16)
        for device, _, _ in others:
            send(fin.at[rows(mine, piece)], fin.at[rows(mine, piece)], device)
        yield
        drain(fin.at[pl.ds(first, filled)], arrivals.at[stage])
        stage += 1
        for keep, size, peer in reversed(starts):
            send(fin.at[rows(keep, size)], fin.at[rows(keep, size)], {"tensor": peer})
            yield
            drain(fin.at[pl.ds(first, size)], arrivals.at[stage])
            stage += 1
        sizes = [size for _, size, _ in starts]
        for i, size in enumerate([*sizes, filled, filled, *reversed(sizes)]):
            sent.append((first, size, sends.at[i]))

    sent = []
    chunks = [all_reduce(0, False), all_reduce(1, False), all_reduce(2, JOINT)]

    def advance(order):
        for chunk in order:
            next(chunks[chunk], None)

    advance([0, 0])
    down_products(0)
    advance([1])
    advance([0, 1] if bits > 1 else [1])
    down_products(1)
    advance([2])
    advance([1, 0, 2, 0, 1, 0, 2, 1, 2, 0, 1, 2, 0, 1, 2, 0, 1, 2])

    def lanes(first, last=None):
        return slice(first * LANES, (first + 1 if last is None else last) * LANES)

    for name, target, number in (("q", acc_q, layers - 1), ("r", acc_w, layers)):
        for layer in range(number):
            row = at[name] + layer * half
            target[:, lanes(layer)] = unpacked(fin[row : row + half])
    for pair in range(layers // 2):
        row, last_row = (at["p", h] + pair * half for h in range(2))
        first = unpacked(fin[row : row + half])
        last = unpacked(fin[last_row : last_row + half])
        for which in range(2):
            acc_p[:, lanes(2 * pair + which)] = layer_of(first, last, which, left)
    for k in range(layers - 1):
        for other in range(k, layers - 1):
            row = at["u", k, other]
            big_u[k, :, lanes(other)] = widened(fin[row : row + rank])
        for pair in range((k + 1) // 2, layers // 2):
            first, last = (
                fin[row : row + rank].astype(f32)
                for row in (at["m", h, k, pair] for h in range(2))
            )
            for which in range(2):
                if 2 * pair + which > k:
                    block = layer_of(first, last, 0 if k == left_k else which, left_rank)
                    big_m[k, :, lanes(2 * pair + which)] = widened(block)
    folded = fin[0:TILE].astype(f32)
    squares = jnp.concatenate(
        [
            jnp.sum(jnp.where(tall == q, folded, 0.0), 1, keepdims=True)
            for q in range(slots // TILE)
        ],
        0,
    )

    scales = []
    for k in range(layers):
        scale_rows = lax.rsqrt(squares / width + EPS)
        scales.append(scale_rows)
        latent = (acc_p[:, lanes(k)] * scale_rows).astype(bf16)
        zs[k] = latent
        x = first_x[...] if k == 0 else cur[...]
        xs[k] = x.astype(bf16)
        if k < layers - 1:
            cur[...] = x + SCALE * matmul(latent, w_up[k], NN)
            acc_p[:, lanes(k + 1, layers)] += SCALE * matmul(
                latent, big_m[k, :, lanes(k + 1, layers)], NN
            )
            inner = acc_q[:, lanes(k)]
            step = SCALE * matmul(latent, big_u[k, :, lanes(k, layers - 1)], NN)
            squares = jnp.maximum(
                squares
                + jnp.sum(
                    latent.astype(f32) * (inner + 0.5 * step[:, 0:LANES]), 1, keepdims=True
                ),
                0.0,
            )
            acc_q[:, lanes(k, layers - 1)] += step
            if k > 0:
                others = big_u[0:k, :, lanes(k)].reshape(k * LANES, LANES)
                acc_q[:, lanes(0, k)] += SCALE * matmul(latent, others, NT)
            seen[k + 1, :, lanes(0, k + 1)] = acc_q[:, lanes(0, k + 1)].astype(bf16)

    for m in reversed(range(layers)):
        rank_low = (SCALE * acc_w[:, lanes(m)]).astype(bf16)
        product = rank_low.astype(f32) * zs[m].astype(f32)
        prods[m] = product
        scale_rows = scales[m]
        scaled = (rank_low.astype(f32) * scale_rows).astype(bf16)
        rd[m] = scaled
        g = first_cot[...] if m == layers - 1 else cur[...]
        gs[m] = g.astype(bf16)
        if m > 0:
            weight = scale_rows * scale_rows * jnp.sum(product, 1, keepdims=True) / width
            cur[...] = (
                g + matmul(scaled, w_down[m], NN) - weight * xs[m].astype(f32)
            )
            others = big_m[0:m, :, lanes(m)].reshape(m * LANES, LANES)
            acc_w[:, lanes(0, m)] += matmul(scaled, others, NT) - weight * seen[
                m, :, lanes(0, m)
            ].astype(f32)

    for layer in range(layers):
        drain(w_gain.at[layer], wg_r.at[layer])

    def down_grad(layer):
        gain = w_gain[layer, 0:1].astype(f32)
        back_d[layer] = (matmul(rd[layer], xs[layer], TN) * gain).astype(bf16)
        return back_d.at[layer], grad_down.at[:, columns(section)], gd_s, gd_r

    def up_grad(layer):
        back_u[layer] = (SCALE * matmul(zs[layer], gs[layer], TN)).astype(bf16)
        return back_u.at[layer], grad_up.at[:, columns(section)], gu_s, gu_r

    for layer in peers("section"):
        for make in (down_grad, up_grad):
            source, target, send, recv = make(layer)
            pltpu.make_async_remote_copy(
                source, target, send, recv, {"section": layer}, MESH
            ).start()
    for make in (down_grad, up_grad):
        source, target, _, recv = make(section)
        pltpu.make_async_copy(source, target, recv).start()

    slope_row[:, 0:slots] = lax.dot_general(
        jnp.full((8, LANES), 1.0 / math.sqrt(width), f32),
        prods[section],
        (NT, ((), ())),
        preferred_element_type=f32,
        precision=lax.Precision.HIGHEST,
    )
    for peer in peers("dp"):
        pltpu.make_async_remote_copy(
            slope_row, slopes.at[dp], sl_s, sl_r, {"dp": peer}, MESH
        ).start()
    slopes[dp] = slope_row[...]

    drain(recvbuf.at[pl.ds(0, groups - 1)], tok_s)
    drain(w_down.at[pl.ds(0, layers - 1)], wd_s)
    drain(w_up.at[pl.ds(0, layers - 1)], wu_s)
    drain(w_gain.at[pl.ds(0, layers - 1)], wg_s)
    for first, size, sem in sent:
        drain(fin.at[pl.ds(first, size)], sem)
    drain(back_d.at[pl.ds(0, layers - 1)], gd_s)
    drain(back_u.at[pl.ds(0, layers - 1)], gu_s)
    drain(slopes.at[pl.ds(0, groups - 1)], sl_s)

    drain(slopes.at[pl.ds(0, groups - 1)], sl_r)
    wide = slopes.shape[2]
    found = jnp.zeros((count, wide), f32)
    for d in range(groups):
        found = jnp.where(own_col == d, slopes[d, 0:1], found)
    first_slot = (dp * each).astype(f32)
    place_col = jnp.sum(jnp.where(diagonal, place, 0.0), 1, keepdims=True) + first_slot
    here = lax.broadcasted_iota(jnp.int32, (count, wide), 1).astype(f32) == place_col
    slope_col = jnp.sum(jnp.where(here, found, 0.0), 1, keepdims=True)
    slope_out[...] = jnp.sum(jnp.where(diagonal, slope_col, 0.0), 0, keepdims=True)

    drain(grad_up, gu_r)
    drain(grad_down, gd_r)


def finish(raw_down, raw_up, raw_slope, grad_down, grad_up, slope, v_down, v_up, v_slope, loads, stores):
    parts = (loads.shape[0] - 1) // 2
    rows = grad_up.shape[0] // parts
    pieces = [(raw_slope, v_slope, slope)]
    for i, block in enumerate((0, 2, 1, 3)):
        some, home = pl.ds(i * rows, rows), pl.ds(block * rows, rows)
        pieces.append((raw_up.at[some], v_up.at[some], grad_up.at[home]))
        pieces.append((raw_down.at[some], v_down.at[some], grad_down.at[home]))
    reads = [
        pltpu.make_async_copy(source, through, loads.at[i])
        for i, (source, through, _) in enumerate(pieces)
    ]
    writes = [
        pltpu.make_async_copy(through, target, stores.at[i])
        for i, (_, through, target) in enumerate(pieces)
    ]
    for read in reads:
        read.start()
    for read, write in zip(reads, writes):
        read.wait()
        write.start()
    for write in writes:
        write.wait()


def on_device(
    tokens,
    owner_indices,
    local_adapter_index,
    gains,
    adapter_down_weights,
    adapter_up_weights,
    cotangent,
):
    groups, layers, ranks = (lax.axis_size(a) for a in ("dp", "section", "tensor"))
    count, local = tokens.shape
    micro = count // MTOK
    cap = 5 * MTOK // (4 * groups)
    each = micro * cap
    spad = round_up(each, TILE)
    slots = groups * each
    fw = local // layers
    adapters, rank = adapter_down_weights.shape[1:3]
    weight_rows = adapters * rank
    half = slots // 2
    wide = round_up(slots, LANES)
    _, ends = payload_rows(layers, half, rank, TILE * layers * ranks)
    rows = ends[-1]
    most = max(b - a for a, b in zip([0] + ends, ends))
    stages = 2 * (ranks.bit_length() - 1) + 2
    vmem = pl.BlockSpec(memory_space=pltpu.VMEM)
    anywhere = pl.BlockSpec(memory_space=pltpu.HBM)
    b16, f32 = jnp.bfloat16, jnp.float32
    dma = pltpu.SemaphoreType.DMA
    raw = pl.pallas_call(
        functools.partial(kernel, cap),
        out_shape=(
            jax.ShapeDtypeStruct((weight_rows, local), b16),
            jax.ShapeDtypeStruct((weight_rows, local), b16),
            jax.ShapeDtypeStruct((1, count), f32),
        ),
        in_specs=[anywhere] * 7,
        out_specs=(anywhere, anywhere, vmem),
        scratch_shapes=[
            pltpu.VMEM((1, count), jnp.int32),
            pltpu.VMEM((1, count), jnp.int32),
            pltpu.VMEM((1, local), b16),
            pltpu.VMEM((weight_rows, local), b16),
            pltpu.VMEM((weight_rows, local), b16),
            pltpu.VMEM((count, fw), b16),
            pltpu.VMEM((count, fw), b16),
            pltpu.VMEM((groups, spad, 2 * fw + LANES), b16),
            pltpu.VMEM((groups, spad, 2 * fw + LANES), b16),
            pltpu.VMEM((TILE, local), b16),
            pltpu.VMEM((layers, TILE, fw), b16),
            pltpu.VMEM((weight_rows, local), b16),
            pltpu.VMEM((layers, weight_rows, fw), b16),
            pltpu.VMEM((layers, weight_rows, fw), b16),
            pltpu.VMEM((rows, LANES), b16),
            pltpu.VMEM((rows, LANES), b16),
            pltpu.VMEM((rows, LANES), b16),
            pltpu.VMEM((3, most, LANES), b16),
            pltpu.VMEM((slots, layers * LANES), f32),
            pltpu.VMEM((slots, layers * LANES), f32),
            pltpu.VMEM((slots, layers * LANES), f32),
            pltpu.VMEM((layers, slots, layers * LANES), b16),
            pltpu.VMEM((layers, LANES, layers * LANES), b16),
            pltpu.VMEM((layers, LANES, layers * LANES), b16),
            pltpu.VMEM((layers, slots, fw), b16),
            pltpu.VMEM((layers, slots, fw), b16),
            pltpu.VMEM((layers, slots, LANES), b16),
            pltpu.VMEM((layers, slots, LANES), b16),
            pltpu.VMEM((layers, slots, LANES), f32),
            pltpu.VMEM((slots, fw), f32),
            pltpu.VMEM((slots, fw), f32),
            pltpu.VMEM((slots, fw), f32),
            pltpu.VMEM((slots, LANES), f32),
            pltpu.VMEM((layers, weight_rows, fw), b16),
            pltpu.VMEM((layers, weight_rows, fw), b16),
            pltpu.VMEM((8, wide), f32),
            pltpu.VMEM((groups, 8, wide), f32),
            pltpu.SemaphoreType.REGULAR,
            pltpu.SemaphoreType.REGULAR,
            dma((13,)),
            dma,
            dma,
            dma,
            dma,
            dma,
            dma((2, layers)),
            dma((layers,)),
            dma((layers,)),
            dma((3, stages)),
            dma((3, stages)),
            dma,
            dma,
            dma,
            dma,
            dma,
            dma,
        ],
        compiler_params=pltpu.CompilerParams(
            collective_id=0, has_side_effects=True, vmem_limit_bytes=62 * 1024 * 1024
        ),
    )(
        owner_indices.reshape(1, count),
        local_adapter_index.reshape(1, count),
        gains,
        adapter_down_weights.reshape(weight_rows, local),
        tokens,
        cotangent,
        adapter_up_weights.reshape(weight_rows, local),
    )
    grad_down, grad_up, slope = pl.pallas_call(
        finish,
        out_shape=tuple(jax.ShapeDtypeStruct(r.shape, r.dtype) for r in raw),
        in_specs=[anywhere] * 3,
        out_specs=(anywhere,) * 3,
        scratch_shapes=[pltpu.VMEM(r.shape, r.dtype) for r in raw] + [dma((9,)), dma((9,))],
        compiler_params=pltpu.CompilerParams(vmem_limit_bytes=62 * 1024 * 1024),
    )(*raw)
    shape = (1, adapters, rank, local)
    return (grad_down.reshape(shape), grad_up.reshape(shape), slope)


def solution(mesh):
    return jax.shard_map(
        on_device,
        mesh=mesh,
        in_specs=(
            P("dp", "tensor"),
            P("dp", None),
            P("dp"),
            P("section", "tensor"),
            P("section", "dp", None, "tensor"),
            P("section", "dp", None, "tensor"),
            P("dp", "tensor"),
        ),
        out_specs=(
            P("section", "dp", None, "tensor"),
            P("section", "dp", None, "tensor"),
            P("section", "dp"),
        ),
        check_vma=False,
    )
```
